512 devices in a mesh: gx: 16 (over z, core), gy: 4 (over y_hi), gz: 8 (over y_lo, x).
Axes of the slice: x: 4, y: 8 (y_hi: 4, y_lo: 2; y = y_hi * 2 + y_lo), z: 8, core: 2. Of those that a mesh axis runs over, the one named last changes fastest.
Arguments:
- tokens: bfloat16 [128, 32, 64, 384], P('gx', 'gy', 'gz'), may hold values from -60 to 60
- frozen: int32 [128, 32, 64], P('gx', 'gy', 'gz'), may hold values 0 or 1
- cotangent: bfloat16 [128, 32, 64, 384], P('gx', 'gy', 'gz'), may hold values from -6 to 6
- w_qkv: bfloat16 [384, 1152], replicated, may hold values from -0.3125 to 0.3125
- w_proj: bfloat16 [384, 384], replicated, may hold values from -0.3125 to 0.3125
- norm_gain: float32 [384], replicated, may hold values from 0.5 to 8
Outputs:
- block_out: bfloat16 [128, 32, 64, 384], P('gx', 'gy', 'gz')
- tokens_grad: bfloat16 [128, 32, 64, 384], P('gx', 'gy', 'gz')
- qkv_grad: float32 [384, 1152], replicated
- proj_grad: float32 [384, 384], replicated
- gain_grad: float32 [384], replicated
The draws below stay inside these ranges and needn't reach their ends.
All inputs are finite; a program needn't handle non-finite values. No bound on the sum of `frozen` on one device may be relied on, other than what follows from the above.
Results may differ from the reference program's by a relative error of at most 0.015.
The reference program's roundings to bfloat16 on the way count: a program that leaves them out, or rounds other values in their place, can miss the bound.
Values may be sent and summed in bfloat16 or wider, within the bound.
No kernel may reach another device: no remote copies, remote signals or barrier semaphores. Data moves between devices by JAX's collectives and lax.ppermute only.
A program may use at most 64 MiB of HBM per device.

```python
import math
import jax
import jax.numpy as jnp
from jax import lax

D = 384
HEADS = 12
HDIM = 32
WIN = 8
NX = 128
NY = 32
NZ = 64


def draw_tokens(key, part):
    key = jax.random.fold_in(key, 11)
    key_base, key_scale = jax.random.split(key, 2)
    shape_all = (NX, NY, NZ, D)
    base_draw = jnp.clip(jax.random.normal(key_base, shape_all, jnp.float32), -6.0, 6.0)
    row_scale = jnp.exp(jax.random.uniform(key_scale, (NX, NY, NZ, 1), jnp.float32, 0.0, math.log(10.0)))
    return jnp.clip(base_draw * row_scale, -60.0, 60.0).astype(jnp.bfloat16)


def draw_norm_gain(key, part):
    key = jax.random.fold_in(key, 12)
    return jax.random.uniform(key, (D,), jnp.float32, 0.5, 2.0)


def place_ends(values, own_key, smallest, top_value):
    longest = values.shape.index(max(values.shape))
    spots = []
    for shift in (0, 1):
        where = [jax.random.randint(jax.random.fold_in(own_key, axis), (), 0, length) for axis, length in enumerate(values.shape)]
        where[longest] = (where[longest] + shift) % values.shape[longest]
        spots.append(tuple(where))
    return values.at[spots[0]].set(smallest).at[spots[1]].set(top_value)


def block_levels(key, shape, pieces, smallest, top_value):
    level = 1.0
    for axis_at, blocks in pieces:
        draws = jax.random.uniform(jax.random.fold_in(jax.random.fold_in(key, 6), axis_at), (blocks,), jnp.float32, smallest / len(pieces), top_value / len(pieces))
        level = level * jnp.repeat(jnp.exp(draws), shape[axis_at] // blocks).reshape((-1,) + (1,) * (len(shape) - 1 - axis_at))
    return level


def gaussian(key, extent, deviation, limit, cuts=(), kind=jnp.bfloat16):
    drawn = jax.random.normal(key, extent, jnp.float32) * deviation
    if len(cuts) > 0:
        drawn = block_levels(key, extent, cuts, -0.22, 0.18) * drawn
    return jnp.clip(drawn, min=-limit, max=limit).astype(kind)


def setup_inputs(seed: int = 0) -> dict:
    splits = jax.random.split(jax.random.key(seed), 7)
    tokens = draw_tokens(jax.random.fold_in(splits[6], 71), 0)
    frozen = place_ends((jax.random.randint(splits[1], (NX, NY, NZ), 0, 2) < 1).astype(jnp.int32), jax.random.fold_in(splits[1], 1), 0, 1)
    cotangent = gaussian(splits[2], (NX, NY, NZ, D), 1.0, 6.0, ((0, 16), (1, 4), (2, 8)))
    w_qkv = gaussian(splits[3], (D, 3 * D), D ** -0.5, 0.3125)
    w_proj = gaussian(splits[4], (D, D), D ** -0.5, 0.3125)
    norm_gain = draw_norm_gain(jax.random.fold_in(splits[6], 71), 0)
    return dict(tokens=tokens, frozen=frozen, cotangent=cotangent, w_qkv=w_qkv, w_proj=w_proj, norm_gain=norm_gain)


EPSILON = 1e-05

def head_pass(queries, key_rows, values, d_mixed):
    score_scale = HDIM ** (-0.5)
    scores = jnp.dot(queries, key_rows.T, preferred_element_type=jnp.float32) * score_scale
    top_score = lax.optimization_barrier(jnp.max(scores, axis=-1, keepdims=True))
    exp_terms = jnp.exp(scores - top_score)
    attn_probs = exp_terms / lax.optimization_barrier(jnp.sum(exp_terms, axis=-1, keepdims=True))
    probs_low = attn_probs.astype(jnp.bfloat16)
    mixed_head = jnp.dot(probs_low, values, preferred_element_type=jnp.float32).astype(jnp.bfloat16)
    d_values = jnp.dot(probs_low.T, d_mixed, preferred_element_type=jnp.float32).astype(jnp.bfloat16)
    d_probs = jnp.dot(d_mixed, values.T, preferred_element_type=jnp.float32)
    d_scores = (attn_probs * (d_probs - lax.optimization_barrier(jnp.sum(attn_probs * d_probs, axis=-1, keepdims=True))) * score_scale).astype(jnp.bfloat16)
    d_queries = jnp.dot(d_scores, key_rows, preferred_element_type=jnp.float32).astype(jnp.bfloat16)
    d_keys = jnp.dot(d_scores.T, queries, preferred_element_type=jnp.float32).astype(jnp.bfloat16)
    return (mixed_head, d_queries, d_keys, d_values)

def split_heads(rows):
    return rows.reshape(rows.shape[0], HEADS, HDIM).transpose(1, 0, 2)

def join_heads(heads_rows):
    return heads_rows.transpose(1, 0, 2).reshape(heads_rows.shape[1], HEADS * HDIM)

def window_pass(window_rows, window_cot, w_qkv, w_proj, norm_gain):
    widened = window_rows.astype(jnp.float32)
    row_mean = lax.optimization_barrier(jnp.mean(widened, axis=-1, keepdims=True))
    centred = widened - row_mean
    inv_std = lax.rsqrt(lax.optimization_barrier(jnp.mean(centred * centred, axis=-1, keepdims=True)) + EPSILON)
    unit_rows = centred * inv_std
    normed = (unit_rows * norm_gain).astype(jnp.bfloat16)
    qkv_rows = jnp.dot(normed, w_qkv, preferred_element_type=jnp.float32).astype(jnp.bfloat16)
    d_mixed = jnp.dot(window_cot, w_proj.T, preferred_element_type=jnp.float32).astype(jnp.bfloat16)
    heads_out = lax.map(lambda grouped: head_pass(*grouped), (split_heads(qkv_rows[:, :D]), split_heads(qkv_rows[:, D:2 * D]), split_heads(qkv_rows[:, 2 * D:]), split_heads(d_mixed)))
    mixed_rows = join_heads(heads_out[0])
    branch = jnp.dot(mixed_rows, w_proj, preferred_element_type=jnp.float32).astype(jnp.bfloat16)
    d_qkv = jnp.concatenate([join_heads(heads_out[1]), join_heads(heads_out[2]), join_heads(heads_out[3])], axis=1)
    proj_term = jnp.dot(mixed_rows.T, window_cot, preferred_element_type=jnp.float32)
    qkv_term = jnp.dot(normed.T, d_qkv, preferred_element_type=jnp.float32)
    d_normed = jnp.dot(d_qkv, w_qkv.T, preferred_element_type=jnp.float32)
    gain_term = lax.optimization_barrier(jnp.sum(d_normed * unit_rows, axis=0))
    scaled_grad = d_normed * norm_gain
    d_rows = (inv_std * (scaled_grad - lax.optimization_barrier(jnp.mean(scaled_grad, axis=-1, keepdims=True)) - unit_rows * lax.optimization_barrier(jnp.mean(scaled_grad * unit_rows, axis=-1, keepdims=True)))).astype(jnp.bfloat16)
    return (branch, d_rows, qkv_term, proj_term, gain_term)

def partition(block):
    first, second, third, width = block.shape
    grid = block.reshape(first // WIN, WIN, second // WIN, WIN, third // WIN, WIN, width)
    return grid.transpose(0, 2, 4, 1, 3, 5, 6).reshape(-1, WIN ** 3, width)

def assemble(windows, first, second, third):
    grid = windows.reshape(first // WIN, second // WIN, third // WIN, WIN, WIN, WIN, windows.shape[-1])
    return grid.transpose(0, 3, 1, 4, 2, 5, 6).reshape(first, second, third, windows.shape[-1])

def reference(tokens, frozen, cotangent, w_qkv, w_proj, norm_gain):
    kept = jnp.where(frozen[..., None] == 1, tokens, jnp.zeros_like(tokens))
    half_width = WIN // 2
    shifted = jnp.roll(kept, (-half_width, -half_width, -half_width), axis=(0, 1, 2))
    shifted_cot = jnp.roll(cotangent, (-half_width, -half_width, -half_width), axis=(0, 1, 2))
    zeros_init = (jnp.zeros((D, 3 * D), jnp.float32), jnp.zeros((D, D), jnp.float32), jnp.zeros((D,), jnp.float32))

    def window_step(totals, window_pair):
        results = window_pass(window_pair[0], window_pair[1], w_qkv, w_proj, norm_gain)
        return ((totals[0] + results[2], totals[1] + results[3], totals[2] + results[4]), (results[0], results[1]))
    totals, blocks = lax.scan(window_step, zeros_init, (partition(shifted), partition(shifted_cot)))
    branch = jnp.roll(assemble(blocks[0], NX, NY, NZ), (half_width, half_width, half_width), axis=(0, 1, 2))
    d_rows = jnp.roll(assemble(blocks[1], NX, NY, NZ), (half_width, half_width, half_width), axis=(0, 1, 2))
    block_out = (kept.astype(jnp.float32) + branch.astype(jnp.float32)).astype(jnp.bfloat16)
    tokens_grad = jnp.where(frozen[..., None] == 1, cotangent.astype(jnp.float32) + d_rows.astype(jnp.float32), jnp.zeros((), jnp.float32)).astype(jnp.bfloat16)
    grad_scale = (NX * NY * NZ) ** (-0.5)
    return (block_out, tokens_grad, totals[0] * grad_scale, totals[1] * grad_scale, totals[2] * grad_scale)
```

```python
import jax
import jax.numpy as jnp
import numpy as np
from jax import lax
from jax.experimental import pallas as pl
from jax.experimental.pallas import tpu as pltpu
from jax.sharding import Mesh, PartitionSpec as P

D = 384
HEADS = 12
HDIM = 32
WIN = 8
HALF = WIN // 2
ROWS = WIN**3
PIECE = HALF**3
EPSILON = 1e-05
BF = jnp.bfloat16
F32 = jnp.float32
LANES = 128
PER = LANES // HDIM
CHUNK = 256
SCALE = HDIM ** (-0.5)
LOG2E = 1.4426950408889634
GRAD_ROWS = 5120


def dot(left, right):
    return jnp.dot(left, right, preferred_element_type=F32)


def dot_t(left, right):
    return lax.dot_general(left, right, (((1,), (1,)), ((), ())), preferred_element_type=F32)


def window_kernel(
    tok, cot, w_qkv, w_proj, gain, branch, d_rows, grads,
    qkv, d_mixed, keys_t, values_t, mixed_t, d_queries_t, d_qkv, unit, inv_std, normed,
):
    step = 128
    for start in range(0, ROWS, step):
        part = pl.ds(start, step)
        rows = tok[part, :].astype(F32)
        centred = rows - jnp.mean(rows, axis=-1, keepdims=True)
        inverse = lax.rsqrt(jnp.mean(centred * centred, axis=-1, keepdims=True) + EPSILON)
        unit_rows = centred * inverse
        unit[part, :] = unit_rows
        inv_std[part, :] = jnp.broadcast_to(inverse, (step, LANES))
        normed[part, :] = (unit_rows * gain[...]).astype(BF)
    qkv[...] = dot(normed[...], w_qkv[...]).astype(BF)
    d_mixed[...] = dot_t(cot[...], w_proj[...]).astype(BF)
    keys_t[...] = qkv[:, D : 2 * D].T
    values_t[...] = qkv[:, 2 * D :].T
    lane = lax.broadcasted_iota(jnp.int32, (1, LANES), 1)

    def head_block(index, carry):
        offset = pl.multiple_of(index * LANES, LANES)
        q_block = qkv[:, pl.ds(offset, LANES)]
        k_block = qkv[:, pl.ds(offset + D, LANES)]
        v_block = qkv[:, pl.ds(offset + 2 * D, LANES)]
        m_block = d_mixed[:, pl.ds(offset, LANES)]
        d_keys = jnp.zeros((ROWS, LANES), F32)
        d_values = jnp.zeros((ROWS, LANES), F32)
        for head in range(PER):
            mine = (lane // HDIM) == head
            q_head = jnp.where(mine, q_block, jnp.zeros_like(q_block))
            m_head = jnp.where(mine, m_block, jnp.zeros_like(m_block))
            rows = pl.ds(offset + head * HDIM, HDIM)
            k_head_t = keys_t[rows, :]
            v_head_t = values_t[rows, :]
            for start in range(0, ROWS, CHUNK):
                q_part = q_head[start : start + CHUNK]
                m_part = m_head[start : start + CHUNK]
                scores = dot_t(k_block, q_part)
                top = jnp.max(scores, axis=0, keepdims=True)
                terms = jnp.exp2(scores * (SCALE * LOG2E) - top * (SCALE * LOG2E))
                inverse = 1.0 / jnp.sum(terms, axis=0, keepdims=True)
                probs_low = (terms * inverse).astype(BF)
                d_probs = dot_t(v_block, m_part)
                mixed_t[rows, pl.ds(start, CHUNK)] = dot(v_head_t, probs_low).astype(BF)
                d_values = d_values + dot(probs_low, m_part)
                scaled = inverse * SCALE
                shift = jnp.sum(terms * d_probs, axis=0, keepdims=True) * (inverse * scaled)
                d_scores = (terms * (d_probs * scaled - shift)).astype(BF)
                d_queries_t[rows, pl.ds(start, CHUNK)] = dot(k_head_t, d_scores).astype(BF)
                d_keys = d_keys + dot(d_scores, q_part)
        d_qkv[:, pl.ds(offset + D, LANES)] = d_keys.astype(BF)
        d_qkv[:, pl.ds(offset + 2 * D, LANES)] = d_values.astype(BF)
        return carry

    lax.fori_loop(0, D // LANES, head_block, 0)
    d_qkv[:, pl.ds(0, D)] = d_queries_t[...].T
    branch[...] = dot(mixed_t[...].T, w_proj[...]).astype(BF)
    normed_t = normed[...].T
    for block in range(9):
        term = dot(normed_t, d_qkv[:, block * LANES : (block + 1) * LANES])
        grads[pl.ds(block * D, D), :] = term.astype(BF)
    for block in range(3):
        term = dot(mixed_t[...], cot[:, block * LANES : (block + 1) * LANES])
        grads[pl.ds((9 + block) * D, D), :] = term.astype(BF)
    total = jnp.zeros((1, D), F32)
    for start in range(0, ROWS, step):
        part = pl.ds(start, step)
        d_normed = dot_t(d_qkv[part, :], w_qkv[...])
        unit_rows = unit[part, :]
        total = total + jnp.sum(d_normed * unit_rows, axis=0, keepdims=True)
        scaled = d_normed * gain[...]
        mean_1 = jnp.mean(scaled, axis=-1, keepdims=True)
        mean_2 = jnp.mean(scaled * unit_rows, axis=-1, keepdims=True)
        d_rows[part, :] = (inv_std[part, 0:1] * (scaled - mean_1 - unit_rows * mean_2)).astype(BF)
    tail = jnp.concatenate(
        [total[:, block * LANES : (block + 1) * LANES] for block in range(3)]
        + [jnp.zeros((13, LANES), F32)],
        axis=0,
    )
    grads[pl.ds(12 * D, 16), :] = tail.astype(BF)
    rest = GRAD_ROWS - 12 * D - 16
    grads[pl.ds(12 * D + 16, rest), :] = jnp.zeros((rest, LANES), BF)


def window_pass(tok, cot, w_qkv, w_proj, norm_gain):
    def buffer(shape, kind):
        return pltpu.VMEM(shape, kind)

    return pl.pallas_call(
        window_kernel,
        out_shape=(
            jax.ShapeDtypeStruct((ROWS, D), BF),
            jax.ShapeDtypeStruct((ROWS, D), BF),
            jax.ShapeDtypeStruct((GRAD_ROWS, LANES), BF),
        ),
        scratch_shapes=[
            buffer((ROWS, 3 * D), BF),
            buffer((ROWS, D), BF),
            buffer((D, ROWS), BF),
            buffer((D, ROWS), BF),
            buffer((D, ROWS), BF),
            buffer((D, ROWS), BF),
            buffer((ROWS, 3 * D), BF),
            buffer((ROWS, D), F32),
            buffer((ROWS, LANES), F32),
            buffer((ROWS, D), BF),
        ],
        compiler_params=pltpu.CompilerParams(vmem_limit_bytes=40 * 1024 * 1024),
        cost_estimate=pl.CostEstimate(
            flops=16_000_000_000, bytes_accessed=5_000_000, transcendentals=3_200_000
        ),
    )(tok, cot, w_qkv, w_proj, norm_gain.reshape(1, D))


LATTICE = ("z", "core", "y_hi", "y_lo", "x")
FIRST = ("z", "core")
SECOND = ("y_hi",)
THIRD = ("y_lo", "x")
SIZES = {"z": 8, "core": 2, "y_hi": 4, "y_lo": 2, "x": 4}


def extent(axes):
    return int(np.prod([SIZES[axis] for axis in axes]))


def scatter_sum(rows, axes):
    count = extent(axes)
    parts = rows.reshape(count, rows.shape[0] // count, LANES)
    arrived = lax.all_to_all(parts, axes, 0, 0)
    return jnp.sum(arrived.astype(F32), axis=0).astype(BF)


def everywhere(rows, axes):
    count = extent(axes)
    return lax.all_to_all(jnp.broadcast_to(rows[None], (count,) + rows.shape), axes, 0, 0)


def sum_over_devices(rows):
    rows = scatter_sum(rows, ("core",))
    rows = scatter_sum(rows, ("x",))
    rows = scatter_sum(rows, ("y_hi", "y_lo"))
    rows = jnp.sum(everywhere(rows, ("z",)).astype(F32), axis=0).astype(BF)
    for axes in (("y_hi", "y_lo"), ("x",), ("core",)):
        rows = everywhere(rows, axes).reshape(-1, LANES)
    return rows


def device_at(first, second, third):
    return ((first % 16) * 4 + second % 4) * 8 + third % 8


def route(kind, back):
    pairs = []
    for first in range(16):
        for second in range(4):
            for third in range(8):
                sign = 1 if first % 2 else -1
                move = {
                    "first": (first - 1, second, third),
                    "second": (first, second + sign, third),
                    "third": (first, second, third + sign),
                }[kind]
                pair = (device_at(first, second, third), device_at(*move))
                pairs.append(pair[::-1] if back else pair)
    return pairs


def send(block, kind, back=False):
    return lax.ppermute(block, LATTICE, route(kind, back))


def octants(block):
    grid = block.reshape(2, HALF, 2, HALF, 2, HALF, D)
    return grid.transpose(0, 2, 4, 1, 3, 5, 6).reshape(2, 2, 2, PIECE, D)


def whole(pieces):
    grid = pieces.reshape(2, 2, 2, HALF, HALF, HALF, D)
    return grid.transpose(0, 3, 1, 4, 2, 5, 6).reshape(WIN, WIN, WIN, D)


def slots(pieces, odd):
    even_order = jnp.stack([pieces[0], pieces[1, ::-1, ::-1]])
    odd_order = jnp.stack([pieces[0, ::-1, ::-1], pieces[1]])
    return jnp.where(odd, odd_order, even_order)


def gather_window(tok, cot):
    both = jnp.stack([tok, cot], axis=3)
    both = jnp.stack([both[1], send(both[0], "first")])
    both = jnp.stack([both[:, 0], send(both[:, 1], "second")])
    both = jnp.stack([both[:, :, 0], send(both[:, :, 1], "third")])
    windows = both.transpose(3, 0, 1, 2, 4, 5).reshape(2, ROWS, D)
    return windows[0], windows[1]


def return_window(branch, d_rows):
    both = jnp.stack([branch, d_rows]).reshape(2, 2, 2, 2, PIECE, D).transpose(1, 2, 3, 0, 4, 5)
    both = jnp.stack([both[0], send(both[1], "third", True)], axis=2)
    both = jnp.stack([both[0], send(both[1], "second", True)], axis=1)
    both = jnp.stack([send(both[1], "first", True), both[0]])
    return both[:, :, :, 0], both[:, :, :, 1]


def local(tokens, frozen, cotangent, w_qkv, w_proj, norm_gain):
    odd = lax.axis_index("core") == 1
    keep = frozen[..., None] == 1
    kept = jnp.where(keep, tokens, jnp.zeros_like(tokens))
    tok, cot = gather_window(slots(octants(kept), odd), slots(octants(cotangent), odd))
    branch, d_rows, grads = window_pass(tok, cot, w_qkv, w_proj, norm_gain)
    total = sum_over_devices(grads)
    branch, d_rows = return_window(branch, d_rows)
    branch = whole(slots(branch, odd))
    d_rows = whole(slots(d_rows, odd))
    block_out = (kept.astype(F32) + branch.astype(F32)).astype(BF)
    tokens_grad = jnp.where(keep, cotangent.astype(F32) + d_rows.astype(F32), 0.0).astype(BF)
    grad_scale = (ROWS * 512) ** (-0.5)
    blocks = total[: 12 * D].reshape(12, D, LANES).astype(F32) * grad_scale
    qkv_grad = blocks[:9].transpose(1, 0, 2).reshape(D, 3 * D)
    proj_grad = blocks[9:].transpose(1, 0, 2).reshape(D, D)
    gain_grad = total[12 * D : 12 * D + 3].reshape(D).astype(F32) * grad_scale
    return block_out, tokens_grad, qkv_grad, proj_grad, gain_grad


def solution(mesh):
    inner = Mesh(mesh.devices.reshape([SIZES[axis] for axis in LATTICE]), LATTICE)
    lattice = P(FIRST, SECOND, THIRD)
    wide = P(FIRST, SECOND, THIRD, None)
    return jax.shard_map(
        local,
        mesh=inner,
        in_specs=(wide, lattice, wide, P(), P(), P()),
        out_specs=(wide, wide, P(), P(), P()),
        check_vma=False,
    )
```

```python
import jax
import jax.numpy as jnp
import numpy as np
from jax import lax
from jax.experimental import pallas as pl
from jax.experimental.pallas import tpu as pltpu
from jax.sharding import Mesh, PartitionSpec as P

D = 384
HEADS = 12
HDIM = 32
WIN = 8
HALF = WIN // 2
ROWS = WIN**3
PIECE = HALF**3
EPSILON = 1e-05
BF = jnp.bfloat16
F32 = jnp.float32
LANES = 128
PER = LANES // HDIM
CHUNK = 256
SCALE = HDIM ** (-0.5)
LOG2E = 1.4426950408889634
GRAD_ROWS = 5120


def dot(left, right):
    return jnp.dot(left, right, preferred_element_type=F32)


def dot_t(left, right):
    return lax.dot_general(left, right, (((1,), (1,)), ((), ())), preferred_element_type=F32)


def window_kernel(
    own, behind, side_1, side_2, side_3, w_qkv, w_proj, gain, back_0, back_1, back_2, back_3, grads,
    cot, qkv, d_mixed, keys_t, values_t, mixed_t, d_queries_t, d_qkv, unit, inv_std, normed,
):
    step = 2 * PIECE
    gain_row = gain[...]

    def arrived(group, array):
        if group == 0:
            return own[0, array], behind[0, array]
        side = (side_1, side_2, side_3)[group - 1]
        return side[0, array], side[1, array]

    for group in range(4):
        part = pl.ds(group * step, step)
        cot[part, :] = jnp.concatenate(arrived(group, 1), axis=0)
        rows = jnp.concatenate(arrived(group, 0), axis=0).astype(F32)
        centred = rows - jnp.mean(rows, axis=-1, keepdims=True)
        inverse = lax.rsqrt(jnp.mean(centred * centred, axis=-1, keepdims=True) + EPSILON)
        unit_rows = centred * inverse
        unit[part, :] = unit_rows
        inv_std[part, :] = jnp.broadcast_to(inverse, (step, LANES))
        normed[part, :] = (unit_rows * gain_row).astype(BF)
    qkv[...] = dot(normed[...], w_qkv[...]).astype(BF)
    d_mixed[...] = dot_t(cot[...], w_proj[...]).astype(BF)
    keys_t[...] = qkv[:, D : 2 * D].T
    values_t[...] = qkv[:, 2 * D :].T
    lane = lax.broadcasted_iota(jnp.int32, (1, LANES), 1)

    def head_block(index, carry):
        offset = pl.multiple_of(index * LANES, LANES)
        q_block = qkv[:, pl.ds(offset, LANES)]
        k_block = qkv[:, pl.ds(offset + D, LANES)]
        v_block = qkv[:, pl.ds(offset + 2 * D, LANES)]
        m_block = d_mixed[:, pl.ds(offset, LANES)]
        d_keys = jnp.zeros((ROWS, LANES), F32)
        d_values = jnp.zeros((ROWS, LANES), F32)
        for head in range(PER):
            mine = (lane // HDIM) == head
            q_head = jnp.where(mine, q_block, jnp.zeros_like(q_block))
            m_head = jnp.where(mine, m_block, jnp.zeros_like(m_block))
            rows = pl.ds(offset + head * HDIM, HDIM)
            k_head_t = keys_t[rows, :]
            v_head_t = values_t[rows, :]
            for start in range(0, ROWS, CHUNK):
                q_part = q_head[start : start + CHUNK]
                m_part = m_head[start : start + CHUNK]
                scores = dot_t(k_block, q_part)
                top = jnp.max(scores, axis=0, keepdims=True)
                terms = jnp.exp2(scores * (SCALE * LOG2E) - top * (SCALE * LOG2E))
                inverse = 1.0 / jnp.sum(terms, axis=0, keepdims=True)
                probs_low = (terms * inverse).astype(BF)
                d_probs = dot_t(v_block, m_part)
                mixed_t[rows, pl.ds(start, CHUNK)] = dot(v_head_t, probs_low).astype(BF)
                d_values = d_values + dot(probs_low, m_part)
                scaled = inverse * SCALE
                shift = jnp.sum(terms * d_probs, axis=0, keepdims=True) * (inverse * scaled)
                d_scores = (terms * (d_probs * scaled - shift)).astype(BF)
                d_queries_t[rows, pl.ds(start, CHUNK)] = dot(k_head_t, d_scores).astype(BF)
                d_keys = d_keys + dot(d_scores, q_part)
        d_qkv[:, pl.ds(offset + D, LANES)] = d_keys.astype(BF)
        d_qkv[:, pl.ds(offset + 2 * D, LANES)] = d_values.astype(BF)
        return carry

    lax.fori_loop(0, D // LANES, head_block, 0)
    d_qkv[:, pl.ds(0, D)] = d_queries_t[...].T
    branch = dot(mixed_t[...].T, w_proj[...]).astype(BF)
    backs = (back_0, back_1, back_2, back_3)
    for group in range(4):
        for place in range(2):
            start = (2 * group + place) * PIECE
            backs[group][place, 0] = branch[start : start + PIECE]
    normed_t = normed[...].T
    for block in range(9):
        term = dot(normed_t, d_qkv[:, block * LANES : (block + 1) * LANES])
        grads[pl.ds(block * D, D), :] = term.astype(BF)
    for block in range(3):
        term = dot(mixed_t[...], cot[:, block * LANES : (block + 1) * LANES])
        grads[pl.ds((9 + block) * D, D), :] = term.astype(BF)
    total = jnp.zeros((1, D), F32)
    for group in range(4):
        part = pl.ds(group * step, step)
        d_normed = dot_t(d_qkv[part, :], w_qkv[...])
        unit_rows = unit[part, :]
        total = total + jnp.sum(d_normed * unit_rows, axis=0, keepdims=True)
        scaled = d_normed * gain_row
        mean_1 = jnp.mean(scaled, axis=-1, keepdims=True)
        mean_2 = jnp.mean(scaled * unit_rows, axis=-1, keepdims=True)
        d_rows = (inv_std[part, 0:1] * (scaled - mean_1 - unit_rows * mean_2)).astype(BF)
        backs[group][0, 1] = d_rows[:PIECE]
        backs[group][1, 1] = d_rows[PIECE:]
    tail = jnp.concatenate(
        [total[:, block * LANES : (block + 1) * LANES] for block in range(3)]
        + [jnp.zeros((13, LANES), F32)],
        axis=0,
    )
    grads[pl.ds(12 * D, 16), :] = tail.astype(BF)
    rest = GRAD_ROWS - 12 * D - 16
    grads[pl.ds(12 * D + 16, rest), :] = jnp.zeros((rest, LANES), BF)


def order(odd, upper, inverse):
    flip = odd if upper == 0 else 1 - odd
    shape = (WIN * WIN, WIN * WIN)
    row = lax.broadcasted_iota(jnp.int32, shape, 1 if inverse else 0)
    token = lax.broadcasted_iota(jnp.int32, shape, 0 if inverse else 1)
    along_y = ((row >> 5) ^ flip) * HALF + ((row >> 2) & 3)
    along_z = (((row >> 4) & 1) ^ flip) * HALF + (row & 3)
    return token == along_y * WIN + along_z


def ones_where(chosen):
    return jnp.where(chosen, 1.0, 0.0)


def cut_kernel(odd, tokens, frozen, cotangent, own, ahead):
    for upper, target in ((0, ahead), (1, own)):
        matrix = ones_where(order(odd[0], upper, False))
        for plane in range(HALF):
            index = upper * HALF + plane
            part = pl.ds(index * WIN * WIN, WIN * WIN)
            keep = ones_where(frozen[index : index + 1, :] == 1)
            kept = dot((matrix * keep).astype(BF), tokens[part, :]).astype(BF)
            cot = dot(matrix.astype(BF), cotangent[part, :]).astype(BF)
            for group in range(4):
                rows = slice(group * 16, group * 16 + 16)
                target[group, 0, pl.ds(plane * 16, 16), :] = kept[rows]
                target[group, 1, pl.ds(plane * 16, 16), :] = cot[rows]


def join_kernel(odd, tokens, frozen, cotangent, home_0, home_1, home_2, home_3, ahead, block_out, tokens_grad):
    homes = (home_0, home_1, home_2, home_3)
    shape = (WIN * WIN, WIN * WIN)
    diagonal = ones_where(lax.broadcasted_iota(jnp.int32, shape, 0) == lax.broadcasted_iota(jnp.int32, shape, 1))
    for upper in range(2):
        matrix = ones_where(order(odd[0], upper, True)).astype(BF)
        for plane in range(HALF):
            index = upper * HALF + plane
            part = pl.ds(index * WIN * WIN, WIN * WIN)
            keep = (diagonal * ones_where(frozen[index : index + 1, :] == 1)).astype(BF)
            rows = pl.ds(plane * 16, 16)

            def pieces(array):
                if upper:
                    found = [homes[group][0, array, rows, :] for group in range(4)]
                else:
                    found = [ahead[group, array, rows, :] for group in range(4)]
                return dot(matrix, jnp.concatenate(found, axis=0))

            block_out[part, :] = (dot(keep, tokens[part, :]) + pieces(0)).astype(BF)
            grown = (cotangent[part, :].astype(F32) + pieces(1)).astype(BF)
            tokens_grad[part, :] = dot(keep, grown).astype(BF)


def total_kernel(copies, parts, out):
    total = parts[0].astype(F32)
    for index in range(1, parts.shape[0]):
        total = total + parts[index].astype(F32)
    total = total.astype(BF)
    for index in range(copies):
        out[index] = total


def total_of(parts, copies):
    return pl.pallas_call(
        lambda *refs: total_kernel(copies, *refs),
        out_shape=jax.ShapeDtypeStruct((copies,) + parts.shape[1:], BF),
    )(parts)


def grads_kernel(core, mine, other, qkv_grad, proj_grad, gain_grad):
    grad_scale = (ROWS * 512) ** (-0.5)
    half = GRAD_ROWS // 2
    first = core[0] == 0

    def rows(start, stop):
        found = []
        if start < half:
            part = pl.ds(start, min(stop, half) - start)
            found.append(jnp.where(first, mine[part, :].astype(F32), other[part, :].astype(F32)))
        if stop > half:
            low = max(start, half)
            part = pl.ds(low - half, stop - low)
            found.append(jnp.where(first, other[part, :].astype(F32), mine[part, :].astype(F32)))
        return (found[0] if len(found) == 1 else jnp.concatenate(found, axis=0)) * grad_scale

    for block in range(12):
        target, column = (qkv_grad, block) if block < 9 else (proj_grad, block - 9)
        target[:, column * LANES : (column + 1) * LANES] = rows(block * D, (block + 1) * D)
    tail = rows(12 * D, 12 * D + 16)
    for block in range(3):
        gain_grad[:, block * LANES : (block + 1) * LANES] = tail[block : block + 1]


SCALAR = pl.BlockSpec(memory_space=pltpu.SMEM)
WHOLE = pl.BlockSpec(memory_space=pltpu.VMEM)


def window_pass(own, behind, sides, w_qkv, w_proj, norm_gain):
    def buffer(shape, kind):
        return pltpu.VMEM(shape, kind)

    return pl.pallas_call(
        window_kernel,
        out_shape=(jax.ShapeDtypeStruct((2, 2, PIECE, D), BF),) * 4
        + (jax.ShapeDtypeStruct((GRAD_ROWS, LANES), BF),),
        scratch_shapes=[
            buffer((ROWS, D), BF),
            buffer((ROWS, 3 * D), BF),
            buffer((ROWS, D), BF),
            buffer((D, ROWS), BF),
            buffer((D, ROWS), BF),
            buffer((D, ROWS), BF),
            buffer((D, ROWS), BF),
            buffer((ROWS, 3 * D), BF),
            buffer((ROWS, D), F32),
            buffer((ROWS, LANES), F32),
            buffer((ROWS, D), BF),
        ],
        compiler_params=pltpu.CompilerParams(vmem_limit_bytes=40 * 1024 * 1024),
        cost_estimate=pl.CostEstimate(
            flops=16_000_000_000, bytes_accessed=5_000_000, transcendentals=3_200_000
        ),
    )(own, behind, *sides, w_qkv, w_proj, norm_gain.reshape(1, D))


LATTICE = ("z_hi", "z_lo", "core", "y_hi", "y_lo", "x")
FIRST = ("z_hi", "z_lo", "core")
SECOND = ("y_hi",)
THIRD = ("y_lo", "x")
SIZES = {"z_hi": 4, "z_lo": 2, "core": 2, "y_hi": 4, "y_lo": 2, "x": 4}
NEAR = ("x", "y_lo", "z_lo")
FAR = ("y_hi", "z_hi")
GROUP = 16


def sum_over_devices(rows):
    halves = lax.all_to_all(rows.reshape(2, GRAD_ROWS // 2, LANES), "core", 0, 0)
    parts = total_of(halves, 1).reshape(GROUP, GRAD_ROWS // 2 // GROUP, LANES)
    parts = lax.all_to_all(parts, NEAR, 0, 0)
    parts = lax.all_to_all(total_of(parts, GROUP), FAR, 0, 0)
    parts = lax.all_to_all(total_of(parts, GROUP), NEAR, 0, 0)
    mine = parts.reshape(GRAD_ROWS // 2, LANES)
    return mine, lax.ppermute(mine, "core", [(0, 1), (1, 0)])


def device_at(first, second, third):
    return ((first % 16) * 4 + second % 4) * 8 + third % 8


def route(kind, back):
    pairs = []
    for first in range(16):
        for second in range(4):
            for third in range(8):
                sign = 1 if first % 2 else -1
                if kind == 0:
                    move = (first - 1, second, third)
                else:
                    move = (first, second + sign * (kind >> 1), third + sign * (kind & 1))
                pair = (device_at(first, second, third), device_at(*move))
                pairs.append(pair[::-1] if back else pair)
    return pairs


def send(block, kind, back=False):
    return lax.ppermute(block, LATTICE, route(kind, back))


def local(tokens, frozen, cotangent, w_qkv, w_proj, norm_gain):
    core = lax.axis_index("core").reshape(1)
    token_rows, cot_rows = tokens.reshape(ROWS, D), cotangent.reshape(ROWS, D)
    frozen_rows = frozen.reshape(WIN, WIN * WIN)
    own, ahead = pl.pallas_call(
        cut_kernel,
        out_shape=(jax.ShapeDtypeStruct((4, 2, PIECE, D), BF),) * 2,
        in_specs=[SCALAR, WHOLE, WHOLE, WHOLE],
    )(core, token_rows, frozen_rows, cot_rows)
    behind = send(ahead, 0)
    sides = [None] * 4
    for kind in (3, 2, 1):
        sides[kind] = send(jnp.stack([own[kind], behind[kind]]), kind)
    *backs, grads = window_pass(own, behind, sides[1:], w_qkv, w_proj, norm_gain)
    mine, other = sum_over_devices(grads)
    for kind in (3, 2, 1):
        backs[kind] = send(backs[kind], kind, True)
    ahead = send(jnp.stack([back[1] for back in backs]), 0, True)
    block_out, tokens_grad = pl.pallas_call(
        join_kernel,
        out_shape=(jax.ShapeDtypeStruct((ROWS, D), BF),) * 2,
        in_specs=[SCALAR] + [WHOLE] * 8,
    )(core, token_rows, frozen_rows, cot_rows, *backs, ahead)
    qkv_grad, proj_grad, gain_grad = pl.pallas_call(
        grads_kernel,
        out_shape=(
            jax.ShapeDtypeStruct((D, 3 * D), F32),
            jax.ShapeDtypeStruct((D, D), F32),
            jax.ShapeDtypeStruct((1, D), F32),
        ),
        in_specs=[SCALAR, WHOLE, WHOLE],
    )(core, mine, other)
    shape = (WIN, WIN, WIN, D)
    return block_out.reshape(shape), tokens_grad.reshape(shape), qkv_grad, proj_grad, gain_grad.reshape(D)


def solution(mesh):
    inner = Mesh(mesh.devices.reshape([SIZES[axis] for axis in LATTICE]), LATTICE)
    lattice = P(FIRST, SECOND, THIRD)
    wide = P(FIRST, SECOND, THIRD, None)
    return jax.shard_map(
        local,
        mesh=inner,
        in_specs=(wide, lattice, wide, P(), P(), P()),
        out_specs=(wide, wide, P(), P(), P()),
        check_vma=False,
    )
```

```python
import jax
import jax.numpy as jnp
import numpy as np
from jax import lax
from jax.experimental import pallas as pl
from jax.experimental.pallas import tpu as pltpu
from jax.sharding import Mesh, PartitionSpec as P

D = 384
HEADS = 12
HDIM = 32
WIN = 8
HALF = WIN // 2
ROWS = WIN**3
PIECE = HALF**3
EPSILON = 1e-05
BF = jnp.bfloat16
F32 = jnp.float32
LANES = 128
PER = LANES // HDIM
CHUNK = 256
SCALE = HDIM ** (-0.5)
LOG2E = 1.4426950408889634
GRAD_ROWS = 12 * D


def dot(left, right):
    return jnp.dot(left, right, preferred_element_type=F32)


def dot_t(left, right):
    return lax.dot_general(left, right, (((1,), (1,)), ((), ())), preferred_element_type=F32)


def window_kernel(
    own, behind, side_1, side_2, side_3, w_qkv, w_proj, gain, back_0, back_1, back_2, back_3, grads,
    cot, qkv, d_mixed, keys_t, values_t, mixed_t, d_queries_t, d_qkv, unit, inv_std, normed,
):
    step = 2 * PIECE
    gain_row = gain[...]

    def arrived(group, array):
        if group == 0:
            return own[0, array], behind[0, array]
        side = (side_1, side_2, side_3)[group - 1]
        return side[0, array], side[1, array]

    for group in range(4):
        part = pl.ds(group * step, step)
        cot[part, :] = jnp.concatenate(arrived(group, 1), axis=0)
        rows = jnp.concatenate(arrived(group, 0), axis=0).astype(F32)
        centred = rows - jnp.mean(rows, axis=-1, keepdims=True)
        inverse = lax.rsqrt(jnp.mean(centred * centred, axis=-1, keepdims=True) + EPSILON)
        unit_rows = centred * inverse
        unit[part, :] = unit_rows
        inv_std[part, :] = jnp.broadcast_to(inverse, (step, LANES))
        normed[part, :] = (unit_rows * gain_row).astype(BF)
    qkv[...] = dot(normed[...], w_qkv[...]).astype(BF)
    d_mixed[...] = dot_t(cot[...], w_proj[...]).astype(BF)
    keys_t[...] = qkv[:, D : 2 * D].T
    values_t[...] = qkv[:, 2 * D :].T
    lane = lax.broadcasted_iota(jnp.int32, (1, LANES), 1)

    def head_block(index, carry):
        offset = pl.multiple_of(index * LANES, LANES)
        q_block = qkv[:, pl.ds(offset, LANES)]
        k_block = qkv[:, pl.ds(offset + D, LANES)]
        v_block = qkv[:, pl.ds(offset + 2 * D, LANES)]
        m_block = d_mixed[:, pl.ds(offset, LANES)]
        d_keys = jnp.zeros((ROWS, LANES), F32)
        d_values = jnp.zeros((ROWS, LANES), F32)
        for head in range(PER):
            mine = (lane // HDIM) == head
            q_head = jnp.where(mine, q_block, jnp.zeros_like(q_block))
            m_head = jnp.where(mine, m_block, jnp.zeros_like(m_block))
            rows = pl.ds(offset + head * HDIM, HDIM)
            k_head_t = keys_t[rows, :]
            v_head_t = values_t[rows, :]
            for start in range(0, ROWS, CHUNK):
                q_part = q_head[start : start + CHUNK]
                m_part = m_head[start : start + CHUNK]
                scores = dot_t(k_block, q_part)
                top = jnp.max(scores, axis=0, keepdims=True)
                terms = jnp.exp2(scores * (SCALE * LOG2E) - top * (SCALE * LOG2E))
                inverse = 1.0 / jnp.sum(terms, axis=0, keepdims=True)
                probs_low = (terms * inverse).astype(BF)
                d_probs = dot_t(v_block, m_part)
                mixed_t[rows, pl.ds(start, CHUNK)] = dot(v_head_t, probs_low).astype(BF)
                d_values = d_values + dot(probs_low, m_part)
                scaled = inverse * SCALE
                shift = jnp.sum(terms * d_probs, axis=0, keepdims=True) * (inverse * scaled)
                d_scores = (terms * (d_probs * scaled - shift)).astype(BF)
                d_queries_t[rows, pl.ds(start, CHUNK)] = dot(k_head_t, d_scores).astype(BF)
                d_keys = d_keys + dot(d_scores, q_part)
        d_qkv[:, pl.ds(offset + D, LANES)] = d_keys.astype(BF)
        d_qkv[:, pl.ds(offset + 2 * D, LANES)] = d_values.astype(BF)
        return carry

    lax.fori_loop(0, D // LANES, head_block, 0)
    d_qkv[:, pl.ds(0, D)] = d_queries_t[...].T
    branch = dot(mixed_t[...].T, w_proj[...]).astype(BF)
    backs = (back_0, back_1, back_2, back_3)
    for group in range(4):
        for place in range(2):
            start = (2 * group + place) * PIECE
            backs[group][place, 0] = branch[start : start + PIECE]
    normed_t = normed[...].T
    for block in range(9):
        term = dot(normed_t, d_qkv[:, block * LANES : (block + 1) * LANES])
        grads[pl.ds(block * D, D), :] = term.astype(BF)
    for block in range(3):
        term = dot(mixed_t[...], cot[:, block * LANES : (block + 1) * LANES])
        grads[pl.ds((9 + block) * D, D), :] = term.astype(BF)
    for group in range(4):
        part = pl.ds(group * step, step)
        d_normed = dot_t(d_qkv[part, :], w_qkv[...])
        unit_rows = unit[part, :]
        scaled = d_normed * gain_row
        mean_1 = jnp.mean(scaled, axis=-1, keepdims=True)
        mean_2 = jnp.mean(scaled * unit_rows, axis=-1, keepdims=True)
        d_rows = (inv_std[part, 0:1] * (scaled - mean_1 - unit_rows * mean_2)).astype(BF)
        backs[group][0, 1] = d_rows[:PIECE]
        backs[group][1, 1] = d_rows[PIECE:]


def order(odd, upper, inverse):
    flip = odd if upper == 0 else 1 - odd
    shape = (WIN * WIN, WIN * WIN)
    row = lax.broadcasted_iota(jnp.int32, shape, 1 if inverse else 0)
    token = lax.broadcasted_iota(jnp.int32, shape, 0 if inverse else 1)
    along_y = ((row >> 5) ^ flip) * HALF + ((row >> 2) & 3)
    along_z = (((row >> 4) & 1) ^ flip) * HALF + (row & 3)
    return token == along_y * WIN + along_z


def ones_where(chosen):
    return jnp.where(chosen, 1.0, 0.0)


def keep_rows(frozen):
    table = ones_where(frozen[...].reshape(WIN * WIN, WIN) == 1).astype(BF)
    column = lax.broadcasted_iota(jnp.int32, (WIN, WIN * WIN), 1)
    row = lax.broadcasted_iota(jnp.int32, (WIN, WIN * WIN), 0)
    spread = dot(table, ones_where((column & 7) == row).astype(BF))
    chosen = ones_where((column >> 3) == row)
    return [
        jnp.sum(spread[plane * WIN : (plane + 1) * WIN] * chosen, axis=0, keepdims=True)
        for plane in range(WIN)
    ]


def cut_kernel(odd, tokens, frozen, cotangent, own, ahead):
    keeps = keep_rows(frozen)
    for upper, target in ((0, ahead), (1, own)):
        matrix = ones_where(order(odd[0], upper, False))
        for plane in range(HALF):
            index = upper * HALF + plane
            part = pl.ds(index * WIN * WIN, WIN * WIN)
            kept = dot((matrix * keeps[index]).astype(BF), tokens[part, :]).astype(BF)
            cot = dot(matrix.astype(BF), cotangent[part, :]).astype(BF)
            for group in range(4):
                rows = slice(group * 16, group * 16 + 16)
                target[group, 0, pl.ds(plane * 16, 16), :] = kept[rows]
                target[group, 1, pl.ds(plane * 16, 16), :] = cot[rows]


def join_kernel(odd, tokens, frozen, cotangent, home_0, home_1, home_2, home_3, ahead, block_out, tokens_grad):
    homes = (home_0, home_1, home_2, home_3)
    keeps = keep_rows(frozen)
    shape = (WIN * WIN, WIN * WIN)
    diagonal = ones_where(lax.broadcasted_iota(jnp.int32, shape, 0) == lax.broadcasted_iota(jnp.int32, shape, 1))
    for upper in range(2):
        matrix = ones_where(order(odd[0], upper, True)).astype(BF)
        for plane in range(HALF):
            index = upper * HALF + plane
            part = pl.ds(index * WIN * WIN, WIN * WIN)
            keep = (diagonal * keeps[index]).astype(BF)
            rows = pl.ds(plane * 16, 16)

            def pieces(array):
                if upper:
                    found = [homes[group][0, array, rows, :] for group in range(4)]
                else:
                    found = [ahead[group, array, rows, :] for group in range(4)]
                return dot(matrix, jnp.concatenate(found, axis=0))

            block_out[part, :] = (dot(keep, tokens[part, :]) + pieces(0)).astype(BF)
            grown = (cotangent[part, :].astype(F32) + pieces(1)).astype(BF)
            tokens_grad[part, :] = dot(keep, grown).astype(BF)


SCALAR = pl.BlockSpec(memory_space=pltpu.SMEM)
WHOLE = pl.BlockSpec(memory_space=pltpu.VMEM)
SMALL = pltpu.CompilerParams(vmem_limit_bytes=12 * 1024 * 1024)


def total_kernel(copies, parts, *rest):
    out = rest[-1]
    total = parts[0].astype(F32)
    for index in range(1, parts.shape[0]):
        total = total + parts[index].astype(F32)
    total = total.astype(BF)
    for index in range(copies):
        out[index] = total


def total_of(parts, copies, after=()):
    return pl.pallas_call(
        lambda *refs: total_kernel(copies, *refs),
        out_shape=jax.ShapeDtypeStruct((copies,) + parts.shape[1:], BF),
        in_specs=[WHOLE] + [pl.BlockSpec(memory_space=pl.ANY)] * len(after),
        compiler_params=SMALL,
    )(parts, *after)


def grads_kernel(core, mine, other, w_qkv, gain, qkv_grad, proj_grad, gain_grad):
    grad_scale = (ROWS * 512) ** (-0.5)
    half = GRAD_ROWS // 2
    first = core[0] == 0
    weighted = jnp.zeros((D, LANES), F32)
    for block in range(12):
        start = block * D
        if start < half:
            part = pl.ds(start, D)
            found = jnp.where(first, mine[part, :].astype(F32), other[part, :].astype(F32))
        else:
            part = pl.ds(start - half, D)
            found = jnp.where(first, other[part, :].astype(F32), mine[part, :].astype(F32))
        found = found * grad_scale
        target, column = (qkv_grad, block) if block < 9 else (proj_grad, block - 9)
        columns = slice(column * LANES, (column + 1) * LANES)
        target[:, columns] = found
        if block < 9:
            weighted = weighted + found * w_qkv[:, columns].astype(F32)
    gain_grad[...] = jnp.sum(weighted.T, axis=0, keepdims=True) / gain[...]


def window_pass(own, behind, sides, w_qkv, w_proj, norm_gain):
    def buffer(shape, kind):
        return pltpu.VMEM(shape, kind)

    return pl.pallas_call(
        window_kernel,
        out_shape=(jax.ShapeDtypeStruct((2, 2, PIECE, D), BF),) * 4
        + (jax.ShapeDtypeStruct((GRAD_ROWS, LANES), BF),),
        scratch_shapes=[
            buffer((ROWS, D), BF),
            buffer((ROWS, 3 * D), BF),
            buffer((ROWS, D), BF),
            buffer((D, ROWS), BF),
            buffer((D, ROWS), BF),
            buffer((D, ROWS), BF),
            buffer((D, ROWS), BF),
            buffer((ROWS, 3 * D), BF),
            buffer((ROWS, D), F32),
            buffer((ROWS, LANES), F32),
            buffer((ROWS, D), BF),
        ],
        compiler_params=pltpu.CompilerParams(vmem_limit_bytes=40 * 1024 * 1024),
        cost_estimate=pl.CostEstimate(
            flops=16_000_000_000, bytes_accessed=5_000_000, transcendentals=3_200_000
        ),
    )(own, behind, *sides, w_qkv, w_proj, norm_gain.reshape(1, D))


LATTICE = ("z_hi", "z_lo", "core", "y_hi", "y_lo", "x")
FIRST = ("z_hi", "z_lo", "core")
SECOND = ("y_hi",)
THIRD = ("y_lo", "x")
SIZES = {"z_hi": 4, "z_lo": 2, "core": 2, "y_hi": 4, "y_lo": 2, "x": 4}
NEAR = ("x", "y_lo", "z_lo")
FAR = ("y_hi", "z_hi")
GROUP = 16


def near_sum(rows):
    halves = lax.all_to_all(rows.reshape(2, GRAD_ROWS // 2, LANES), "core", 0, 0)
    parts = total_of(halves, 1).reshape(GROUP, GRAD_ROWS // 2 // GROUP, LANES)
    parts = lax.all_to_all(parts, NEAR, 0, 0)
    return parts


def far_sum(parts, after):
    return lax.all_to_all(total_of(parts, GROUP, after), FAR, 0, 0)


def spread_sum(parts, after):
    parts = lax.all_to_all(total_of(parts, GROUP, after), NEAR, 0, 0)
    mine = parts.reshape(GRAD_ROWS // 2, LANES)
    return mine, lax.ppermute(mine, "core", [(0, 1), (1, 0)])


def device_at(first, second, third):
    return ((first % 16) * 4 + second % 4) * 8 + third % 8


def route(kind, back):
    pairs = []
    for first in range(16):
        for second in range(4):
            for third in range(8):
                sign = 1 if first % 2 else -1
                if kind == 0:
                    move = (first - 1, second, third)
                else:
                    move = (first, second + sign * (kind >> 1), third + sign * (kind & 1))
                pair = (device_at(first, second, third), device_at(*move))
                pairs.append(pair[::-1] if back else pair)
    return pairs


def send(block, kind, back=False):
    return lax.ppermute(block, LATTICE, route(kind, back))


def local(tokens, frozen, cotangent, w_qkv, w_proj, norm_gain):
    core = lax.axis_index("core").reshape(1)
    token_rows, cot_rows = tokens.reshape(ROWS, D), cotangent.reshape(ROWS, D)
    own, ahead = pl.pallas_call(
        cut_kernel,
        out_shape=(jax.ShapeDtypeStruct((4, 2, PIECE, D), BF),) * 2,
        in_specs=[SCALAR, WHOLE, WHOLE, WHOLE],
        compiler_params=SMALL,
    )(core, token_rows, frozen, cot_rows)
    behind = send(ahead, 0)
    sides = [None] * 4
    for kind in (3, 2, 1):
        sides[kind] = send(jnp.stack([own[kind], behind[kind]]), kind)
    *backs, grads = window_pass(own, behind, sides[1:], w_qkv, w_proj, norm_gain)
    parts = near_sum(grads)
    for kind in (3, 2, 1):
        backs[kind] = send(backs[kind], kind, True)
    parts = far_sum(parts, backs[1:])
    ahead = send(jnp.stack([back[1] for back in backs]), 0, True)
    block_out, tokens_grad = pl.pallas_call(
        join_kernel,
        out_shape=(jax.ShapeDtypeStruct((ROWS, D), BF),) * 2,
        in_specs=[SCALAR] + [WHOLE] * 8,
        compiler_params=SMALL,
    )(core, token_rows, frozen, cot_rows, *backs, ahead)
    mine, other = spread_sum(parts, (block_out, tokens_grad))
    qkv_grad, proj_grad, gain_grad = pl.pallas_call(
        grads_kernel,
        out_shape=(
            jax.ShapeDtypeStruct((D, 3 * D), F32),
            jax.ShapeDtypeStruct((D, D), F32),
            jax.ShapeDtypeStruct((1, D), F32),
        ),
        in_specs=[SCALAR] + [WHOLE] * 4,
        compiler_params=SMALL,
    )(core, mine, other, w_qkv, norm_gain.reshape(1, D))
    shape = (WIN, WIN, WIN, D)
    return block_out.reshape(shape), tokens_grad.reshape(shape), qkv_grad, proj_grad, gain_grad.reshape(D)


def solution(mesh):
    inner = Mesh(mesh.devices.reshape([SIZES[axis] for axis in LATTICE]), LATTICE)
    lattice = P(FIRST, SECOND, THIRD)
    wide = P(FIRST, SECOND, THIRD, None)
    return jax.shard_map(
        local,
        mesh=inner,
        in_specs=(wide, lattice, wide, P(), P(), P()),
        out_specs=(wide, wide, P(), P(), P()),
        check_vma=False,
    )
```

```python
import jax
import jax.numpy as jnp
import numpy as np
from jax import lax
from jax.experimental import pallas as pl
from jax.experimental.pallas import tpu as pltpu
from jax.sharding import Mesh, PartitionSpec as P

D = 384
HEADS = 12
HDIM = 32
WIN = 8
HALF = WIN // 2
ROWS = WIN**3
PIECE = HALF**3
EPSILON = 1e-05
BF = jnp.bfloat16
F32 = jnp.float32
LANES = 128
PER = LANES // HDIM
CHUNK = 256
SCALE = HDIM ** (-0.5)
LOG2E = 1.4426950408889634
GRAD_ROWS = 12 * D


def dot(left, right):
    return jnp.dot(left, right, preferred_element_type=F32)


def dot_t(left, right):
    return lax.dot_general(left, right, (((1,), (1,)), ((), ())), preferred_element_type=F32)


def window_kernel(
    own, behind, side_1, side_2, side_3, w_qkv, w_proj, gain, back_0, back_1, back_2, back_3, grads,
    cot, qkv, d_mixed, keys_t, values_t, mixed_t, d_queries_t, d_qkv, unit, inv_std, normed,
):
    step = 2 * PIECE
    gain_row = gain[...]

    def arrived(group, array):
        if group == 0:
            return own[0, array], behind[0, array]
        side = (side_1, side_2, side_3)[group - 1]
        return side[0, array], side[1, array]

    for group in range(4):
        part = pl.ds(group * step, step)
        cot[part, :] = jnp.concatenate(arrived(group, 1), axis=0)
        rows = jnp.concatenate(arrived(group, 0), axis=0).astype(F32)
        centred = rows - jnp.mean(rows, axis=-1, keepdims=True)
        inverse = lax.rsqrt(jnp.mean(centred * centred, axis=-1, keepdims=True) + EPSILON)
        unit_rows = centred * inverse
        unit[part, :] = unit_rows
        inv_std[part, :] = jnp.broadcast_to(inverse, (step, LANES))
        normed[part, :] = (unit_rows * gain_row).astype(BF)
    qkv[...] = dot(normed[...], w_qkv[...]).astype(BF)
    d_mixed[...] = dot_t(cot[...], w_proj[...]).astype(BF)
    keys_t[...] = qkv[:, D : 2 * D].T
    values_t[...] = qkv[:, 2 * D :].T
    lane = lax.broadcasted_iota(jnp.int32, (1, LANES), 1)

    def head_block(index, carry):
        offset = pl.multiple_of(index * LANES, LANES)
        q_block = qkv[:, pl.ds(offset, LANES)]
        k_block = qkv[:, pl.ds(offset + D, LANES)]
        v_block = qkv[:, pl.ds(offset + 2 * D, LANES)]
        m_block = d_mixed[:, pl.ds(offset, LANES)]
        d_keys = jnp.zeros((ROWS, LANES), F32)
        d_values = jnp.zeros((ROWS, LANES), F32)
        for head in range(PER):
            mine = (lane // HDIM) == head
            q_head = jnp.where(mine, q_block, jnp.zeros_like(q_block))
            m_head = jnp.where(mine, m_block, jnp.zeros_like(m_block))
            rows = pl.ds(offset + head * HDIM, HDIM)
            k_head_t = keys_t[rows, :]
            v_head_t = values_t[rows, :]
            for start in range(0, ROWS, CHUNK):
                q_part = q_head[start : start + CHUNK]
                m_part = m_head[start : start + CHUNK]
                scores = dot_t(k_block, q_part)
                top = jnp.max(scores, axis=0, keepdims=True)
                terms = jnp.exp2(scores * (SCALE * LOG2E) - top * (SCALE * LOG2E))
                inverse = 1.0 / jnp.sum(terms, axis=0, keepdims=True)
                probs_low = (terms * inverse).astype(BF)
                d_probs = dot_t(v_block, m_part)
                mixed_t[rows, pl.ds(start, CHUNK)] = dot(v_head_t, probs_low).astype(BF)
                d_values = d_values + dot(probs_low, m_part)
                scaled = inverse * SCALE
                shift = jnp.sum(terms * d_probs, axis=0, keepdims=True) * (inverse * scaled)
                d_scores = (terms * (d_probs * scaled - shift)).astype(BF)
                d_queries_t[rows, pl.ds(start, CHUNK)] = dot(k_head_t, d_scores).astype(BF)
                d_keys = d_keys + dot(d_scores, q_part)
        d_qkv[:, pl.ds(offset + D, LANES)] = d_keys.astype(BF)
        d_qkv[:, pl.ds(offset + 2 * D, LANES)] = d_values.astype(BF)
        return carry

    lax.fori_loop(0, D // LANES, head_block, 0)
    d_qkv[:, pl.ds(0, D)] = d_queries_t[...].T
    branch = dot(mixed_t[...].T, w_proj[...]).astype(BF)
    backs = (back_0, back_1, back_2, back_3)
    for group in range(4):
        for place in range(2):
            start = (2 * group + place) * PIECE
            backs[group][place, 0] = branch[start : start + PIECE]
    normed_t = normed[...].T
    for block in range(9):
        term = dot(normed_t, d_qkv[:, block * LANES : (block + 1) * LANES])
        grads[pl.ds(block * D, D), :] = term.astype(BF)
    for block in range(3):
        term = dot(mixed_t[...], cot[:, block * LANES : (block + 1) * LANES])
        grads[pl.ds((9 + block) * D, D), :] = term.astype(BF)
    for group in range(4):
        part = pl.ds(group * step, step)
        d_normed = dot_t(d_qkv[part, :], w_qkv[...])
        unit_rows = unit[part, :]
        scaled = d_normed * gain_row
        mean_1 = jnp.mean(scaled, axis=-1, keepdims=True)
        mean_2 = jnp.mean(scaled * unit_rows, axis=-1, keepdims=True)
        d_rows = (inv_std[part, 0:1] * (scaled - mean_1 - unit_rows * mean_2)).astype(BF)
        backs[group][0, 1] = d_rows[:PIECE]
        backs[group][1, 1] = d_rows[PIECE:]


def order(odd, upper, inverse):
    flip = odd if upper == 0 else 1 - odd
    shape = (WIN * WIN, WIN * WIN)
    row = lax.broadcasted_iota(jnp.int32, shape, 1 if inverse else 0)
    token = lax.broadcasted_iota(jnp.int32, shape, 0 if inverse else 1)
    along_y = ((row >> 5) ^ flip) * HALF + ((row >> 2) & 3)
    along_z = (((row >> 4) & 1) ^ flip) * HALF + (row & 3)
    return token == along_y * WIN + along_z


def ones_where(chosen):
    return jnp.where(chosen, 1.0, 0.0)


def keep_rows(frozen):
    table = ones_where(frozen[...].reshape(WIN * WIN, WIN) == 1).astype(BF)
    column = lax.broadcasted_iota(jnp.int32, (WIN, WIN * WIN), 1)
    row = lax.broadcasted_iota(jnp.int32, (WIN, WIN * WIN), 0)
    spread = dot(table, ones_where((column & 7) == row).astype(BF))
    chosen = ones_where((column >> 3) == row)
    return [
        jnp.sum(spread[plane * WIN : (plane + 1) * WIN] * chosen, axis=0, keepdims=True)
        for plane in range(WIN)
    ]


def cut_kernel(odd, tokens_in, frozen_in, cotangent_in, own, ahead, tokens, frozen, cotangent, arrivals):
    moves = [
        pltpu.make_async_copy(source, target, arrivals.at[index])
        for index, (source, target) in enumerate(
            ((frozen_in, frozen), (tokens_in, tokens), (cotangent_in, cotangent))
        )
    ]
    for move in moves:
        move.start()
    for move in moves:
        move.wait()
    keeps = keep_rows(frozen)
    for upper, target in ((0, ahead), (1, own)):
        matrix = ones_where(order(odd[0], upper, False))
        for plane in range(HALF):
            index = upper * HALF + plane
            part = pl.ds(index * WIN * WIN, WIN * WIN)
            kept = dot((matrix * keeps[index]).astype(BF), tokens[part, :]).astype(BF)
            cot = dot(matrix.astype(BF), cotangent[part, :]).astype(BF)
            for group in range(4):
                rows = slice(group * 16, group * 16 + 16)
                target[group, 0, pl.ds(plane * 16, 16), :] = kept[rows]
                target[group, 1, pl.ds(plane * 16, 16), :] = cot[rows]


def join_kernel(odd, tokens, frozen, cotangent, home_0, home_1, home_2, home_3, ahead, block_out, tokens_grad):
    homes = (home_0, home_1, home_2, home_3)
    keeps = keep_rows(frozen)
    shape = (WIN * WIN, WIN * WIN)
    diagonal = ones_where(lax.broadcasted_iota(jnp.int32, shape, 0) == lax.broadcasted_iota(jnp.int32, shape, 1))
    for upper in range(2):
        matrix = ones_where(order(odd[0], upper, True)).astype(BF)
        for plane in range(HALF):
            index = upper * HALF + plane
            part = pl.ds(index * WIN * WIN, WIN * WIN)
            keep = (diagonal * keeps[index]).astype(BF)
            rows = pl.ds(plane * 16, 16)

            def pieces(array):
                if upper:
                    found = [homes[group][0, array, rows, :] for group in range(4)]
                else:
                    found = [ahead[group, array, rows, :] for group in range(4)]
                return dot(matrix, jnp.concatenate(found, axis=0))

            block_out[part, :] = (dot(keep, tokens[part, :]) + pieces(0)).astype(BF)
            grown = (cotangent[part, :].astype(F32) + pieces(1)).astype(BF)
            tokens_grad[part, :] = dot(keep, grown).astype(BF)


SCALAR = pl.BlockSpec(memory_space=pltpu.SMEM)
WHOLE = pl.BlockSpec(memory_space=pltpu.VMEM)
SMALL = pltpu.CompilerParams(vmem_limit_bytes=12 * 1024 * 1024)


def total_kernel(copies, parts, *rest):
    out = rest[-1]
    total = parts[0].astype(F32)
    for index in range(1, parts.shape[0]):
        total = total + parts[index].astype(F32)
    total = total.astype(BF)
    for index in range(copies):
        out[index] = total


def total_of(parts, copies, after=()):
    return pl.pallas_call(
        lambda *refs: total_kernel(copies, *refs),
        out_shape=jax.ShapeDtypeStruct((copies,) + parts.shape[1:], BF),
        in_specs=[WHOLE] + [pl.BlockSpec(memory_space=pl.ANY)] * len(after),
        compiler_params=SMALL,
    )(parts, *after)


def grads_kernel(core, mine, other, w_qkv, gain, qkv_grad, proj_grad, gain_grad):
    grad_scale = (ROWS * 512) ** (-0.5)
    half = GRAD_ROWS // 2
    first = core[0] == 0
    weighted = jnp.zeros((D, LANES), F32)
    for block in range(12):
        start = block * D
        if start < half:
            part = pl.ds(start, D)
            found = jnp.where(first, mine[part, :].astype(F32), other[part, :].astype(F32))
        else:
            part = pl.ds(start - half, D)
            found = jnp.where(first, other[part, :].astype(F32), mine[part, :].astype(F32))
        found = found * grad_scale
        target, column = (qkv_grad, block) if block < 9 else (proj_grad, block - 9)
        columns = slice(column * LANES, (column + 1) * LANES)
        target[:, columns] = found
        if block < 9:
            weighted = weighted + found * w_qkv[:, columns].astype(F32)
    gain_grad[...] = (jnp.sum(weighted.T, axis=0, keepdims=True) / gain[...]).reshape(D)


def window_pass(own, behind, sides, w_qkv, w_proj, norm_gain):
    def buffer(shape, kind):
        return pltpu.VMEM(shape, kind)

    return pl.pallas_call(
        window_kernel,
        out_shape=(jax.ShapeDtypeStruct((2, 2, PIECE, D), BF),) * 4
        + (jax.ShapeDtypeStruct((GRAD_ROWS, LANES), BF),),
        scratch_shapes=[
            buffer((ROWS, D), BF),
            buffer((ROWS, 3 * D), BF),
            buffer((ROWS, D), BF),
            buffer((D, ROWS), BF),
            buffer((D, ROWS), BF),
            buffer((D, ROWS), BF),
            buffer((D, ROWS), BF),
            buffer((ROWS, 3 * D), BF),
            buffer((ROWS, D), F32),
            buffer((ROWS, LANES), F32),
            buffer((ROWS, D), BF),
        ],
        compiler_params=pltpu.CompilerParams(vmem_limit_bytes=40 * 1024 * 1024),
        cost_estimate=pl.CostEstimate(
            flops=16_000_000_000, bytes_accessed=5_000_000, transcendentals=3_200_000
        ),
    )(own, behind, *sides, w_qkv, w_proj, norm_gain.reshape(1, D))


LATTICE = ("z_hi", "z_lo", "core", "y_hi", "y_lo", "x")
FIRST = ("z_hi", "z_lo", "core")
SECOND = ("y_hi",)
THIRD = ("y_lo", "x")
SIZES = {"z_hi": 4, "z_lo": 2, "core": 2, "y_hi": 4, "y_lo": 2, "x": 4}
NEAR = ("x", "y_lo", "z_lo")
GROUP = 16
FAR = 4


def near_sum(rows):
    halves = lax.all_to_all(rows.reshape(2, GRAD_ROWS // 2, LANES), "core", 0, 0)
    parts = total_of(halves, 1).reshape(GROUP, GRAD_ROWS // 2 // GROUP, LANES)
    parts = lax.all_to_all(parts, NEAR, 0, 0)
    return parts


def far_sum(parts, axis, after=()):
    return lax.all_to_all(total_of(parts, FAR, after), axis, 0, 0)


def spread_sum(parts, after):
    parts = lax.all_to_all(total_of(parts, GROUP, after), NEAR, 0, 0)
    mine = parts.reshape(GRAD_ROWS // 2, LANES)
    return mine, lax.ppermute(mine, "core", [(0, 1), (1, 0)])


def device_at(first, second, third):
    return ((first % 16) * 4 + second % 4) * 8 + third % 8


def route(kind, back):
    pairs = []
    for first in range(16):
        for second in range(4):
            for third in range(8):
                sign = 1 if first % 2 else -1
                if kind == 0:
                    move = (first - 1, second, third)
                else:
                    move = (first, second + sign * (kind >> 1), third + sign * (kind & 1))
                pair = (device_at(first, second, third), device_at(*move))
                pairs.append(pair[::-1] if back else pair)
    return pairs


def send(block, kind, back=False):
    return lax.ppermute(block, LATTICE, route(kind, back))


def local(tokens, frozen, cotangent, w_qkv, w_proj, norm_gain):
    core = lax.axis_index("core").reshape(1)
    token_rows, cot_rows = tokens.reshape(ROWS, D), cotangent.reshape(ROWS, D)
    own, ahead = pl.pallas_call(
        cut_kernel,
        out_shape=(jax.ShapeDtypeStruct((4, 2, PIECE, D), BF),) * 2,
        in_specs=[SCALAR] + [pl.BlockSpec(memory_space=pltpu.HBM)] * 3,
        scratch_shapes=[
            pltpu.VMEM((ROWS, D), BF),
            pltpu.VMEM((WIN, WIN, WIN), jnp.int32),
            pltpu.VMEM((ROWS, D), BF),
            pltpu.SemaphoreType.DMA((3,)),
        ],
        compiler_params=pltpu.CompilerParams(vmem_limit_bytes=56 * 1024 * 1024),
    )(core, token_rows, frozen, cot_rows)
    behind = send(ahead, 0)
    sides = [None] * 4
    for kind in (3, 2, 1):
        sides[kind] = send(jnp.stack([own[kind], behind[kind]]), kind)
    *backs, grads = window_pass(own, behind, sides[1:], w_qkv, w_proj, norm_gain)
    parts = near_sum(grads)
    for kind in (3, 2, 1):
        backs[kind] = send(backs[kind], kind, True)
    parts = far_sum(far_sum(parts, "y_hi"), "z_hi", backs[1:])
    ahead = send(jnp.stack([back[1] for back in backs]), 0, True)
    block_out, tokens_grad = pl.pallas_call(
        join_kernel,
        out_shape=(jax.ShapeDtypeStruct((ROWS, D), BF),) * 2,
        in_specs=[SCALAR] + [WHOLE] * 8,
        compiler_params=SMALL,
    )(core, token_rows, frozen, cot_rows, *backs, ahead)
    mine, other = spread_sum(parts, (ahead,))
    qkv_grad, proj_grad, gain_grad = pl.pallas_call(
        grads_kernel,
        out_shape=(
            jax.ShapeDtypeStruct((D, 3 * D), F32),
            jax.ShapeDtypeStruct((D, D), F32),
            jax.ShapeDtypeStruct((D,), F32),
        ),
        in_specs=[SCALAR] + [WHOLE] * 4,
        compiler_params=SMALL,
    )(core, mine, other, w_qkv, norm_gain.reshape(1, D))
    shape = (WIN, WIN, WIN, D)
    return block_out.reshape(shape), tokens_grad.reshape(shape), qkv_grad, proj_grad, gain_grad


def solution(mesh):
    inner = Mesh(mesh.devices.reshape([SIZES[axis] for axis in LATTICE]), LATTICE)
    lattice = P(FIRST, SECOND, THIRD)
    wide = P(FIRST, SECOND, THIRD, None)
    return jax.shard_map(
        local,
        mesh=inner,
        in_specs=(wide, lattice, wide, P(), P(), P()),
        out_specs=(wide, wide, P(), P(), P()),
        check_vma=False,
    )
```

```python
import functools

import jax
import jax.numpy as jnp
import numpy as np
from jax import lax
from jax.experimental import pallas as pl
from jax.experimental.pallas import tpu as pltpu
from jax.sharding import Mesh, PartitionSpec as P

D = 384
HEADS = 12
HDIM = 32
WIN = 8
HALF = WIN // 2
ROWS = WIN**3
PIECE = HALF**3
EPSILON = 1e-05
BF = jnp.bfloat16
F32 = jnp.float32
LANES = 128
PER = LANES // HDIM
CHUNK = 256
SCALE = HDIM ** (-0.5)
LOG2E = 1.4426950408889634
GRAD_ROWS = 12 * D


def dot(left, right):
    return jnp.dot(left, right, preferred_element_type=F32)


def dot_t(left, right):
    return lax.dot_general(left, right, (((1,), (1,)), ((), ())), preferred_element_type=F32)


def window_kernel(
    own, behind, side_3, side_2, side_1, w_qkv, w_proj, gain, back_0, back_1, back_2, back_3, grads,
    cot, qkv, d_mixed, keys_t, values_t, mixed_t, d_queries_t, d_qkv, unit, inv_std, normed,
):
    step = 2 * PIECE
    gain_row = gain[...]

    def arrived(group, array):
        if group == 0:
            return own[0, array], behind[0, array]
        side = (side_1, side_2, side_3)[group - 1]
        return side[0, array], side[1, array]

    for group in range(4):
        part = pl.ds(group * step, step)
        cot[part, :] = jnp.concatenate(arrived(group, 1), axis=0)
        rows = jnp.concatenate(arrived(group, 0), axis=0).astype(F32)
        centred = rows - jnp.mean(rows, axis=-1, keepdims=True)
        inverse = lax.rsqrt(jnp.mean(centred * centred, axis=-1, keepdims=True) + EPSILON)
        unit_rows = centred * inverse
        unit[part, :] = unit_rows
        inv_std[part, :] = jnp.broadcast_to(inverse, (step, LANES))
        normed[part, :] = (unit_rows * gain_row).astype(BF)
    qkv[...] = dot(normed[...], w_qkv[...]).astype(BF)
    d_mixed[...] = dot_t(cot[...], w_proj[...]).astype(BF)
    keys_t[...] = qkv[:, D : 2 * D].T
    values_t[...] = qkv[:, 2 * D :].T
    lane = lax.broadcasted_iota(jnp.int32, (1, LANES), 1)

    def first_products(head, start):
        block = slice(head // PER * LANES, (head // PER + 1) * LANES)
        mine = (lane // HDIM) == head % PER
        queries = pl.ds(start, CHUNK)
        zeros = jnp.zeros((CHUNK, LANES), BF)
        q_part = jnp.where(mine, qkv[queries, block], zeros)
        m_part = jnp.where(mine, d_mixed[queries, block], zeros)
        scores = dot_t(qkv[:, D + block.start : D + block.stop], q_part)
        d_probs = dot_t(qkv[:, 2 * D + block.start : 2 * D + block.stop], m_part)
        return q_part, m_part, scores, d_probs

    steps = [(head, start) for head in range(HEADS) for start in range(0, ROWS, CHUNK)]
    ready = first_products(*steps[0])
    for index, (head, start) in enumerate(steps):
        q_part, m_part, scores, d_probs = ready
        if index + 1 < len(steps):
            ready = first_products(*steps[index + 1])
        if head % PER == 0 and start == 0:
            d_keys = jnp.zeros((ROWS, LANES), F32)
            d_values = jnp.zeros((ROWS, LANES), F32)
        rows = pl.ds(head * HDIM, HDIM)
        top = jnp.max(scores, axis=0, keepdims=True)
        terms = jnp.exp2(scores * (SCALE * LOG2E) - top * (SCALE * LOG2E))
        inverse = 1.0 / jnp.sum(terms, axis=0, keepdims=True)
        probs_low = (terms * inverse).astype(BF)
        mixed_t[rows, pl.ds(start, CHUNK)] = dot(values_t[rows, :], probs_low).astype(BF)
        d_values = d_values + dot(probs_low, m_part)
        scaled = inverse * SCALE
        shift = jnp.sum(terms * d_probs, axis=0, keepdims=True) * (inverse * scaled)
        d_scores = (terms * (d_probs * scaled - shift)).astype(BF)
        d_queries_t[rows, pl.ds(start, CHUNK)] = dot(keys_t[rows, :], d_scores).astype(BF)
        d_keys = d_keys + dot(d_scores, q_part)
        if head % PER == PER - 1 and start + CHUNK == ROWS:
            block = head // PER * LANES
            d_qkv[:, D + block : D + block + LANES] = d_keys.astype(BF)
            d_qkv[:, 2 * D + block : 2 * D + block + LANES] = d_values.astype(BF)

    d_qkv[:, pl.ds(0, D)] = d_queries_t[...].T
    branch = dot(mixed_t[...].T, w_proj[...]).astype(BF)
    backs = (back_0, back_1, back_2, back_3)
    for group in range(4):
        for place in range(2):
            start = (2 * group + place) * PIECE
            backs[group][place, 0] = branch[start : start + PIECE]
    normed_t = normed[...].T
    for block in range(9):
        term = dot(normed_t, d_qkv[:, block * LANES : (block + 1) * LANES])
        grads[pl.ds(block * D, D), :] = term.astype(BF)
    for block in range(3):
        term = dot(mixed_t[...], cot[:, block * LANES : (block + 1) * LANES])
        grads[pl.ds((9 + block) * D, D), :] = term.astype(BF)
    for group in range(4):
        part = pl.ds(group * step, step)
        d_normed = dot_t(d_qkv[part, :], w_qkv[...])
        unit_rows = unit[part, :]
        scaled = d_normed * gain_row
        mean_1 = jnp.mean(scaled, axis=-1, keepdims=True)
        mean_2 = jnp.mean(scaled * unit_rows, axis=-1, keepdims=True)
        d_rows = (inv_std[part, 0:1] * (scaled - mean_1 - unit_rows * mean_2)).astype(BF)
        backs[group][0, 1] = d_rows[:PIECE]
        backs[group][1, 1] = d_rows[PIECE:]


def order(odd, upper, inverse):
    flip = odd if upper == 0 else 1 - odd
    shape = (WIN * WIN, WIN * WIN)
    row = lax.broadcasted_iota(jnp.int32, shape, 1 if inverse else 0)
    token = lax.broadcasted_iota(jnp.int32, shape, 0 if inverse else 1)
    along_y = ((row >> 5) ^ flip) * HALF + ((row >> 2) & 3)
    along_z = (((row >> 4) & 1) ^ flip) * HALF + (row & 3)
    return token == along_y * WIN + along_z


def ones_where(chosen):
    return jnp.where(chosen, 1.0, 0.0)


def keep_rows(frozen):
    table = ones_where(frozen[...].reshape(WIN * WIN, WIN) == 1).astype(BF)
    column = lax.broadcasted_iota(jnp.int32, (WIN, WIN * WIN), 1)
    row = lax.broadcasted_iota(jnp.int32, (WIN, WIN * WIN), 0)
    spread = dot(table, ones_where((column & 7) == row).astype(BF))
    chosen = ones_where((column >> 3) == row)
    return [
        jnp.sum(spread[plane * WIN : (plane + 1) * WIN] * chosen, axis=0, keepdims=True)
        for plane in range(WIN)
    ]


def cut_kernel(odd, tokens_in, frozen_in, cotangent_in, own, ahead, tokens, frozen, cotangent, arrivals):
    moves = [
        pltpu.make_async_copy(source, target, arrivals.at[index])
        for index, (source, target) in enumerate(
            ((frozen_in, frozen), (tokens_in, tokens), (cotangent_in, cotangent))
        )
    ]
    for move in moves:
        move.start()
    for move in moves:
        move.wait()
    keeps = keep_rows(frozen)
    for upper, target in ((0, ahead), (1, own)):
        matrix = ones_where(order(odd[0], upper, False))
        for plane in range(HALF):
            index = upper * HALF + plane
            part = pl.ds(index * WIN * WIN, WIN * WIN)
            kept = dot((matrix * keeps[index]).astype(BF), tokens[part, :]).astype(BF)
            cot = dot(matrix.astype(BF), cotangent[part, :]).astype(BF)
            for group in range(4):
                rows = slice(group * 16, group * 16 + 16)
                target[group, 0, pl.ds(plane * 16, 16), :] = kept[rows]
                target[group, 1, pl.ds(plane * 16, 16), :] = cot[rows]


def join_kernel(odd, tokens, frozen, cotangent, home_0, home_1, home_2, home_3, ahead, block_out, tokens_grad):
    homes = (home_0, home_1, home_2, home_3)
    keeps = keep_rows(frozen)
    shape = (WIN * WIN, WIN * WIN)
    diagonal = ones_where(lax.broadcasted_iota(jnp.int32, shape, 0) == lax.broadcasted_iota(jnp.int32, shape, 1))
    for upper in range(2):
        matrix = ones_where(order(odd[0], upper, True)).astype(BF)
        for plane in range(HALF):
            index = upper * HALF + plane
            part = pl.ds(index * WIN * WIN, WIN * WIN)
            keep = (diagonal * keeps[index]).astype(BF)
            rows = pl.ds(plane * 16, 16)

            def pieces(array):
                if upper:
                    found = [homes[group][0, array, rows, :] for group in range(4)]
                else:
                    found = [ahead[group, array, rows, :] for group in range(4)]
                return dot(matrix, jnp.concatenate(found, axis=0))

            block_out[part, :] = (dot(keep, tokens[part, :]) + pieces(0)).astype(BF)
            grown = (cotangent[part, :].astype(F32) + pieces(1)).astype(BF)
            tokens_grad[part, :] = dot(keep, grown).astype(BF)


SCALAR = pl.BlockSpec(memory_space=pltpu.SMEM)
WHOLE = pl.BlockSpec(memory_space=pltpu.VMEM)
SMALL = pltpu.CompilerParams(vmem_limit_bytes=12 * 1024 * 1024)


def total_kernel(parts, *rest, copies, out_at):
    out = rest[out_at]
    total = parts[0].astype(F32)
    for index in range(1, parts.shape[0]):
        total = total + parts[index].astype(F32)
    total = total.astype(BF)
    for index in range(copies):
        out[index] = total


def total_of(parts, copies, after=(), through=()):
    anywhere = pl.BlockSpec(memory_space=pl.ANY)
    total, *passed = pl.pallas_call(
        functools.partial(total_kernel, copies=copies, out_at=len(after) + len(through)),
        out_shape=[jax.ShapeDtypeStruct((copies,) + parts.shape[1:], BF)]
        + [jax.ShapeDtypeStruct(array.shape, array.dtype) for array in through],
        in_specs=[WHOLE] + [anywhere] * (len(after) + len(through)),
        out_specs=[WHOLE] + [anywhere] * len(through),
        input_output_aliases={1 + len(after) + at: 1 + at for at in range(len(through))},
        compiler_params=SMALL,
    )(parts, *after, *through)
    return (total, *passed) if through else total


def grads_kernel(core, mine, other, w_qkv, gain, qkv_grad, proj_grad, gain_grad):
    grad_scale = (ROWS * 512) ** (-0.5)
    half = GRAD_ROWS // 2
    first = core[0] == 0
    weighted = jnp.zeros((D, LANES), F32)
    for block in range(12):
        start = block * D
        if start < half:
            part = pl.ds(start, D)
            found = jnp.where(first, mine[part, :].astype(F32), other[part, :].astype(F32))
        else:
            part = pl.ds(start - half, D)
            found = jnp.where(first, other[part, :].astype(F32), mine[part, :].astype(F32))
        found = found * grad_scale
        target, column = (qkv_grad, block) if block < 9 else (proj_grad, block - 9)
        columns = slice(column * LANES, (column + 1) * LANES)
        target[:, columns] = found
        if block < 9:
            weighted = weighted + found * w_qkv[:, columns].astype(F32)
    gain_grad[...] = (jnp.sum(weighted.T, axis=0, keepdims=True) / gain[...]).reshape(D)


def window_pass(own, behind, sides, w_qkv, w_proj, norm_gain):
    def buffer(shape, kind):
        return pltpu.VMEM(shape, kind)

    return pl.pallas_call(
        window_kernel,
        out_shape=(jax.ShapeDtypeStruct((2, 2, PIECE, D), BF),) * 4
        + (jax.ShapeDtypeStruct((GRAD_ROWS, LANES), BF),),
        scratch_shapes=[
            buffer((ROWS, D), BF),
            buffer((ROWS, 3 * D), BF),
            buffer((ROWS, D), BF),
            buffer((D, ROWS), BF),
            buffer((D, ROWS), BF),
            buffer((D, ROWS), BF),
            buffer((D, ROWS), BF),
            buffer((ROWS, 3 * D), BF),
            buffer((ROWS, D), F32),
            buffer((ROWS, LANES), F32),
            buffer((ROWS, D), BF),
        ],
        compiler_params=pltpu.CompilerParams(vmem_limit_bytes=40 * 1024 * 1024),
        cost_estimate=pl.CostEstimate(
            flops=16_000_000_000, bytes_accessed=5_000_000, transcendentals=3_200_000
        ),
    )(own, behind, *sides[::-1], w_qkv, w_proj, norm_gain.reshape(1, D))


LATTICE = ("z_hi", "z_lo", "core", "y_hi", "y_lo", "x")
FIRST = ("z_hi", "z_lo", "core")
SECOND = ("y_hi",)
THIRD = ("y_lo", "x")
SIZES = {"z_hi": 4, "z_lo": 2, "core": 2, "y_hi": 4, "y_lo": 2, "x": 4}
NEAR = ("x", "y_lo", "z_lo")
GROUP = 16
FAR = 4


def near_sum(rows):
    halves = lax.all_to_all(rows.reshape(2, GRAD_ROWS // 2, LANES), "core", 0, 0)
    parts = total_of(halves, 1).reshape(GROUP, GRAD_ROWS // 2 // GROUP, LANES)
    parts = lax.all_to_all(parts, NEAR, 0, 0)
    return parts


def spread_sum(parts, after):
    parts = lax.all_to_all(total_of(parts, GROUP, after), NEAR, 0, 0)
    mine = parts.reshape(GRAD_ROWS // 2, LANES)
    return mine, lax.ppermute(mine, "core", [(0, 1), (1, 0)])


def device_at(first, second, third):
    return ((first % 16) * 4 + second % 4) * 8 + third % 8


def route(kind, back):
    pairs = []
    for first in range(16):
        for second in range(4):
            for third in range(8):
                sign = 1 if first % 2 else -1
                if kind == 0:
                    move = (first - 1, second, third)
                else:
                    move = (first, second + sign * (kind >> 1), third + sign * (kind & 1))
                pair = (device_at(first, second, third), device_at(*move))
                pairs.append(pair[::-1] if back else pair)
    return pairs


def send(block, kind, back=False):
    return lax.ppermute(block, LATTICE, route(kind, back))


def local(tokens, frozen, cotangent, w_qkv, w_proj, norm_gain):
    core = lax.axis_index("core").reshape(1)
    token_rows, cot_rows = tokens.reshape(ROWS, D), cotangent.reshape(ROWS, D)
    own, ahead = pl.pallas_call(
        cut_kernel,
        out_shape=(jax.ShapeDtypeStruct((4, 2, PIECE, D), BF),) * 2,
        in_specs=[SCALAR] + [pl.BlockSpec(memory_space=pltpu.HBM)] * 3,
        scratch_shapes=[
            pltpu.VMEM((ROWS, D), BF),
            pltpu.VMEM((WIN, WIN, WIN), jnp.int32),
            pltpu.VMEM((ROWS, D), BF),
            pltpu.SemaphoreType.DMA((3,)),
        ],
        compiler_params=pltpu.CompilerParams(vmem_limit_bytes=56 * 1024 * 1024),
    )(core, token_rows, frozen, cot_rows)
    behind = send(ahead, 0)
    sides = [None] * 4
    for kind in (1, 2, 3):
        sides[kind] = send(jnp.stack([own[kind], behind[kind]]), kind)
    *backs, grads = window_pass(own, behind, sides[1:], w_qkv, w_proj, norm_gain)
    parts = near_sum(grads)
    parts, *backs[1:] = total_of(parts, FAR, through=backs[1:])
    for kind in (1, 2, 3):
        backs[kind] = send(backs[kind], kind, True)
    ahead = send(jnp.stack([back[1] for back in backs]), 0, True)
    parts = total_of(lax.all_to_all(parts, "y_hi", 0, 0), FAR)
    parts = lax.all_to_all(parts, "z_hi", 0, 0)
    block_out, tokens_grad = pl.pallas_call(
        join_kernel,
        out_shape=(jax.ShapeDtypeStruct((ROWS, D), BF),) * 2,
        in_specs=[SCALAR] + [WHOLE] * 8,
        compiler_params=SMALL,
    )(core, token_rows, frozen, cot_rows, *backs, ahead)
    mine, other = spread_sum(parts, (ahead,))
    qkv_grad, proj_grad, gain_grad = pl.pallas_call(
        grads_kernel,
        out_shape=(
            jax.ShapeDtypeStruct((D, 3 * D), F32),
            jax.ShapeDtypeStruct((D, D), F32),
            jax.ShapeDtypeStruct((D,), F32),
        ),
        in_specs=[SCALAR] + [WHOLE] * 4,
        compiler_params=SMALL,
    )(core, mine, other, w_qkv, norm_gain.reshape(1, D))
    shape = (WIN, WIN, WIN, D)
    return block_out.reshape(shape), tokens_grad.reshape(shape), qkv_grad, proj_grad, gain_grad


def solution(mesh):
    inner = Mesh(mesh.devices.reshape([SIZES[axis] for axis in LATTICE]), LATTICE)
    lattice = P(FIRST, SECOND, THIRD)
    wide = P(FIRST, SECOND, THIRD, None)
    return jax.shard_map(
        local,
        mesh=inner,
        in_specs=(wide, lattice, wide, P(), P(), P()),
        out_specs=(wide, wide, P(), P(), P()),
        check_vma=False,
    )
```

```python
import functools

import jax
import jax.numpy as jnp
import numpy as np
from jax import lax
from jax.experimental import pallas as pl
from jax.experimental.pallas import tpu as pltpu
from jax.sharding import Mesh, PartitionSpec as P

D = 384
HEADS = 12
HDIM = 32
WIN = 8
HALF = WIN // 2
ROWS = WIN**3
PIECE = HALF**3
EPSILON = 1e-05
BF = jnp.bfloat16
F32 = jnp.float32
LANES = 128
PER = LANES // HDIM
CHUNK = 256
SCALE = HDIM ** (-0.5)
LOG2E = 1.4426950408889634
GRAD_ROWS = 12 * D


def dot(left, right):
    return jnp.dot(left, right, preferred_element_type=F32)


def dot_t(left, right):
    return lax.dot_general(left, right, (((1,), (1,)), ((), ())), preferred_element_type=F32)


def window_kernel(
    own, behind, side_3, side_2, side_1, w_qkv, w_proj, gain, grads, mixed_t, d_qkv, unit, inv_std,
    cot, qkv, d_mixed, keys_t, values_t, d_queries_t, normed,
):
    step = 2 * PIECE
    gain_row = gain[...]

    def arrived(group, array):
        if group == 0:
            return own[0, array], behind[0, array]
        side = (side_1, side_2, side_3)[group - 1]
        return side[0, array], side[1, array]

    for group in range(4):
        part = pl.ds(group * step, step)
        cot[part, :] = jnp.concatenate(arrived(group, 1), axis=0)
        rows = jnp.concatenate(arrived(group, 0), axis=0).astype(F32)
        centred = rows - jnp.mean(rows, axis=-1, keepdims=True)
        inverse = lax.rsqrt(jnp.mean(centred * centred, axis=-1, keepdims=True) + EPSILON)
        unit_rows = centred * inverse
        unit[part, :] = unit_rows
        inv_std[part, :] = jnp.broadcast_to(inverse, (step, LANES))
        normed[part, :] = (unit_rows * gain_row).astype(BF)
    qkv[...] = dot(normed[...], w_qkv[...]).astype(BF)
    d_mixed[...] = dot_t(cot[...], w_proj[...]).astype(BF)
    keys_t[...] = qkv[:, D : 2 * D].T
    values_t[...] = qkv[:, 2 * D :].T
    lane = lax.broadcasted_iota(jnp.int32, (1, LANES), 1)

    def first_products(head, start):
        block = slice(head // PER * LANES, (head // PER + 1) * LANES)
        mine = (lane // HDIM) == head % PER
        queries = pl.ds(start, CHUNK)
        zeros = jnp.zeros((CHUNK, LANES), BF)
        q_part = jnp.where(mine, qkv[queries, block], zeros)
        m_part = jnp.where(mine, d_mixed[queries, block], zeros)
        scores = dot_t(qkv[:, D + block.start : D + block.stop], q_part)
        d_probs = dot_t(qkv[:, 2 * D + block.start : 2 * D + block.stop], m_part)
        return q_part, m_part, scores, d_probs

    steps = [(head, start) for head in range(HEADS) for start in range(0, ROWS, CHUNK)]
    ready = first_products(*steps[0])
    for index, (head, start) in enumerate(steps):
        q_part, m_part, scores, d_probs = ready
        if index + 1 < len(steps):
            ready = first_products(*steps[index + 1])
        if head % PER == 0 and start == 0:
            d_keys = jnp.zeros((ROWS, LANES), F32)
            d_values = jnp.zeros((ROWS, LANES), F32)
        rows = pl.ds(head * HDIM, HDIM)
        top = jnp.max(scores, axis=0, keepdims=True)
        terms = jnp.exp2(scores * (SCALE * LOG2E) - top * (SCALE * LOG2E))
        inverse = 1.0 / jnp.sum(terms, axis=0, keepdims=True)
        probs_low = (terms * inverse).astype(BF)
        mixed_t[rows, pl.ds(start, CHUNK)] = dot(values_t[rows, :], probs_low).astype(BF)
        d_values = d_values + dot(probs_low, m_part)
        scaled = inverse * SCALE
        shift = jnp.sum(terms * d_probs, axis=0, keepdims=True) * (inverse * scaled)
        d_scores = (terms * (d_probs * scaled - shift)).astype(BF)
        d_queries_t[rows, pl.ds(start, CHUNK)] = dot(keys_t[rows, :], d_scores).astype(BF)
        d_keys = d_keys + dot(d_scores, q_part)
        if head % PER == PER - 1 and start + CHUNK == ROWS:
            block = head // PER * LANES
            d_qkv[:, D + block : D + block + LANES] = d_keys.astype(BF)
            d_qkv[:, 2 * D + block : 2 * D + block + LANES] = d_values.astype(BF)

    d_qkv[:, pl.ds(0, D)] = d_queries_t[...].T
    normed_t = normed[...].T
    for block in range(9):
        term = dot(normed_t, d_qkv[:, block * LANES : (block + 1) * LANES])
        grads[pl.ds(block * D, D), :] = term.astype(BF)
    for block in range(3):
        term = dot(mixed_t[...], cot[:, block * LANES : (block + 1) * LANES])
        grads[pl.ds((9 + block) * D, D), :] = term.astype(BF)


def rows_kernel(mixed_t, d_qkv, unit, inv_std, w_qkv, w_proj, gain, back_0, back_1, back_y):
    step = 2 * PIECE
    backs = (back_0, back_1, back_y.at[0], back_y.at[1])
    branch = dot(mixed_t[...].T, w_proj[...]).astype(BF)
    for group in range(4):
        part = pl.ds(group * step, step)
        d_normed = dot_t(d_qkv[part, :], w_qkv[...])
        unit_rows = unit[part, :]
        scaled = d_normed * gain[...]
        mean_1 = jnp.mean(scaled, axis=-1, keepdims=True)
        mean_2 = jnp.mean(scaled * unit_rows, axis=-1, keepdims=True)
        d_rows = (inv_std[part, 0:1] * (scaled - mean_1 - unit_rows * mean_2)).astype(BF)
        for place in range(2):
            start = (2 * group + place) * PIECE
            backs[group][place, 0] = branch[start : start + PIECE]
            backs[group][place, 1] = d_rows[place * PIECE : (place + 1) * PIECE]


def order(odd, upper, inverse):
    flip = odd if upper == 0 else 1 - odd
    shape = (WIN * WIN, WIN * WIN)
    row = lax.broadcasted_iota(jnp.int32, shape, 1 if inverse else 0)
    token = lax.broadcasted_iota(jnp.int32, shape, 0 if inverse else 1)
    along_y = ((row >> 5) ^ flip) * HALF + ((row >> 2) & 3)
    along_z = (((row >> 4) & 1) ^ flip) * HALF + (row & 3)
    return token == along_y * WIN + along_z


def ones_where(chosen):
    return jnp.where(chosen, 1.0, 0.0)


def keep_rows(frozen):
    table = ones_where(frozen[...].reshape(WIN * WIN, WIN) == 1).astype(BF)
    column = lax.broadcasted_iota(jnp.int32, (WIN, WIN * WIN), 1)
    row = lax.broadcasted_iota(jnp.int32, (WIN, WIN * WIN), 0)
    spread = dot(table, ones_where((column & 7) == row).astype(BF))
    chosen = ones_where((column >> 3) == row)
    return [
        jnp.sum(spread[plane * WIN : (plane + 1) * WIN] * chosen, axis=0, keepdims=True)
        for plane in range(WIN)
    ]


def cut_kernel(odd, tokens_in, frozen_in, cotangent_in, own, ahead, tokens, frozen, cotangent, arrivals):
    moves = [
        pltpu.make_async_copy(source, target, arrivals.at[index])
        for index, (source, target) in enumerate(
            ((frozen_in, frozen), (tokens_in, tokens), (cotangent_in, cotangent))
        )
    ]
    for move in moves:
        move.start()
    for move in moves:
        move.wait()
    keeps = keep_rows(frozen)
    for upper, target in ((0, ahead), (1, own)):
        matrix = ones_where(order(odd[0], upper, False))
        for plane in range(HALF):
            index = upper * HALF + plane
            part = pl.ds(index * WIN * WIN, WIN * WIN)
            kept = dot((matrix * keeps[index]).astype(BF), tokens[part, :]).astype(BF)
            cot = dot(matrix.astype(BF), cotangent[part, :]).astype(BF)
            for group in range(4):
                rows = slice(group * 16, group * 16 + 16)
                target[group, 0, pl.ds(plane * 16, 16), :] = kept[rows]
                target[group, 1, pl.ds(plane * 16, 16), :] = cot[rows]


def join_kernel(odd, tokens, frozen, cotangent, home_0, home_x, home_2, ahead, block_out, tokens_grad, token):
    homes = (home_0, home_x.at[0], home_2.at[0], home_x.at[1])
    token[...] = jnp.zeros_like(token)
    keeps = keep_rows(frozen)
    shape = (WIN * WIN, WIN * WIN)
    diagonal = ones_where(lax.broadcasted_iota(jnp.int32, shape, 0) == lax.broadcasted_iota(jnp.int32, shape, 1))
    for upper in range(2):
        matrix = ones_where(order(odd[0], upper, True)).astype(BF)
        for plane in range(HALF):
            index = upper * HALF + plane
            part = pl.ds(index * WIN * WIN, WIN * WIN)
            keep = (diagonal * keeps[index]).astype(BF)
            rows = pl.ds(plane * 16, 16)

            def pieces(array):
                if upper:
                    found = [homes[group][0, array, rows, :] for group in range(4)]
                else:
                    found = [ahead[group, array, rows, :] for group in range(4)]
                return dot(matrix, jnp.concatenate(found, axis=0))

            block_out[part, :] = (dot(keep, tokens[part, :]) + pieces(0)).astype(BF)
            grown = (cotangent[part, :].astype(F32) + pieces(1)).astype(BF)
            tokens_grad[part, :] = dot(keep, grown).astype(BF)


SCALAR = pl.BlockSpec(memory_space=pltpu.SMEM)
WHOLE = pl.BlockSpec(memory_space=pltpu.VMEM)
SMALL = pltpu.CompilerParams(vmem_limit_bytes=12 * 1024 * 1024)


def total_kernel(parts, *rest, copies, out_at):
    out = rest[out_at]
    total = parts[0].astype(F32)
    for index in range(1, parts.shape[0]):
        total = total + parts[index].astype(F32)
    total = total.astype(BF)
    for index in range(copies):
        out[index] = total


def total_of(parts, copies, after=(), through=()):
    anywhere = pl.BlockSpec(memory_space=pl.ANY)
    total, *passed = pl.pallas_call(
        functools.partial(total_kernel, copies=copies, out_at=len(after) + len(through)),
        out_shape=[jax.ShapeDtypeStruct((copies,) + parts.shape[1:], BF)]
        + [jax.ShapeDtypeStruct(array.shape, array.dtype) for array in through],
        in_specs=[WHOLE] + [anywhere] * (len(after) + len(through)),
        out_specs=[WHOLE] + [anywhere] * len(through),
        input_output_aliases={1 + len(after) + at: 1 + at for at in range(len(through))},
        compiler_params=SMALL,
    )(parts, *after, *through)
    return (total, *passed) if through else total


def hold(array, until):
    anywhere = pl.BlockSpec(memory_space=pl.ANY)
    return pl.pallas_call(
        lambda *refs: None,
        out_shape=jax.ShapeDtypeStruct(array.shape, array.dtype),
        in_specs=[anywhere] * 2,
        out_specs=anywhere,
        input_output_aliases={0: 0},
        compiler_params=SMALL,
    )(array, until)


def grads_kernel(core, mine, other, w_qkv, gain, qkv_grad, proj_grad, gain_grad):
    grad_scale = (ROWS * 512) ** (-0.5)
    half = GRAD_ROWS // 2
    first = core[0] == 0
    weighted = jnp.zeros((D, LANES), F32)
    for block in range(12):
        start = block * D
        if start < half:
            part = pl.ds(start, D)
            found = jnp.where(first, mine[part, :].astype(F32), other[part, :].astype(F32))
        else:
            part = pl.ds(start - half, D)
            found = jnp.where(first, other[part, :].astype(F32), mine[part, :].astype(F32))
        found = found * grad_scale
        target, column = (qkv_grad, block) if block < 9 else (proj_grad, block - 9)
        columns = slice(column * LANES, (column + 1) * LANES)
        target[:, columns] = found
        if block < 9:
            weighted = weighted + found * w_qkv[:, columns].astype(F32)
    gain_grad[...] = (jnp.sum(weighted.T, axis=0, keepdims=True) / gain[...]).reshape(D)


def window_pass(own, behind, sides, w_qkv, w_proj, norm_gain):
    def buffer(shape, kind):
        return pltpu.VMEM(shape, kind)

    gain = norm_gain.reshape(1, D)
    grads, *kept = pl.pallas_call(
        window_kernel,
        out_shape=(
            jax.ShapeDtypeStruct((GRAD_ROWS, LANES), BF),
            jax.ShapeDtypeStruct((D, ROWS), BF),
            jax.ShapeDtypeStruct((ROWS, 3 * D), BF),
            jax.ShapeDtypeStruct((ROWS, D), F32),
            jax.ShapeDtypeStruct((ROWS, LANES), F32),
        ),
        scratch_shapes=[
            buffer((ROWS, D), BF),
            buffer((ROWS, 3 * D), BF),
            buffer((ROWS, D), BF),
            buffer((D, ROWS), BF),
            buffer((D, ROWS), BF),
            buffer((D, ROWS), BF),
            buffer((ROWS, D), BF),
        ],
        compiler_params=pltpu.CompilerParams(vmem_limit_bytes=32 * 1024 * 1024),
        cost_estimate=pl.CostEstimate(
            flops=12_000_000_000, bytes_accessed=5_000_000, transcendentals=3_200_000
        ),
    )(own, behind, *sides[::-1], w_qkv, w_proj, gain)
    backs = pl.pallas_call(
        rows_kernel,
        out_shape=(jax.ShapeDtypeStruct((2, 2, PIECE, D), BF),) * 2
        + (jax.ShapeDtypeStruct((2, 2, 2, PIECE, D), BF),),
        compiler_params=pltpu.CompilerParams(vmem_limit_bytes=24 * 1024 * 1024),
        cost_estimate=pl.CostEstimate(flops=2_000_000_000, bytes_accessed=4_000_000, transcendentals=0),
    )(*kept, w_qkv, w_proj, gain)
    return *backs, grads


LATTICE = ("z_hi", "z_lo", "core", "y_hi", "y_lo", "x")
FIRST = ("z_hi", "z_lo", "core")
SECOND = ("y_hi",)
THIRD = ("y_lo", "x")
SIZES = {"z_hi": 4, "z_lo": 2, "core": 2, "y_hi": 4, "y_lo": 2, "x": 4}
NEAR = ("x", "y_lo", "z_lo")
GROUP = 16
FAR = 4


def near_sum(rows):
    halves = lax.all_to_all(rows.reshape(2, GRAD_ROWS // 2, LANES), "core", 0, 0)
    parts = total_of(halves, 1).reshape(GROUP, GRAD_ROWS // 2 // GROUP, LANES)
    parts = lax.all_to_all(parts, NEAR, 0, 0)
    return parts


def device_at(first, second, third):
    return ((first % 16) * 4 + second % 4) * 8 + third % 8


def route(kind, back):
    pairs = []
    for first in range(16):
        for second in range(4):
            for third in range(8):
                sign = 1 if first % 2 else -1
                if kind == 0:
                    move = (first - 1, second, third)
                else:
                    move = (first, second + sign * (kind >> 1), third + sign * (kind & 1))
                pair = (device_at(first, second, third), device_at(*move))
                pairs.append(pair[::-1] if back else pair)
    return pairs


def send(block, kind, back=False):
    return lax.ppermute(block, LATTICE, route(kind, back))


def local(tokens, frozen, cotangent, w_qkv, w_proj, norm_gain):
    core = lax.axis_index("core").reshape(1)
    token_rows, cot_rows = tokens.reshape(ROWS, D), cotangent.reshape(ROWS, D)
    own, ahead = pl.pallas_call(
        cut_kernel,
        out_shape=(jax.ShapeDtypeStruct((4, 2, PIECE, D), BF),) * 2,
        in_specs=[SCALAR] + [pl.BlockSpec(memory_space=pltpu.HBM)] * 3,
        scratch_shapes=[
            pltpu.VMEM((ROWS, D), BF),
            pltpu.VMEM((WIN, WIN, WIN), jnp.int32),
            pltpu.VMEM((ROWS, D), BF),
            pltpu.SemaphoreType.DMA((3,)),
        ],
        compiler_params=pltpu.CompilerParams(vmem_limit_bytes=56 * 1024 * 1024),
    )(core, token_rows, frozen, cot_rows)
    behind = send(ahead, 0)
    sides = [None] * 4
    for kind in (1, 2, 3):
        sides[kind] = send(jnp.stack([own[kind], behind[kind]]), kind)
    back_0, back_1, back_y, grads = window_pass(own, behind, sides[1:], w_qkv, w_proj, norm_gain)
    parts = near_sum(grads)
    parts, back_y = total_of(parts, FAR, through=(back_y,))
    home_y = send(back_y, 2, True)
    parts = total_of(lax.all_to_all(parts, "y_hi", 0, 0), FAR)
    home_x = send(jnp.stack([back_1, home_y[1]]), 1, True)
    parts = total_of(lax.all_to_all(parts, "z_hi", 0, 0), GROUP, after=(home_x,))
    mine = lax.all_to_all(parts, NEAR, 0, 0).reshape(GRAD_ROWS // 2, LANES)
    ahead = send(jnp.stack([back_0[1], home_x[0, 1], home_y[0, 1], home_x[1, 1]]), 0, True)
    block_out, tokens_grad, token = pl.pallas_call(
        join_kernel,
        out_shape=(jax.ShapeDtypeStruct((ROWS, D), BF),) * 2 + (jax.ShapeDtypeStruct((8, LANES), F32),),
        in_specs=[SCALAR] + [WHOLE] * 7,
        compiler_params=SMALL,
        cost_estimate=pl.CostEstimate(flops=300_000_000, bytes_accessed=4_000_000, transcendentals=0),
    )(core, token_rows, frozen, cot_rows, back_0, home_x, home_y, ahead)
    mine = hold(mine, token)
    other = lax.ppermute(mine, "core", [(0, 1), (1, 0)])
    qkv_grad, proj_grad, gain_grad = pl.pallas_call(
        grads_kernel,
        out_shape=(
            jax.ShapeDtypeStruct((D, 3 * D), F32),
            jax.ShapeDtypeStruct((D, D), F32),
            jax.ShapeDtypeStruct((D,), F32),
        ),
        in_specs=[SCALAR] + [WHOLE] * 4,
        compiler_params=SMALL,
    )(core, mine, other, w_qkv, norm_gain.reshape(1, D))
    shape = (WIN, WIN, WIN, D)
    return block_out.reshape(shape), tokens_grad.reshape(shape), qkv_grad, proj_grad, gain_grad


def solution(mesh):
    inner = Mesh(mesh.devices.reshape([SIZES[axis] for axis in LATTICE]), LATTICE)
    lattice = P(FIRST, SECOND, THIRD)
    wide = P(FIRST, SECOND, THIRD, None)
    return jax.shard_map(
        local,
        mesh=inner,
        in_specs=(wide, lattice, wide, P(), P(), P()),
        out_specs=(wide, wide, P(), P(), P()),
        check_vma=False,
    )
```

```python
import functools

import jax
import jax.numpy as jnp
import numpy as np
from jax import lax
from jax.experimental import pallas as pl
from jax.experimental.pallas import tpu as pltpu
from jax.sharding import Mesh, PartitionSpec as P

D = 384
HEADS = 12
HDIM = 32
WIN = 8
HALF = WIN // 2
ROWS = WIN**3
PIECE = HALF**3
EPSILON = 1e-05
BF = jnp.bfloat16
F32 = jnp.float32
LANES = 128
PER = LANES // HDIM
CHUNK = 256
SCALE = HDIM ** (-0.5)
LOG2E = 1.4426950408889634
GRAD_ROWS = 12 * D


def dot(left, right):
    return jnp.dot(left, right, preferred_element_type=F32)


def dot_t(left, right):
    return lax.dot_general(left, right, (((1,), (1,)), ((), ())), preferred_element_type=F32)


def window_kernel(
    own, behind, side_3, side_2, side_1, w_qkv, w_proj, gain, back_0, back_2, back_x, grads,
    cot, qkv, d_mixed, keys_t, values_t, mixed_t, d_queries_t, d_qkv, unit, inv_std, normed,
):
    step = 2 * PIECE
    gain_row = gain[...]

    def arrived(group, array):
        if group == 0:
            return own[0, array], behind[0, array]
        side = (side_1, side_2, side_3)[group - 1]
        return side[0, array], side[1, array]

    for group in range(4):
        part = pl.ds(group * step, step)
        cot[part, :] = jnp.concatenate(arrived(group, 1), axis=0)
        rows = jnp.concatenate(arrived(group, 0), axis=0).astype(F32)
        centred = rows - jnp.mean(rows, axis=-1, keepdims=True)
        inverse = lax.rsqrt(jnp.mean(centred * centred, axis=-1, keepdims=True) + EPSILON)
        unit_rows = centred * inverse
        unit[part, :] = unit_rows
        inv_std[part, :] = jnp.broadcast_to(inverse, (step, LANES))
        normed[part, :] = (unit_rows * gain_row).astype(BF)
    qkv[...] = dot(normed[...], w_qkv[...]).astype(BF)
    d_mixed[...] = dot_t(cot[...], w_proj[...]).astype(BF)
    keys_t[...] = qkv[:, D : 2 * D].T
    values_t[...] = qkv[:, 2 * D :].T
    lane = lax.broadcasted_iota(jnp.int32, (1, LANES), 1)

    def first_products(head, start):
        block = slice(head // PER * LANES, (head // PER + 1) * LANES)
        mine = (lane // HDIM) == head % PER
        queries = pl.ds(start, CHUNK)
        zeros = jnp.zeros((CHUNK, LANES), BF)
        q_part = jnp.where(mine, qkv[queries, block], zeros)
        m_part = jnp.where(mine, d_mixed[queries, block], zeros)
        scores = dot_t(qkv[:, D + block.start : D + block.stop], q_part)
        d_probs = dot_t(qkv[:, 2 * D + block.start : 2 * D + block.stop], m_part)
        return q_part, m_part, scores, d_probs

    steps = [(head, start) for head in range(HEADS) for start in range(0, ROWS, CHUNK)]
    ready = first_products(*steps[0])
    for index, (head, start) in enumerate(steps):
        q_part, m_part, scores, d_probs = ready
        if index + 1 < len(steps):
            ready = first_products(*steps[index + 1])
        if head % PER == 0 and start == 0:
            d_keys = jnp.zeros((ROWS, LANES), F32)
            d_values = jnp.zeros((ROWS, LANES), F32)
        rows = pl.ds(head * HDIM, HDIM)
        top = jnp.max(scores, axis=0, keepdims=True)
        terms = jnp.exp2(scores * (SCALE * LOG2E) - top * (SCALE * LOG2E))
        inverse = 1.0 / jnp.sum(terms, axis=0, keepdims=True)
        probs_low = (terms * inverse).astype(BF)
        mixed_t[rows, pl.ds(start, CHUNK)] = dot(values_t[rows, :], probs_low).astype(BF)
        d_values = d_values + dot(probs_low, m_part)
        scaled = inverse * SCALE
        shift = jnp.sum(terms * d_probs, axis=0, keepdims=True) * (inverse * scaled)
        d_scores = (terms * (d_probs * scaled - shift)).astype(BF)
        d_queries_t[rows, pl.ds(start, CHUNK)] = dot(keys_t[rows, :], d_scores).astype(BF)
        d_keys = d_keys + dot(d_scores, q_part)
        if head % PER == PER - 1 and start + CHUNK == ROWS:
            block = head // PER * LANES
            d_qkv[:, D + block : D + block + LANES] = d_keys.astype(BF)
            d_qkv[:, 2 * D + block : 2 * D + block + LANES] = d_values.astype(BF)

    d_qkv[:, pl.ds(0, D)] = d_queries_t[...].T
    branch = dot(mixed_t[...].T, w_proj[...]).astype(BF)
    backs = (back_0, back_x.at[0], back_2, back_x.at[1])
    for group in range(4):
        for place in range(2):
            start = (2 * group + place) * PIECE
            backs[group][place, 0] = branch[start : start + PIECE]
    normed_t = normed[...].T
    for block in range(9):
        term = dot(normed_t, d_qkv[:, block * LANES : (block + 1) * LANES])
        grads[pl.ds(block * D, D), :] = term.astype(BF)
    for block in range(3):
        term = dot(mixed_t[...], cot[:, block * LANES : (block + 1) * LANES])
        grads[pl.ds((9 + block) * D, D), :] = term.astype(BF)
    for group in range(4):
        part = pl.ds(group * step, step)
        d_normed = dot_t(d_qkv[part, :], w_qkv[...])
        unit_rows = unit[part, :]
        scaled = d_normed * gain_row
        mean_1 = jnp.mean(scaled, axis=-1, keepdims=True)
        mean_2 = jnp.mean(scaled * unit_rows, axis=-1, keepdims=True)
        d_rows = (inv_std[part, 0:1] * (scaled - mean_1 - unit_rows * mean_2)).astype(BF)
        backs[group][0, 1] = d_rows[:PIECE]
        backs[group][1, 1] = d_rows[PIECE:]


def order(odd, upper, inverse):
    flip = odd if upper == 0 else 1 - odd
    shape = (WIN * WIN, WIN * WIN)
    row = lax.broadcasted_iota(jnp.int32, shape, 1 if inverse else 0)
    token = lax.broadcasted_iota(jnp.int32, shape, 0 if inverse else 1)
    along_y = ((row >> 5) ^ flip) * HALF + ((row >> 2) & 3)
    along_z = (((row >> 4) & 1) ^ flip) * HALF + (row & 3)
    return token == along_y * WIN + along_z


def ones_where(chosen):
    return jnp.where(chosen, 1.0, 0.0)


def keep_rows(frozen):
    table = ones_where(frozen[...].reshape(WIN * WIN, WIN) == 1).astype(BF)
    column = lax.broadcasted_iota(jnp.int32, (WIN, WIN * WIN), 1)
    row = lax.broadcasted_iota(jnp.int32, (WIN, WIN * WIN), 0)
    spread = dot(table, ones_where((column & 7) == row).astype(BF))
    chosen = ones_where((column >> 3) == row)
    return [
        jnp.sum(spread[plane * WIN : (plane + 1) * WIN] * chosen, axis=0, keepdims=True)
        for plane in range(WIN)
    ]


def cut_kernel(odd, tokens_in, frozen_in, cotangent_in, own, ahead, tokens, frozen, cotangent, arrivals):
    moves = [
        pltpu.make_async_copy(source, target, arrivals.at[index])
        for index, (source, target) in enumerate(
            ((frozen_in, frozen), (tokens_in, tokens), (cotangent_in, cotangent))
        )
    ]
    for move in moves:
        move.start()
    for move in moves:
        move.wait()
    keeps = keep_rows(frozen)
    for upper, target in ((0, ahead), (1, own)):
        matrix = ones_where(order(odd[0], upper, False))
        for plane in range(HALF):
            index = upper * HALF + plane
            part = pl.ds(index * WIN * WIN, WIN * WIN)
            kept = dot((matrix * keeps[index]).astype(BF), tokens[part, :]).astype(BF)
            cot = dot(matrix.astype(BF), cotangent[part, :]).astype(BF)
            for group in range(4):
                rows = slice(group * 16, group * 16 + 16)
                target[group, 0, pl.ds(plane * 16, 16), :] = kept[rows]
                target[group, 1, pl.ds(plane * 16, 16), :] = cot[rows]


def join_kernel(odd, tokens, frozen, cotangent, home_0, home_x, home_y, ahead, block_out, tokens_grad, token):
    homes = (home_0, home_x.at[0], home_y.at[0], home_y.at[1])
    token[...] = jnp.zeros_like(token)
    keeps = keep_rows(frozen)
    shape = (WIN * WIN, WIN * WIN)
    diagonal = ones_where(lax.broadcasted_iota(jnp.int32, shape, 0) == lax.broadcasted_iota(jnp.int32, shape, 1))
    for upper in range(2):
        matrix = ones_where(order(odd[0], upper, True)).astype(BF)
        for plane in range(HALF):
            index = upper * HALF + plane
            part = pl.ds(index * WIN * WIN, WIN * WIN)
            keep = (diagonal * keeps[index]).astype(BF)
            rows = pl.ds(plane * 16, 16)

            def pieces(array):
                if upper:
                    found = [homes[group][0, array, rows, :] for group in range(4)]
                else:
                    found = [ahead[group, array, rows, :] for group in range(4)]
                return dot(matrix, jnp.concatenate(found, axis=0))

            block_out[part, :] = (dot(keep, tokens[part, :]) + pieces(0)).astype(BF)
            grown = (cotangent[part, :].astype(F32) + pieces(1)).astype(BF)
            tokens_grad[part, :] = dot(keep, grown).astype(BF)


SCALAR = pl.BlockSpec(memory_space=pltpu.SMEM)
WHOLE = pl.BlockSpec(memory_space=pltpu.VMEM)
SMALL = pltpu.CompilerParams(vmem_limit_bytes=12 * 1024 * 1024)


def total_kernel(parts, *rest, copies, out_at):
    out = rest[out_at]
    total = parts[0].astype(F32)
    for index in range(1, parts.shape[0]):
        total = total + parts[index].astype(F32)
    total = total.astype(BF)
    for index in range(copies):
        out[index] = total


def total_of(parts, copies, after=(), through=()):
    anywhere = pl.BlockSpec(memory_space=pl.ANY)
    total, *passed = pl.pallas_call(
        functools.partial(total_kernel, copies=copies, out_at=len(after) + len(through)),
        out_shape=[jax.ShapeDtypeStruct((copies,) + parts.shape[1:], BF)]
        + [jax.ShapeDtypeStruct(array.shape, array.dtype) for array in through],
        in_specs=[WHOLE] + [anywhere] * (len(after) + len(through)),
        out_specs=[WHOLE] + [anywhere] * len(through),
        input_output_aliases={1 + len(after) + at: 1 + at for at in range(len(through))},
        compiler_params=SMALL,
    )(parts, *after, *through)
    return (total, *passed) if through else total


def hold(array, until):
    anywhere = pl.BlockSpec(memory_space=pl.ANY)
    return pl.pallas_call(
        lambda *refs: None,
        out_shape=jax.ShapeDtypeStruct(array.shape, array.dtype),
        in_specs=[anywhere] * 2,
        out_specs=anywhere,
        input_output_aliases={0: 0},
        compiler_params=SMALL,
    )(array, until)


def grads_kernel(core, mine, other, w_qkv, gain, qkv_grad, proj_grad, gain_grad):
    grad_scale = (ROWS * 512) ** (-0.5)
    half = GRAD_ROWS // 2
    first = core[0] == 0
    weighted = jnp.zeros((D, LANES), F32)
    for block in range(12):
        start = block * D
        if start < half:
            part = pl.ds(start, D)
            found = jnp.where(first, mine[part, :].astype(F32), other[part, :].astype(F32))
        else:
            part = pl.ds(start - half, D)
            found = jnp.where(first, other[part, :].astype(F32), mine[part, :].astype(F32))
        found = found * grad_scale
        target, column = (qkv_grad, block) if block < 9 else (proj_grad, block - 9)
        columns = slice(column * LANES, (column + 1) * LANES)
        target[:, columns] = found
        if block < 9:
            weighted = weighted + found * w_qkv[:, columns].astype(F32)
    gain_grad[...] = (jnp.sum(weighted.T, axis=0, keepdims=True) / gain[...]).reshape(D)


def window_pass(own, behind, sides, w_qkv, w_proj, norm_gain):
    def buffer(shape, kind):
        return pltpu.VMEM(shape, kind)

    return pl.pallas_call(
        window_kernel,
        out_shape=(jax.ShapeDtypeStruct((2, 2, PIECE, D), BF),) * 2
        + (jax.ShapeDtypeStruct((2, 2, 2, PIECE, D), BF), jax.ShapeDtypeStruct((GRAD_ROWS, LANES), BF)),
        scratch_shapes=[
            buffer((ROWS, D), BF),
            buffer((ROWS, 3 * D), BF),
            buffer((ROWS, D), BF),
            buffer((D, ROWS), BF),
            buffer((D, ROWS), BF),
            buffer((D, ROWS), BF),
            buffer((D, ROWS), BF),
            buffer((ROWS, 3 * D), BF),
            buffer((ROWS, D), F32),
            buffer((ROWS, LANES), F32),
            buffer((ROWS, D), BF),
        ],
        compiler_params=pltpu.CompilerParams(vmem_limit_bytes=40 * 1024 * 1024),
        cost_estimate=pl.CostEstimate(
            flops=16_000_000_000, bytes_accessed=5_000_000, transcendentals=3_200_000
        ),
    )(own, behind, *sides[::-1], w_qkv, w_proj, norm_gain.reshape(1, D))


LATTICE = ("z_hi", "z_lo", "core", "y_hi", "y_lo", "x")
FIRST = ("z_hi", "z_lo", "core")
SECOND = ("y_hi",)
THIRD = ("y_lo", "x")
SIZES = {"z_hi": 4, "z_lo": 2, "core": 2, "y_hi": 4, "y_lo": 2, "x": 4}
NEAR = ("x", "y_lo", "z_lo")
GROUP = 16
FAR = 4


def near_sum(rows):
    halves = lax.all_to_all(rows.reshape(2, GRAD_ROWS // 2, LANES), "core", 0, 0)
    parts = total_of(halves, 1).reshape(GROUP, GRAD_ROWS // 2 // GROUP, LANES)
    parts = lax.all_to_all(parts, NEAR, 0, 0)
    return parts


def device_at(first, second, third):
    return ((first % 16) * 4 + second % 4) * 8 + third % 8


def route(kind, back):
    pairs = []
    for first in range(16):
        for second in range(4):
            for third in range(8):
                sign = 1 if first % 2 else -1
                if kind == 0:
                    move = (first - 1, second, third)
                else:
                    move = (first, second + sign * (kind >> 1), third + sign * (kind & 1))
                pair = (device_at(first, second, third), device_at(*move))
                pairs.append(pair[::-1] if back else pair)
    return pairs


def send(block, kind, back=False):
    return lax.ppermute(block, LATTICE, route(kind, back))


def local(tokens, frozen, cotangent, w_qkv, w_proj, norm_gain):
    core = lax.axis_index("core").reshape(1)
    token_rows, cot_rows = tokens.reshape(ROWS, D), cotangent.reshape(ROWS, D)
    own, ahead = pl.pallas_call(
        cut_kernel,
        out_shape=(jax.ShapeDtypeStruct((4, 2, PIECE, D), BF),) * 2,
        in_specs=[SCALAR] + [pl.BlockSpec(memory_space=pltpu.HBM)] * 3,
        scratch_shapes=[
            pltpu.VMEM((ROWS, D), BF),
            pltpu.VMEM((WIN, WIN, WIN), jnp.int32),
            pltpu.VMEM((ROWS, D), BF),
            pltpu.SemaphoreType.DMA((3,)),
        ],
        compiler_params=pltpu.CompilerParams(vmem_limit_bytes=56 * 1024 * 1024),
    )(core, token_rows, frozen, cot_rows)
    behind = send(ahead, 0)
    sides = [None] * 4
    for kind in (1, 2, 3):
        sides[kind] = send(jnp.stack([own[kind], behind[kind]]), kind)
    back_0, back_2, back_x, grads = window_pass(own, behind, sides[1:], w_qkv, w_proj, norm_gain)
    parts = near_sum(grads)
    home_x = send(back_x, 1, True)
    parts, back_2 = total_of(parts, FAR, after=(home_x,), through=(back_2,))
    home_y = send(jnp.stack([back_2, home_x[1]]), 2, True)
    parts, home_y = total_of(lax.all_to_all(parts, "y_hi", 0, 0), FAR, through=(home_y,))
    ahead = send(jnp.stack([back_0[1], home_x[0, 1], home_y[0, 1], home_y[1, 1]]), 0, True)
    parts = total_of(lax.all_to_all(parts, "z_hi", 0, 0), GROUP, after=(ahead,))
    mine = lax.all_to_all(parts, NEAR, 0, 0).reshape(GRAD_ROWS // 2, LANES)
    block_out, tokens_grad, token = pl.pallas_call(
        join_kernel,
        out_shape=(jax.ShapeDtypeStruct((ROWS, D), BF),) * 2 + (jax.ShapeDtypeStruct((8, LANES), F32),),
        in_specs=[SCALAR] + [WHOLE] * 7,
        compiler_params=SMALL,
        cost_estimate=pl.CostEstimate(flops=300_000_000, bytes_accessed=4_000_000, transcendentals=0),
    )(core, token_rows, frozen, cot_rows, back_0, home_x, home_y, ahead)
    mine = hold(mine, token)
    other = lax.ppermute(mine, "core", [(0, 1), (1, 0)])
    qkv_grad, proj_grad, gain_grad = pl.pallas_call(
        grads_kernel,
        out_shape=(
            jax.ShapeDtypeStruct((D, 3 * D), F32),
            jax.ShapeDtypeStruct((D, D), F32),
            jax.ShapeDtypeStruct((D,), F32),
        ),
        in_specs=[SCALAR] + [WHOLE] * 4,
        compiler_params=SMALL,
    )(core, mine, other, w_qkv, norm_gain.reshape(1, D))
    shape = (WIN, WIN, WIN, D)
    return block_out.reshape(shape), tokens_grad.reshape(shape), qkv_grad, proj_grad, gain_grad


def solution(mesh):
    inner = Mesh(mesh.devices.reshape([SIZES[axis] for axis in LATTICE]), LATTICE)
    lattice = P(FIRST, SECOND, THIRD)
    wide = P(FIRST, SECOND, THIRD, None)
    return jax.shard_map(
        local,
        mesh=inner,
        in_specs=(wide, lattice, wide, P(), P(), P()),
        out_specs=(wide, wide, P(), P(), P()),
        check_vma=False,
    )
```

```python
import functools

import jax
import jax.numpy as jnp
import numpy as np
from jax import lax
from jax.experimental import pallas as pl
from jax.experimental.pallas import tpu as pltpu
from jax.sharding import Mesh, PartitionSpec as P

D = 384
HEADS = 12
HDIM = 32
WIN = 8
HALF = WIN // 2
ROWS = WIN**3
PIECE = HALF**3
EPSILON = 1e-05
BF = jnp.bfloat16
F32 = jnp.float32
LANES = 128
PER = LANES // HDIM
CHUNK = 256
SCALE = HDIM ** (-0.5)
LOG2E = 1.4426950408889634
GRAD_ROWS = 12 * D


def dot(left, right):
    return jnp.dot(left, right, preferred_element_type=F32)


def dot_t(left, right):
    return lax.dot_general(left, right, (((1,), (1,)), ((), ())), preferred_element_type=F32)


def window_kernel(
    own, behind, side_3, side_2, side_1, w_qkv, w_proj, gain, grads, mixed_t, d_qkv, unit, inv_std,
    cot, qkv, d_mixed, keys_t, values_t, d_queries_t, normed,
):
    step = 2 * PIECE
    gain_row = gain[...]

    def arrived(group, array):
        if group == 0:
            return own[0, array], behind[0, array]
        side = (side_1, side_2, side_3)[group - 1]
        return side[0, array], side[1, array]

    for group in range(4):
        part = pl.ds(group * step, step)
        cot[part, :] = jnp.concatenate(arrived(group, 1), axis=0)
        rows = jnp.concatenate(arrived(group, 0), axis=0).astype(F32)
        centred = rows - jnp.mean(rows, axis=-1, keepdims=True)
        inverse = lax.rsqrt(jnp.mean(centred * centred, axis=-1, keepdims=True) + EPSILON)
        unit_rows = centred * inverse
        unit[part, :] = unit_rows
        inv_std[part, :] = jnp.broadcast_to(inverse, (step, LANES))
        normed[part, :] = (unit_rows * gain_row).astype(BF)
    qkv[...] = dot(normed[...], w_qkv[...]).astype(BF)
    d_mixed[...] = dot_t(cot[...], w_proj[...]).astype(BF)
    keys_t[...] = qkv[:, D : 2 * D].T
    values_t[...] = qkv[:, 2 * D :].T
    lane = lax.broadcasted_iota(jnp.int32, (1, LANES), 1)

    def first_products(head, start):
        block = slice(head // PER * LANES, (head // PER + 1) * LANES)
        mine = (lane // HDIM) == head % PER
        queries = pl.ds(start, CHUNK)
        zeros = jnp.zeros((CHUNK, LANES), BF)
        q_part = jnp.where(mine, qkv[queries, block], zeros)
        m_part = jnp.where(mine, d_mixed[queries, block], zeros)
        scores = dot_t(qkv[:, D + block.start : D + block.stop], q_part)
        d_probs = dot_t(qkv[:, 2 * D + block.start : 2 * D + block.stop], m_part)
        return q_part, m_part, scores, d_probs

    steps = [(head, start) for head in range(HEADS) for start in range(0, ROWS, CHUNK)]
    ready = first_products(*steps[0])
    for index, (head, start) in enumerate(steps):
        q_part, m_part, scores, d_probs = ready
        if index + 1 < len(steps):
            ready = first_products(*steps[index + 1])
        if head % PER == 0 and start == 0:
            d_keys = jnp.zeros((ROWS, LANES), F32)
            d_values = jnp.zeros((ROWS, LANES), F32)
        rows = pl.ds(head * HDIM, HDIM)
        top = jnp.max(scores, axis=0, keepdims=True)
        terms = jnp.exp2(scores * (SCALE * LOG2E) - top * (SCALE * LOG2E))
        inverse = 1.0 / jnp.sum(terms, axis=0, keepdims=True)
        probs_low = (terms * inverse).astype(BF)
        mixed_t[rows, pl.ds(start, CHUNK)] = dot(values_t[rows, :], probs_low).astype(BF)
        d_values = d_values + dot(probs_low, m_part)
        scaled = inverse * SCALE
        shift = jnp.sum(terms * d_probs, axis=0, keepdims=True) * (inverse * scaled)
        d_scores = (terms * (d_probs * scaled - shift)).astype(BF)
        d_queries_t[rows, pl.ds(start, CHUNK)] = dot(keys_t[rows, :], d_scores).astype(BF)
        d_keys = d_keys + dot(d_scores, q_part)
        if head % PER == PER - 1 and start + CHUNK == ROWS:
            block = head // PER * LANES
            d_qkv[:, D + block : D + block + LANES] = d_keys.astype(BF)
            d_qkv[:, 2 * D + block : 2 * D + block + LANES] = d_values.astype(BF)

    d_qkv[:, pl.ds(0, D)] = d_queries_t[...].T
    normed_t = normed[...].T
    for block in range(9):
        term = dot(normed_t, d_qkv[:, block * LANES : (block + 1) * LANES])
        grads[pl.ds(block * D, D), :] = term.astype(BF)
    for block in range(3):
        term = dot(mixed_t[...], cot[:, block * LANES : (block + 1) * LANES])
        grads[pl.ds((9 + block) * D, D), :] = term.astype(BF)


def rows_kernel(mixed_t, d_qkv, unit, inv_std, w_qkv, w_proj, gain, back_0, back_1, back_y):
    step = 2 * PIECE
    backs = (back_0, back_1, back_y.at[0], back_y.at[1])
    branch = dot(mixed_t[...].T, w_proj[...]).astype(BF)
    for group in range(4):
        part = pl.ds(group * step, step)
        d_normed = dot_t(d_qkv[part, :], w_qkv[...])
        unit_rows = unit[part, :]
        scaled = d_normed * gain[...]
        mean_1 = jnp.mean(scaled, axis=-1, keepdims=True)
        mean_2 = jnp.mean(scaled * unit_rows, axis=-1, keepdims=True)
        d_rows = (inv_std[part, 0:1] * (scaled - mean_1 - unit_rows * mean_2)).astype(BF)
        for place in range(2):
            start = (2 * group + place) * PIECE
            backs[group][place, 0] = branch[start : start + PIECE]
            backs[group][place, 1] = d_rows[place * PIECE : (place + 1) * PIECE]


def order(odd, upper, inverse):
    flip = odd if upper == 0 else 1 - odd
    shape = (WIN * WIN, WIN * WIN)
    row = lax.broadcasted_iota(jnp.int32, shape, 1 if inverse else 0)
    token = lax.broadcasted_iota(jnp.int32, shape, 0 if inverse else 1)
    along_y = ((row >> 5) ^ flip) * HALF + ((row >> 2) & 3)
    along_z = (((row >> 4) & 1) ^ flip) * HALF + (row & 3)
    return token == along_y * WIN + along_z


def ones_where(chosen):
    return jnp.where(chosen, 1.0, 0.0)


def keep_rows(frozen):
    table = ones_where(frozen[...].reshape(WIN * WIN, WIN) == 1).astype(BF)
    column = lax.broadcasted_iota(jnp.int32, (WIN, WIN * WIN), 1)
    row = lax.broadcasted_iota(jnp.int32, (WIN, WIN * WIN), 0)
    spread = dot(table, ones_where((column & 7) == row).astype(BF))
    chosen = ones_where((column >> 3) == row)
    return [
        jnp.sum(spread[plane * WIN : (plane + 1) * WIN] * chosen, axis=0, keepdims=True)
        for plane in range(WIN)
    ]


def cut_kernel(odd, tokens_in, frozen_in, cotangent_in, own, ahead, tokens, frozen, cotangent, arrivals):
    moves = [
        pltpu.make_async_copy(source, target, arrivals.at[index])
        for index, (source, target) in enumerate(
            ((frozen_in, frozen), (tokens_in, tokens), (cotangent_in, cotangent))
        )
    ]
    for move in moves:
        move.start()
    for move in moves:
        move.wait()
    keeps = keep_rows(frozen)
    for upper, target in ((0, ahead), (1, own)):
        matrix = ones_where(order(odd[0], upper, False))
        for plane in range(HALF):
            index = upper * HALF + plane
            part = pl.ds(index * WIN * WIN, WIN * WIN)
            kept = dot((matrix * keeps[index]).astype(BF), tokens[part, :]).astype(BF)
            cot = dot(matrix.astype(BF), cotangent[part, :]).astype(BF)
            for group in range(4):
                rows = slice(group * 16, group * 16 + 16)
                target[group, 0, pl.ds(plane * 16, 16), :] = kept[rows]
                target[group, 1, pl.ds(plane * 16, 16), :] = cot[rows]


def join_kernel(odd, tokens, frozen, cotangent, home_0, home_x, home_2, ahead, block_out, tokens_grad):
    homes = (home_0, home_x.at[0], home_2.at[0], home_x.at[1])
    keeps = keep_rows(frozen)
    shape = (WIN * WIN, WIN * WIN)
    diagonal = ones_where(lax.broadcasted_iota(jnp.int32, shape, 0) == lax.broadcasted_iota(jnp.int32, shape, 1))
    for upper in range(2):
        matrix = ones_where(order(odd[0], upper, True)).astype(BF)
        for plane in range(HALF):
            index = upper * HALF + plane
            part = pl.ds(index * WIN * WIN, WIN * WIN)
            keep = (diagonal * keeps[index]).astype(BF)
            rows = pl.ds(plane * 16, 16)

            def pieces(array):
                if upper:
                    found = [homes[group][0, array, rows, :] for group in range(4)]
                else:
                    found = [ahead[group, array, rows, :] for group in range(4)]
                return dot(matrix, jnp.concatenate(found, axis=0))

            block_out[part, :] = (dot(keep, tokens[part, :]) + pieces(0)).astype(BF)
            grown = (cotangent[part, :].astype(F32) + pieces(1)).astype(BF)
            tokens_grad[part, :] = dot(keep, grown).astype(BF)


SCALAR = pl.BlockSpec(memory_space=pltpu.SMEM)
WHOLE = pl.BlockSpec(memory_space=pltpu.VMEM)
SMALL = pltpu.CompilerParams(vmem_limit_bytes=12 * 1024 * 1024)


def total_kernel(parts, *rest, copies, out_at):
    out = rest[out_at]
    total = parts[0].astype(F32)
    for index in range(1, parts.shape[0]):
        total = total + parts[index].astype(F32)
    total = total.astype(BF)
    for index in range(copies):
        out[index] = total


def total_of(parts, copies, after=(), through=()):
    anywhere = pl.BlockSpec(memory_space=pl.ANY)
    total, *passed = pl.pallas_call(
        functools.partial(total_kernel, copies=copies, out_at=len(after) + len(through)),
        out_shape=[jax.ShapeDtypeStruct((copies,) + parts.shape[1:], BF)]
        + [jax.ShapeDtypeStruct(array.shape, array.dtype) for array in through],
        in_specs=[WHOLE] + [anywhere] * (len(after) + len(through)),
        out_specs=[WHOLE] + [anywhere] * len(through),
        input_output_aliases={1 + len(after) + at: 1 + at for at in range(len(through))},
        compiler_params=SMALL,
    )(parts, *after, *through)
    return (total, *passed) if through else total


def hold(array, until):
    anywhere = pl.BlockSpec(memory_space=pl.ANY)
    return pl.pallas_call(
        lambda *refs: None,
        out_shape=jax.ShapeDtypeStruct(array.shape, array.dtype),
        in_specs=[anywhere] * 2,
        out_specs=anywhere,
        input_output_aliases={0: 0},
        compiler_params=SMALL,
    )(array, until)


def grads_kernel(core, mine, other, w_qkv, gain, qkv_grad, proj_grad, gain_grad):
    grad_scale = (ROWS * 512) ** (-0.5)
    half = GRAD_ROWS // 2
    first = core[0] == 0
    weighted = jnp.zeros((D, LANES), F32)
    for block in range(12):
        start = block * D
        if start < half:
            part = pl.ds(start, D)
            found = jnp.where(first, mine[part, :].astype(F32), other[part, :].astype(F32))
        else:
            part = pl.ds(start - half, D)
            found = jnp.where(first, other[part, :].astype(F32), mine[part, :].astype(F32))
        found = found * grad_scale
        target, column = (qkv_grad, block) if block < 9 else (proj_grad, block - 9)
        columns = slice(column * LANES, (column + 1) * LANES)
        target[:, columns] = found
        if block < 9:
            weighted = weighted + found * w_qkv[:, columns].astype(F32)
    gain_grad[...] = (jnp.sum(weighted.T, axis=0, keepdims=True) / gain[...]).reshape(D)


def window_pass(own, behind, sides, w_qkv, w_proj, norm_gain):
    def buffer(shape, kind):
        return pltpu.VMEM(shape, kind)

    gain = norm_gain.reshape(1, D)
    grads, *kept = pl.pallas_call(
        window_kernel,
        out_shape=(
            jax.ShapeDtypeStruct((GRAD_ROWS, LANES), BF),
            jax.ShapeDtypeStruct((D, ROWS), BF),
            jax.ShapeDtypeStruct((ROWS, 3 * D), BF),
            jax.ShapeDtypeStruct((ROWS, D), F32),
            jax.ShapeDtypeStruct((ROWS, LANES), F32),
        ),
        scratch_shapes=[
            buffer((ROWS, D), BF),
            buffer((ROWS, 3 * D), BF),
            buffer((ROWS, D), BF),
            buffer((D, ROWS), BF),
            buffer((D, ROWS), BF),
            buffer((D, ROWS), BF),
            buffer((ROWS, D), BF),
        ],
        compiler_params=pltpu.CompilerParams(vmem_limit_bytes=32 * 1024 * 1024),
        cost_estimate=pl.CostEstimate(
            flops=12_000_000_000, bytes_accessed=5_000_000, transcendentals=3_200_000
        ),
    )(own, behind, *sides[::-1], w_qkv, w_proj, gain)
    backs = pl.pallas_call(
        rows_kernel,
        out_shape=(jax.ShapeDtypeStruct((2, 2, PIECE, D), BF),) * 2
        + (jax.ShapeDtypeStruct((2, 2, 2, PIECE, D), BF),),
        compiler_params=pltpu.CompilerParams(vmem_limit_bytes=24 * 1024 * 1024),
        cost_estimate=pl.CostEstimate(flops=2_000_000_000, bytes_accessed=4_000_000, transcendentals=0),
    )(*kept, w_qkv, w_proj, gain)
    return *backs, grads


LATTICE = ("z_hi", "z_lo", "core", "y_hi", "y_lo", "x")
FIRST = ("z_hi", "z_lo", "core")
SECOND = ("y_hi",)
THIRD = ("y_lo", "x")
SIZES = {"z_hi": 4, "z_lo": 2, "core": 2, "y_hi": 4, "y_lo": 2, "x": 4}
NEAR = ("x", "y_lo", "z_lo")
GROUP = 16
FAR = 4


def near_sum(rows):
    halves = lax.all_to_all(rows.reshape(2, GRAD_ROWS // 2, LANES), "core", 0, 0)
    parts = total_of(halves, 1).reshape(GROUP, GRAD_ROWS // 2 // GROUP, LANES)
    parts = lax.all_to_all(parts, NEAR, 0, 0)
    return parts


def device_at(first, second, third):
    return ((first % 16) * 4 + second % 4) * 8 + third % 8


def route(kind, back):
    pairs = []
    for first in range(16):
        for second in range(4):
            for third in range(8):
                sign = 1 if first % 2 else -1
                if kind == 0:
                    move = (first - 1, second, third)
                else:
                    move = (first, second + sign * (kind >> 1), third + sign * (kind & 1))
                pair = (device_at(first, second, third), device_at(*move))
                pairs.append(pair[::-1] if back else pair)
    return pairs


def send(block, kind, back=False):
    return lax.ppermute(block, LATTICE, route(kind, back))


def local(tokens, frozen, cotangent, w_qkv, w_proj, norm_gain):
    core = lax.axis_index("core").reshape(1)
    token_rows, cot_rows = tokens.reshape(ROWS, D), cotangent.reshape(ROWS, D)
    own, ahead = pl.pallas_call(
        cut_kernel,
        out_shape=(jax.ShapeDtypeStruct((4, 2, PIECE, D), BF),) * 2,
        in_specs=[SCALAR] + [pl.BlockSpec(memory_space=pltpu.HBM)] * 3,
        scratch_shapes=[
            pltpu.VMEM((ROWS, D), BF),
            pltpu.VMEM((WIN, WIN, WIN), jnp.int32),
            pltpu.VMEM((ROWS, D), BF),
            pltpu.SemaphoreType.DMA((3,)),
        ],
        compiler_params=pltpu.CompilerParams(vmem_limit_bytes=56 * 1024 * 1024),
    )(core, token_rows, frozen, cot_rows)
    behind = send(ahead, 0)
    sides = [None] * 4
    for kind in (1, 2, 3):
        sides[kind] = send(jnp.stack([own[kind], behind[kind]]), kind)
    back_0, back_1, back_y, grads = window_pass(own, behind, sides[1:], w_qkv, w_proj, norm_gain)
    parts = near_sum(grads)
    parts, back_y = total_of(parts, FAR, through=(back_y,))
    home_y = send(back_y, 2, True)
    parts = total_of(lax.all_to_all(parts, "z_hi", 0, 0), FAR)
    home_x = send(jnp.stack([back_1, home_y[1]]), 1, True)
    parts = total_of(lax.all_to_all(parts, "y_hi", 0, 0), GROUP, after=(home_x,))
    mine = lax.all_to_all(parts, NEAR, 0, 0).reshape(GRAD_ROWS // 2, LANES)
    ahead = send(jnp.stack([back_0[1], home_x[0, 1], home_y[0, 1], home_x[1, 1]]), 0, True)
    block_out, tokens_grad = pl.pallas_call(
        join_kernel,
        out_shape=(jax.ShapeDtypeStruct((ROWS, D), BF),) * 2,
        in_specs=[SCALAR] + [WHOLE] * 7,
        compiler_params=SMALL,
        cost_estimate=pl.CostEstimate(flops=300_000_000, bytes_accessed=4_000_000, transcendentals=0),
    )(core, token_rows, frozen, cot_rows, back_0, home_x, home_y, ahead)
    mine = hold(mine, ahead)
    other = lax.ppermute(mine, "core", [(0, 1), (1, 0)])
    qkv_grad, proj_grad, gain_grad = pl.pallas_call(
        grads_kernel,
        out_shape=(
            jax.ShapeDtypeStruct((D, 3 * D), F32),
            jax.ShapeDtypeStruct((D, D), F32),
            jax.ShapeDtypeStruct((D,), F32),
        ),
        in_specs=[SCALAR] + [WHOLE] * 4,
        compiler_params=SMALL,
    )(core, mine, other, w_qkv, norm_gain.reshape(1, D))
    shape = (WIN, WIN, WIN, D)
    return block_out.reshape(shape), tokens_grad.reshape(shape), qkv_grad, proj_grad, gain_grad


def solution(mesh):
    inner = Mesh(mesh.devices.reshape([SIZES[axis] for axis in LATTICE]), LATTICE)
    lattice = P(FIRST, SECOND, THIRD)
    wide = P(FIRST, SECOND, THIRD, None)
    return jax.shard_map(
        local,
        mesh=inner,
        in_specs=(wide, lattice, wide, P(), P(), P()),
        out_specs=(wide, wide, P(), P(), P()),
        check_vma=False,
    )
```

```python
import functools

import jax
import jax.numpy as jnp
import numpy as np
from jax import lax
from jax.experimental import pallas as pl
from jax.experimental.pallas import tpu as pltpu
from jax.sharding import Mesh, PartitionSpec as P

D = 384
HEADS = 12
HDIM = 32
WIN = 8
HALF = WIN // 2
ROWS = WIN**3
PIECE = HALF**3
EPSILON = 1e-05
BF = jnp.bfloat16
F32 = jnp.float32
LANES = 128
PER = LANES // HDIM
CHUNK = 256
SCALE = HDIM ** (-0.5)
LOG2E = 1.4426950408889634
GRAD_ROWS = 12 * D


def dot(left, right):
    return jnp.dot(left, right, preferred_element_type=F32)


def dot_t(left, right):
    return lax.dot_general(left, right, (((1,), (1,)), ((), ())), preferred_element_type=F32)


def window_kernel(
    own, behind, side_3, side_2, side_1, w_qkv, w_proj, gain, grads, mixed_t, d_qkv, unit, inv_std,
    cot, qkv, d_mixed, keys_t, values_t, d_queries_t, normed,
):
    step = 2 * PIECE
    gain_row = gain[...]

    def arrived(group, array):
        if group == 0:
            return own[0, array], behind[0, array]
        side = (side_1, side_2, side_3)[group - 1]
        return side[0, array], side[1, array]

    for group in range(4):
        part = pl.ds(group * step, step)
        cot[part, :] = jnp.concatenate(arrived(group, 1), axis=0)
        rows = jnp.concatenate(arrived(group, 0), axis=0).astype(F32)
        centred = rows - jnp.mean(rows, axis=-1, keepdims=True)
        inverse = lax.rsqrt(jnp.mean(centred * centred, axis=-1, keepdims=True) + EPSILON)
        unit_rows = centred * inverse
        unit[part, :] = unit_rows
        inv_std[part, :] = jnp.broadcast_to(inverse, (step, LANES))
        normed[part, :] = (unit_rows * gain_row).astype(BF)
    qkv[...] = dot(normed[...], w_qkv[...]).astype(BF)
    d_mixed[...] = dot_t(cot[...], w_proj[...]).astype(BF)
    keys_t[...] = qkv[:, D : 2 * D].T
    values_t[...] = qkv[:, 2 * D :].T
    lane = lax.broadcasted_iota(jnp.int32, (1, LANES), 1)

    def first_products(head, start):
        block = slice(head // PER * LANES, (head // PER + 1) * LANES)
        mine = (lane // HDIM) == head % PER
        queries = pl.ds(start, CHUNK)
        zeros = jnp.zeros((CHUNK, LANES), BF)
        q_part = jnp.where(mine, qkv[queries, block], zeros)
        m_part = jnp.where(mine, d_mixed[queries, block], zeros)
        scores = dot_t(qkv[:, D + block.start : D + block.stop], q_part)
        d_probs = dot_t(qkv[:, 2 * D + block.start : 2 * D + block.stop], m_part)
        return q_part, m_part, scores, d_probs

    steps = [(head, start) for head in range(HEADS) for start in range(0, ROWS, CHUNK)]
    ready = first_products(*steps[0])
    for index, (head, start) in enumerate(steps):
        q_part, m_part, scores, d_probs = ready
        if index + 1 < len(steps):
            ready = first_products(*steps[index + 1])
        if head % PER == 0 and start == 0:
            d_keys = jnp.zeros((ROWS, LANES), F32)
            d_values = jnp.zeros((ROWS, LANES), F32)
        rows = pl.ds(head * HDIM, HDIM)
        top = jnp.max(scores, axis=0, keepdims=True)
        terms = jnp.exp2(scores * (SCALE * LOG2E) - top * (SCALE * LOG2E))
        inverse = 1.0 / jnp.sum(terms, axis=0, keepdims=True)
        probs_low = (terms * inverse).astype(BF)
        mixed_t[rows, pl.ds(start, CHUNK)] = dot(values_t[rows, :], probs_low).astype(BF)
        d_values = d_values + dot(probs_low, m_part)
        scaled = inverse * SCALE
        shift = jnp.sum(terms * d_probs, axis=0, keepdims=True) * (inverse * scaled)
        d_scores = (terms * (d_probs * scaled - shift)).astype(BF)
        d_queries_t[rows, pl.ds(start, CHUNK)] = dot(keys_t[rows, :], d_scores).astype(BF)
        d_keys = d_keys + dot(d_scores, q_part)
        if head % PER == PER - 1 and start + CHUNK == ROWS:
            block = head // PER * LANES
            d_qkv[:, D + block : D + block + LANES] = d_keys.astype(BF)
            d_qkv[:, 2 * D + block : 2 * D + block + LANES] = d_values.astype(BF)

    d_qkv[:, pl.ds(0, D)] = d_queries_t[...].T
    normed_t = normed[...].T
    for block in range(9):
        term = dot(normed_t, d_qkv[:, block * LANES : (block + 1) * LANES])
        grads[pl.ds(block * D, D), :] = term.astype(BF)
    for block in range(3):
        term = dot(mixed_t[...], cot[:, block * LANES : (block + 1) * LANES])
        grads[pl.ds((9 + block) * D, D), :] = term.astype(BF)


def rows_kernel(mixed_t, d_qkv, unit, inv_std, w_qkv, w_proj, gain, back_0, back_1, back_y):
    step = 2 * PIECE
    backs = (back_0, back_1, back_y.at[0], back_y.at[1])
    branch = dot(mixed_t[...].T, w_proj[...]).astype(BF)
    for group in range(4):
        part = pl.ds(group * step, step)
        d_normed = dot_t(d_qkv[part, :], w_qkv[...])
        unit_rows = unit[part, :]
        scaled = d_normed * gain[...]
        mean_1 = jnp.mean(scaled, axis=-1, keepdims=True)
        mean_2 = jnp.mean(scaled * unit_rows, axis=-1, keepdims=True)
        d_rows = (inv_std[part, 0:1] * (scaled - mean_1 - unit_rows * mean_2)).astype(BF)
        for place in range(2):
            start = (2 * group + place) * PIECE
            backs[group][place, 0] = branch[start : start + PIECE]
            backs[group][place, 1] = d_rows[place * PIECE : (place + 1) * PIECE]


def order(odd, upper, inverse):
    flip = odd if upper == 0 else 1 - odd
    shape = (WIN * WIN, WIN * WIN)
    row = lax.broadcasted_iota(jnp.int32, shape, 1 if inverse else 0)
    token = lax.broadcasted_iota(jnp.int32, shape, 0 if inverse else 1)
    along_y = ((row >> 5) ^ flip) * HALF + ((row >> 2) & 3)
    along_z = (((row >> 4) & 1) ^ flip) * HALF + (row & 3)
    return token == along_y * WIN + along_z


def ones_where(chosen):
    return jnp.where(chosen, 1.0, 0.0)


def keep_rows(frozen):
    table = ones_where(frozen[...].reshape(WIN * WIN, WIN) == 1).astype(BF)
    column = lax.broadcasted_iota(jnp.int32, (WIN, WIN * WIN), 1)
    row = lax.broadcasted_iota(jnp.int32, (WIN, WIN * WIN), 0)
    spread = dot(table, ones_where((column & 7) == row).astype(BF))
    chosen = ones_where((column >> 3) == row)
    return [
        jnp.sum(spread[plane * WIN : (plane + 1) * WIN] * chosen, axis=0, keepdims=True)
        for plane in range(WIN)
    ]


def cut_kernel(odd, tokens_in, frozen_in, cotangent_in, own, ahead, tokens, frozen, cotangent, arrivals):
    moves = [
        pltpu.make_async_copy(source, target, arrivals.at[index])
        for index, (source, target) in enumerate(
            ((frozen_in, frozen), (tokens_in, tokens), (cotangent_in, cotangent))
        )
    ]
    for move in moves:
        move.start()
    for move in moves:
        move.wait()
    keeps = keep_rows(frozen)
    for upper, target in ((0, ahead), (1, own)):
        matrix = ones_where(order(odd[0], upper, False))
        for plane in range(HALF):
            index = upper * HALF + plane
            part = pl.ds(index * WIN * WIN, WIN * WIN)
            kept = dot((matrix * keeps[index]).astype(BF), tokens[part, :]).astype(BF)
            cot = dot(matrix.astype(BF), cotangent[part, :]).astype(BF)
            for group in range(4):
                rows = slice(group * 16, group * 16 + 16)
                target[group, 0, pl.ds(plane * 16, 16), :] = kept[rows]
                target[group, 1, pl.ds(plane * 16, 16), :] = cot[rows]


def join_kernel(odd, tokens, frozen, cotangent, home_0, home_x, home_2, ahead, block_out, tokens_grad):
    homes = (home_0, home_x.at[0], home_2.at[0], home_x.at[1])
    keeps = keep_rows(frozen)
    shape = (WIN * WIN, WIN * WIN)
    diagonal = ones_where(lax.broadcasted_iota(jnp.int32, shape, 0) == lax.broadcasted_iota(jnp.int32, shape, 1))
    for upper in range(2):
        matrix = ones_where(order(odd[0], upper, True)).astype(BF)
        for plane in range(HALF):
            index = upper * HALF + plane
            part = pl.ds(index * WIN * WIN, WIN * WIN)
            keep = (diagonal * keeps[index]).astype(BF)
            rows = pl.ds(plane * 16, 16)

            def pieces(array):
                if upper:
                    found = [homes[group][0, array, rows, :] for group in range(4)]
                else:
                    found = [ahead[group, array, rows, :] for group in range(4)]
                return dot(matrix, jnp.concatenate(found, axis=0))

            block_out[part, :] = (dot(keep, tokens[part, :]) + pieces(0)).astype(BF)
            grown = (cotangent[part, :].astype(F32) + pieces(1)).astype(BF)
            tokens_grad[part, :] = dot(keep, grown).astype(BF)


SCALAR = pl.BlockSpec(memory_space=pltpu.SMEM)
WHOLE = pl.BlockSpec(memory_space=pltpu.VMEM)
SMALL = pltpu.CompilerParams(vmem_limit_bytes=12 * 1024 * 1024)


def total_kernel(parts, *rest, copies, out_at):
    out = rest[out_at]
    total = parts[0].astype(F32)
    for index in range(1, parts.shape[0]):
        total = total + parts[index].astype(F32)
    total = total.astype(BF)
    for index in range(copies):
        out[index] = total


def total_of(parts, copies, after=(), through=()):
    anywhere = pl.BlockSpec(memory_space=pl.ANY)
    total, *passed = pl.pallas_call(
        functools.partial(total_kernel, copies=copies, out_at=len(after) + len(through)),
        out_shape=[jax.ShapeDtypeStruct((copies,) + parts.shape[1:], BF)]
        + [jax.ShapeDtypeStruct(array.shape, array.dtype) for array in through],
        in_specs=[WHOLE] + [anywhere] * (len(after) + len(through)),
        out_specs=[WHOLE] + [anywhere] * len(through),
        input_output_aliases={1 + len(after) + at: 1 + at for at in range(len(through))},
        compiler_params=SMALL,
    )(parts, *after, *through)
    return (total, *passed) if through else total


def hold(array, until):
    anywhere = pl.BlockSpec(memory_space=pl.ANY)
    return pl.pallas_call(
        lambda *refs: None,
        out_shape=jax.ShapeDtypeStruct(array.shape, array.dtype),
        in_specs=[anywhere] * 2,
        out_specs=anywhere,
        input_output_aliases={0: 0},
        compiler_params=SMALL,
    )(array, until)


def grads_kernel(core, mine, other, w_qkv, gain, qkv_grad, proj_grad, gain_grad):
    grad_scale = (ROWS * 512) ** (-0.5)
    half = GRAD_ROWS // 2
    first = core[0] == 0
    weighted = jnp.zeros((D, LANES), F32)
    for block in range(12):
        start = block * D
        if start < half:
            part = pl.ds(start, D)
            found = jnp.where(first, mine[part, :].astype(F32), other[part, :].astype(F32))
        else:
            part = pl.ds(start - half, D)
            found = jnp.where(first, other[part, :].astype(F32), mine[part, :].astype(F32))
        found = found * grad_scale
        target, column = (qkv_grad, block) if block < 9 else (proj_grad, block - 9)
        columns = slice(column * LANES, (column + 1) * LANES)
        target[:, columns] = found
        if block < 9:
            weighted = weighted + found * w_qkv[:, columns].astype(F32)
    gain_grad[...] = (jnp.sum(weighted.T, axis=0, keepdims=True) / gain[...]).reshape(D)


def window_pass(own, behind, sides, w_qkv, w_proj, norm_gain):
    def buffer(shape, kind):
        return pltpu.VMEM(shape, kind)

    gain = norm_gain.reshape(1, D)
    grads, *kept = pl.pallas_call(
        window_kernel,
        out_shape=(
            jax.ShapeDtypeStruct((GRAD_ROWS, LANES), BF),
            jax.ShapeDtypeStruct((D, ROWS), BF),
            jax.ShapeDtypeStruct((ROWS, 3 * D), BF),
            jax.ShapeDtypeStruct((ROWS, D), F32),
            jax.ShapeDtypeStruct((ROWS, LANES), F32),
        ),
        scratch_shapes=[
            buffer((ROWS, D), BF),
            buffer((ROWS, 3 * D), BF),
            buffer((ROWS, D), BF),
            buffer((D, ROWS), BF),
            buffer((D, ROWS), BF),
            buffer((D, ROWS), BF),
            buffer((ROWS, D), BF),
        ],
        compiler_params=pltpu.CompilerParams(vmem_limit_bytes=32 * 1024 * 1024),
        cost_estimate=pl.CostEstimate(
            flops=12_000_000_000, bytes_accessed=5_000_000, transcendentals=3_200_000
        ),
    )(own, behind, *sides[::-1], w_qkv, w_proj, gain)
    backs = pl.pallas_call(
        rows_kernel,
        out_shape=(jax.ShapeDtypeStruct((2, 2, PIECE, D), BF),) * 2
        + (jax.ShapeDtypeStruct((2, 2, 2, PIECE, D), BF),),
        compiler_params=pltpu.CompilerParams(vmem_limit_bytes=24 * 1024 * 1024),
        cost_estimate=pl.CostEstimate(flops=2_000_000_000, bytes_accessed=4_000_000, transcendentals=0),
    )(*kept, w_qkv, w_proj, gain)
    return *backs, grads


LATTICE = ("z_hi", "z_lo", "core", "y_hi", "y_lo", "x")
FIRST = ("z_hi", "z_lo", "core")
SECOND = ("y_hi",)
THIRD = ("y_lo", "x")
SIZES = {"z_hi": 4, "z_lo": 2, "core": 2, "y_hi": 4, "y_lo": 2, "x": 4}
NEAR = ("x", "y_lo", "z_lo")
GROUP = 16
FAR = 4


def near_sum(rows):
    halves = lax.all_to_all(rows.reshape(2, GRAD_ROWS // 2, LANES), "core", 0, 0)
    parts = total_of(halves, 1).reshape(GROUP, GRAD_ROWS // 2 // GROUP, LANES)
    parts = lax.all_to_all(parts, NEAR, 0, 0)
    return parts


def device_at(first, second, third):
    return ((first % 16) * 4 + second % 4) * 8 + third % 8


def route(kind, back):
    pairs = []
    for first in range(16):
        for second in range(4):
            for third in range(8):
                sign = 1 if first % 2 else -1
                if kind == 0:
                    move = (first - 1, second, third)
                else:
                    move = (first, second + sign * (kind >> 1), third + sign * (kind & 1))
                pair = (device_at(first, second, third), device_at(*move))
                pairs.append(pair[::-1] if back else pair)
    return pairs


def send(block, kind, back=False):
    return lax.ppermute(block, LATTICE, route(kind, back))


def local(tokens, frozen, cotangent, w_qkv, w_proj, norm_gain):
    core = lax.axis_index("core").reshape(1)
    token_rows, cot_rows = tokens.reshape(ROWS, D), cotangent.reshape(ROWS, D)
    own, ahead = pl.pallas_call(
        cut_kernel,
        out_shape=(jax.ShapeDtypeStruct((4, 2, PIECE, D), BF),) * 2,
        in_specs=[SCALAR] + [pl.BlockSpec(memory_space=pltpu.HBM)] * 3,
        scratch_shapes=[
            pltpu.VMEM((ROWS, D), BF),
            pltpu.VMEM((WIN, WIN, WIN), jnp.int32),
            pltpu.VMEM((ROWS, D), BF),
            pltpu.SemaphoreType.DMA((3,)),
        ],
        compiler_params=pltpu.CompilerParams(vmem_limit_bytes=56 * 1024 * 1024),
    )(core, token_rows, frozen, cot_rows)
    behind = send(ahead, 0)
    sides = [None] * 4
    for kind in (1, 2, 3):
        sides[kind] = send(jnp.stack([own[kind], behind[kind]]), kind)
    back_0, back_1, back_y, grads = window_pass(own, behind, sides[1:], w_qkv, w_proj, norm_gain)
    parts = near_sum(grads)
    parts = total_of(parts, FAR)
    home_y = send(back_y, 2, True)
    parts, home_y = total_of(lax.all_to_all(parts, "z_hi", 0, 0), FAR, through=(home_y,))
    home_x = send(jnp.stack([back_1, home_y[1]]), 1, True)
    parts = total_of(lax.all_to_all(parts, "y_hi", 0, 0), GROUP)
    mine = lax.all_to_all(parts, NEAR, 0, 0).reshape(GRAD_ROWS // 2, LANES)
    ahead = send(jnp.stack([back_0[1], home_x[0, 1], home_y[0, 1], home_x[1, 1]]), 0, True)
    block_out, tokens_grad = pl.pallas_call(
        join_kernel,
        out_shape=(jax.ShapeDtypeStruct((ROWS, D), BF),) * 2,
        in_specs=[SCALAR] + [WHOLE] * 7,
        compiler_params=SMALL,
        cost_estimate=pl.CostEstimate(flops=300_000_000, bytes_accessed=4_000_000, transcendentals=0),
    )(core, token_rows, frozen, cot_rows, back_0, home_x, home_y, ahead)
    mine = hold(mine, ahead)
    other = lax.ppermute(mine, "core", [(0, 1), (1, 0)])
    qkv_grad, proj_grad, gain_grad = pl.pallas_call(
        grads_kernel,
        out_shape=(
            jax.ShapeDtypeStruct((D, 3 * D), F32),
            jax.ShapeDtypeStruct((D, D), F32),
            jax.ShapeDtypeStruct((D,), F32),
        ),
        in_specs=[SCALAR] + [WHOLE] * 4,
        compiler_params=SMALL,
    )(core, mine, other, w_qkv, norm_gain.reshape(1, D))
    shape = (WIN, WIN, WIN, D)
    return block_out.reshape(shape), tokens_grad.reshape(shape), qkv_grad, proj_grad, gain_grad


def solution(mesh):
    inner = Mesh(mesh.devices.reshape([SIZES[axis] for axis in LATTICE]), LATTICE)
    lattice = P(FIRST, SECOND, THIRD)
    wide = P(FIRST, SECOND, THIRD, None)
    return jax.shard_map(
        local,
        mesh=inner,
        in_specs=(wide, lattice, wide, P(), P(), P()),
        out_specs=(wide, wide, P(), P(), P()),
        check_vma=False,
    )
```

```python
import functools

import jax
import jax.numpy as jnp
import numpy as np
from jax import lax
from jax.experimental import pallas as pl
from jax.experimental.pallas import tpu as pltpu
from jax.sharding import Mesh, PartitionSpec as P

D = 384
HEADS = 12
HDIM = 32
WIN = 8
HALF = WIN // 2
ROWS = WIN**3
PIECE = HALF**3
HALF_ROWS = ROWS // 2
EPSILON = 1e-05
BF = jnp.bfloat16
F32 = jnp.float32
LANES = 128
PER = LANES // HDIM
CHUNK = 256
SCALE = HDIM ** (-0.5)
LOG2E = 1.4426950408889634
GRAD_ROWS = 12 * D


def dot(left, right):
    return jnp.dot(left, right, preferred_element_type=F32)


def dot_t(left, right):
    return lax.dot_general(left, right, (((1,), (1,)), ((), ())), preferred_element_type=F32)


def window_kernel(
    own, behind, side_3, side_2, side_1, w_qkv, w_proj, gain, grads, mixed_t, d_qkv, unit, inv_std,
    cot, qkv, d_mixed, keys_t, values_t, d_queries_t, normed,
):
    step = 2 * PIECE
    gain_row = gain[...]

    def arrived(group, array):
        if group == 0:
            return own[0, array], behind[0, array]
        side = (side_1, side_2, side_3)[group - 1]
        return side[0, array], side[1, array]

    for group in range(4):
        part = pl.ds(group * step, step)
        cot[part, :] = jnp.concatenate(arrived(group, 1), axis=0)
        rows = jnp.concatenate(arrived(group, 0), axis=0).astype(F32)
        centred = rows - jnp.mean(rows, axis=-1, keepdims=True)
        inverse = lax.rsqrt(jnp.mean(centred * centred, axis=-1, keepdims=True) + EPSILON)
        unit_rows = centred * inverse
        unit[part, :] = unit_rows
        inv_std[part, :] = jnp.broadcast_to(inverse, (step, LANES))
        normed[part, :] = (unit_rows * gain_row).astype(BF)
    qkv[...] = dot(normed[...], w_qkv[...]).astype(BF)
    d_mixed[...] = dot_t(cot[...], w_proj[...]).astype(BF)
    keys_t[...] = qkv[:, D : 2 * D].T
    values_t[...] = qkv[:, 2 * D :].T
    lane = lax.broadcasted_iota(jnp.int32, (1, LANES), 1)

    def first_products(head, start):
        block = slice(head // PER * LANES, (head // PER + 1) * LANES)
        mine = (lane // HDIM) == head % PER
        queries = pl.ds(start, CHUNK)
        zeros = jnp.zeros((CHUNK, LANES), BF)
        q_part = jnp.where(mine, qkv[queries, block], zeros)
        m_part = jnp.where(mine, d_mixed[queries, block], zeros)
        scores = dot_t(qkv[:, D + block.start : D + block.stop], q_part)
        d_probs = dot_t(qkv[:, 2 * D + block.start : 2 * D + block.stop], m_part)
        return q_part, m_part, scores, d_probs

    steps = [(head, start) for head in range(HEADS) for start in range(0, ROWS, CHUNK)]
    ready = first_products(*steps[0])
    for index, (head, start) in enumerate(steps):
        q_part, m_part, scores, d_probs = ready
        if index + 1 < len(steps):
            ready = first_products(*steps[index + 1])
        if head % PER == 0 and start == 0:
            d_keys = jnp.zeros((ROWS, LANES), F32)
            d_values = jnp.zeros((ROWS, LANES), F32)
        rows = pl.ds(head * HDIM, HDIM)
        top = jnp.max(scores, axis=0, keepdims=True)
        terms = jnp.exp2(scores * (SCALE * LOG2E) - top * (SCALE * LOG2E))
        inverse = 1.0 / jnp.sum(terms, axis=0, keepdims=True)
        probs_low = (terms * inverse).astype(BF)
        mixed_t[rows, pl.ds(start, CHUNK)] = dot(values_t[rows, :], probs_low).astype(BF)
        d_values = d_values + dot(probs_low, m_part)
        scaled = inverse * SCALE
        shift = jnp.sum(terms * d_probs, axis=0, keepdims=True) * (inverse * scaled)
        d_scores = (terms * (d_probs * scaled - shift)).astype(BF)
        d_queries_t[rows, pl.ds(start, CHUNK)] = dot(keys_t[rows, :], d_scores).astype(BF)
        d_keys = d_keys + dot(d_scores, q_part)
        if head % PER == PER - 1 and start + CHUNK == ROWS:
            block = head // PER * LANES
            d_qkv[:, D + block : D + block + LANES] = d_keys.astype(BF)
            d_qkv[:, 2 * D + block : 2 * D + block + LANES] = d_values.astype(BF)

    d_qkv[:, pl.ds(0, D)] = d_queries_t[...].T
    normed_t = normed[...].T
    for block in range(9):
        term = dot(normed_t, d_qkv[:, block * LANES : (block + 1) * LANES])
        grads[pl.ds(block * D, D), :] = term.astype(BF)
    for block in range(3):
        term = dot(mixed_t[...], cot[:, block * LANES : (block + 1) * LANES])
        grads[pl.ds((9 + block) * D, D), :] = term.astype(BF)


def rows_kernel(mixed_t, d_qkv, unit, inv_std, w_qkv, w_proj, gain, back_0, back_1, back_y):
    step = 2 * PIECE
    backs = (back_0, back_1, back_y.at[0], back_y.at[1])
    branch = dot(mixed_t[...].T, w_proj[...]).astype(BF)
    for group in range(4):
        part = pl.ds(group * step, step)
        d_normed = dot_t(d_qkv[part, :], w_qkv[...])
        unit_rows = unit[part, :]
        scaled = d_normed * gain[...]
        mean_1 = jnp.mean(scaled, axis=-1, keepdims=True)
        mean_2 = jnp.mean(scaled * unit_rows, axis=-1, keepdims=True)
        d_rows = (inv_std[part, 0:1] * (scaled - mean_1 - unit_rows * mean_2)).astype(BF)
        for place in range(2):
            start = (2 * group + place) * PIECE
            backs[group][place, 0] = branch[start : start + PIECE]
            backs[group][place, 1] = d_rows[place * PIECE : (place + 1) * PIECE]


def order(odd, upper, inverse):
    flip = odd if upper == 0 else 1 - odd
    shape = (WIN * WIN, WIN * WIN)
    row = lax.broadcasted_iota(jnp.int32, shape, 1 if inverse else 0)
    token = lax.broadcasted_iota(jnp.int32, shape, 0 if inverse else 1)
    along_y = ((row >> 5) ^ flip) * HALF + ((row >> 2) & 3)
    along_z = (((row >> 4) & 1) ^ flip) * HALF + (row & 3)
    return token == along_y * WIN + along_z


def ones_where(chosen):
    return jnp.where(chosen, 1.0, 0.0)


def keep_rows(frozen):
    planes = frozen.shape[0]
    table = ones_where(frozen[...].reshape(planes * WIN, WIN) == 1).astype(BF)
    column = lax.broadcasted_iota(jnp.int32, (WIN, WIN * WIN), 1)
    row = lax.broadcasted_iota(jnp.int32, (WIN, WIN * WIN), 0)
    spread = dot(table, ones_where((column & 7) == row).astype(BF))
    chosen = ones_where((column >> 3) == row)
    return [
        jnp.sum(spread[plane * WIN : (plane + 1) * WIN] * chosen, axis=0, keepdims=True)
        for plane in range(planes)
    ]


def cut_kernel(odd, tokens_in, frozen_in, cotangent_in, target, tokens, frozen, cotangent, arrivals, *, upper):
    rows = pl.ds(upper * HALF_ROWS, HALF_ROWS)
    moves = [
        pltpu.make_async_copy(source, target, arrivals.at[index])
        for index, (source, target) in enumerate(
            (
                (frozen_in.at[pl.ds(upper * HALF, HALF)], frozen),
                (tokens_in.at[rows], tokens),
                (cotangent_in.at[rows], cotangent),
            )
        )
    ]
    for move in moves:
        move.start()
    for move in moves:
        move.wait()
    keeps = keep_rows(frozen)
    matrix = ones_where(order(odd[0], upper, False))
    for plane in range(HALF):
        part = pl.ds(plane * WIN * WIN, WIN * WIN)
        kept = dot((matrix * keeps[plane]).astype(BF), tokens[part, :]).astype(BF)
        cot = dot(matrix.astype(BF), cotangent[part, :]).astype(BF)
        for group in range(4):
            rows = slice(group * 16, group * 16 + 16)
            target[group, 0, pl.ds(plane * 16, 16), :] = kept[rows]
            target[group, 1, pl.ds(plane * 16, 16), :] = cot[rows]


def cut(core, tokens, frozen, cotangent, upper):
    return pl.pallas_call(
        functools.partial(cut_kernel, upper=upper),
        out_shape=jax.ShapeDtypeStruct((4, 2, PIECE, D), BF),
        in_specs=[SCALAR] + [pl.BlockSpec(memory_space=pltpu.HBM)] * 3,
        scratch_shapes=[
            pltpu.VMEM((HALF_ROWS, D), BF),
            pltpu.VMEM((HALF, WIN, WIN), jnp.int32),
            pltpu.VMEM((HALF_ROWS, D), BF),
            pltpu.SemaphoreType.DMA((3,)),
        ],
        compiler_params=pltpu.CompilerParams(vmem_limit_bytes=56 * 1024 * 1024),
    )(core, tokens, frozen, cotangent)


def join_kernel(odd, tokens, frozen, cotangent, *rest, upper):
    if upper:
        pieces, (block_out, tokens_grad, token) = rest[:3], rest[-3:]
        token[...] = jnp.zeros_like(token)
    else:
        pieces, (block_out, tokens_grad) = rest[:1], rest[-2:]
    keeps = keep_rows(frozen)
    shape = (WIN * WIN, WIN * WIN)
    diagonal = ones_where(lax.broadcasted_iota(jnp.int32, shape, 0) == lax.broadcasted_iota(jnp.int32, shape, 1))
    matrix = ones_where(order(odd[0], upper, True)).astype(BF)
    for plane in range(HALF):
        part = pl.ds(plane * WIN * WIN, WIN * WIN)
        keep = (diagonal * keeps[plane]).astype(BF)
        rows = pl.ds(plane * 16, 16)

        def piece(group, array):
            if not upper:
                return pieces[0][group, array, rows, :]
            home_0, home_x, home_y = pieces
            home = (home_0, home_x.at[0], home_y.at[0], home_x.at[1])[group]
            return home[0, array, rows, :]

        def ordered(array):
            return dot(matrix, jnp.concatenate([piece(group, array) for group in range(4)], axis=0))

        block_out[part, :] = (dot(keep, tokens[part, :]) + ordered(0)).astype(BF)
        grown = (cotangent[part, :].astype(F32) + ordered(1)).astype(BF)
        tokens_grad[part, :] = dot(keep, grown).astype(BF)


def join(core, tokens, frozen, cotangent, pieces, upper, begun=()):
    half = pl.BlockSpec((HALF_ROWS, D), lambda step: (upper, 0))
    return pl.pallas_call(
        functools.partial(join_kernel, upper=upper),
        grid=(1,),
        out_shape=(jax.ShapeDtypeStruct((ROWS, D), BF),) * 2
        + (jax.ShapeDtypeStruct((8, LANES), F32),) * upper,
        in_specs=[SCALAR, half, pl.BlockSpec((HALF, WIN, WIN), lambda step: (upper, 0, 0)), half]
        + [WHOLE] * len(pieces)
        + [pl.BlockSpec(memory_space=pl.ANY)] * len(begun),
        out_specs=(half, half) + (WHOLE,) * upper,
        input_output_aliases={4 + len(pieces) + at: at for at in range(len(begun))},
        compiler_params=SMALL,
        cost_estimate=pl.CostEstimate(flops=150_000_000, bytes_accessed=2_000_000, transcendentals=0),
    )(core, tokens, frozen, cotangent, *pieces, *begun)


SCALAR = pl.BlockSpec(memory_space=pltpu.SMEM)
WHOLE = pl.BlockSpec(memory_space=pltpu.VMEM)
SMALL = pltpu.CompilerParams(vmem_limit_bytes=12 * 1024 * 1024)


def total_kernel(parts, *rest, copies, out_at):
    out = rest[out_at]
    total = parts[0].astype(F32)
    for index in range(1, parts.shape[0]):
        total = total + parts[index].astype(F32)
    total = total.astype(BF)
    for index in range(copies):
        out[index] = total


def total_of(parts, copies, after=(), through=()):
    anywhere = pl.BlockSpec(memory_space=pl.ANY)
    total, *passed = pl.pallas_call(
        functools.partial(total_kernel, copies=copies, out_at=len(after) + len(through)),
        out_shape=[jax.ShapeDtypeStruct((copies,) + parts.shape[1:], BF)]
        + [jax.ShapeDtypeStruct(array.shape, array.dtype) for array in through],
        in_specs=[WHOLE] + [anywhere] * (len(after) + len(through)),
        out_specs=[WHOLE] + [anywhere] * len(through),
        input_output_aliases={1 + len(after) + at: 1 + at for at in range(len(through))},
        compiler_params=SMALL,
    )(parts, *after, *through)
    return (total, *passed) if through else total


def hold(array, *until):
    anywhere = pl.BlockSpec(memory_space=pl.ANY)
    return pl.pallas_call(
        lambda *refs: None,
        out_shape=jax.ShapeDtypeStruct(array.shape, array.dtype),
        in_specs=[anywhere] * (1 + len(until)),
        out_specs=anywhere,
        input_output_aliases={0: 0},
        compiler_params=SMALL,
    )(array, *until)


def grads_kernel(core, mine, other, w_qkv, gain, qkv_grad, proj_grad, gain_grad):
    grad_scale = (ROWS * 512) ** (-0.5)
    half = GRAD_ROWS // 2
    first = core[0] == 0
    weighted = jnp.zeros((D, LANES), F32)
    for block in range(12):
        start = block * D
        if start < half:
            part = pl.ds(start, D)
            found = jnp.where(first, mine[part, :].astype(F32), other[part, :].astype(F32))
        else:
            part = pl.ds(start - half, D)
            found = jnp.where(first, other[part, :].astype(F32), mine[part, :].astype(F32))
        found = found * grad_scale
        target, column = (qkv_grad, block) if block < 9 else (proj_grad, block - 9)
        columns = slice(column * LANES, (column + 1) * LANES)
        target[:, columns] = found
        if block < 9:
            weighted = weighted + found * w_qkv[:, columns].astype(F32)
    gain_grad[...] = (jnp.sum(weighted.T, axis=0, keepdims=True) / gain[...]).reshape(D)


def window_pass(own, behind, sides, w_qkv, w_proj, norm_gain):
    def buffer(shape, kind):
        return pltpu.VMEM(shape, kind)

    gain = norm_gain.reshape(1, D)
    grads, *kept = pl.pallas_call(
        window_kernel,
        out_shape=(
            jax.ShapeDtypeStruct((GRAD_ROWS, LANES), BF),
            jax.ShapeDtypeStruct((D, ROWS), BF),
            jax.ShapeDtypeStruct((ROWS, 3 * D), BF),
            jax.ShapeDtypeStruct((ROWS, D), F32),
            jax.ShapeDtypeStruct((ROWS, LANES), F32),
        ),
        scratch_shapes=[
            buffer((ROWS, D), BF),
            buffer((ROWS, 3 * D), BF),
            buffer((ROWS, D), BF),
            buffer((D, ROWS), BF),
            buffer((D, ROWS), BF),
            buffer((D, ROWS), BF),
            buffer((ROWS, D), BF),
        ],
        compiler_params=pltpu.CompilerParams(vmem_limit_bytes=32 * 1024 * 1024),
        cost_estimate=pl.CostEstimate(
            flops=12_000_000_000, bytes_accessed=5_000_000, transcendentals=3_200_000
        ),
    )(own, behind, *sides, w_qkv, w_proj, gain)
    backs = pl.pallas_call(
        rows_kernel,
        out_shape=(jax.ShapeDtypeStruct((2, 2, PIECE, D), BF),) * 2
        + (jax.ShapeDtypeStruct((2, 2, 2, PIECE, D), BF),),
        compiler_params=pltpu.CompilerParams(vmem_limit_bytes=24 * 1024 * 1024),
        cost_estimate=pl.CostEstimate(flops=2_000_000_000, bytes_accessed=4_000_000, transcendentals=0),
    )(*kept, w_qkv, w_proj, gain)
    return *backs, grads


LATTICE = ("z_hi", "z_lo", "core", "y_hi", "y_lo", "x")
FIRST = ("z_hi", "z_lo", "core")
SECOND = ("y_hi",)
THIRD = ("y_lo", "x")
SIZES = {"z_hi": 4, "z_lo": 2, "core": 2, "y_hi": 4, "y_lo": 2, "x": 4}
NEAR = ("x", "y_lo", "z_lo")
GROUP = 16
FAR = 4


def near_sum(rows):
    halves = lax.all_to_all(rows.reshape(2, GRAD_ROWS // 2, LANES), "core", 0, 0)
    parts = total_of(halves, 1).reshape(GROUP, GRAD_ROWS // 2 // GROUP, LANES)
    parts = lax.all_to_all(parts, NEAR, 0, 0)
    return parts


def device_at(first, second, third):
    return ((first % 16) * 4 + second % 4) * 8 + third % 8


def route(kind, back):
    pairs = []
    for first in range(16):
        for second in range(4):
            for third in range(8):
                sign = 1 if first % 2 else -1
                if kind == 0:
                    move = (first - 1, second, third)
                else:
                    move = (first, second + sign * (kind >> 1), third + sign * (kind & 1))
                pair = (device_at(first, second, third), device_at(*move))
                pairs.append(pair[::-1] if back else pair)
    return pairs


def send(block, kind, back=False):
    return lax.ppermute(block, LATTICE, route(kind, back))


def local(tokens, frozen, cotangent, w_qkv, w_proj, norm_gain):
    core = lax.axis_index("core").reshape(1)
    token_rows, cot_rows = tokens.reshape(ROWS, D), cotangent.reshape(ROWS, D)
    behind = send(cut(core, token_rows, frozen, cot_rows, 0), 0)
    own = cut(core, token_rows, frozen, cot_rows, 1)
    sides = [send(jnp.stack([own[kind], behind[kind]]), kind) for kind in (3, 2, 1)]
    back_0, back_1, back_y, grads = window_pass(own, behind, sides, w_qkv, w_proj, norm_gain)
    parts = near_sum(grads)
    parts = total_of(parts, FAR)
    home_y = send(back_y, 2, True)
    parts, home_y = total_of(lax.all_to_all(parts, "z_hi", 0, 0), FAR, through=(home_y,))
    home_x = send(jnp.stack([back_1, home_y[1]]), 1, True)
    parts = total_of(lax.all_to_all(parts, "y_hi", 0, 0), GROUP)
    mine = lax.all_to_all(parts, NEAR, 0, 0).reshape(GRAD_ROWS // 2, LANES)
    ahead = send(jnp.stack([back_0[1], home_x[0, 1], home_y[0, 1], home_x[1, 1]]), 0, True)
    *begun, token = join(core, token_rows, frozen, cot_rows, (back_0, home_x, home_y), 1)
    mine = hold(mine, ahead, token)
    block_out, tokens_grad = join(core, token_rows, frozen, cot_rows, (ahead,), 0, begun)
    other = lax.ppermute(mine, "core", [(0, 1), (1, 0)])
    qkv_grad, proj_grad, gain_grad = pl.pallas_call(
        grads_kernel,
        out_shape=(
            jax.ShapeDtypeStruct((D, 3 * D), F32),
            jax.ShapeDtypeStruct((D, D), F32),
            jax.ShapeDtypeStruct((D,), F32),
        ),
        in_specs=[SCALAR] + [WHOLE] * 4,
        compiler_params=SMALL,
    )(core, mine, other, w_qkv, norm_gain.reshape(1, D))
    shape = (WIN, WIN, WIN, D)
    return block_out.reshape(shape), tokens_grad.reshape(shape), qkv_grad, proj_grad, gain_grad


def solution(mesh):
    inner = Mesh(mesh.devices.reshape([SIZES[axis] for axis in LATTICE]), LATTICE)
    lattice = P(FIRST, SECOND, THIRD)
    wide = P(FIRST, SECOND, THIRD, None)
    return jax.shard_map(
        local,
        mesh=inner,
        in_specs=(wide, lattice, wide, P(), P(), P()),
        out_specs=(wide, wide, P(), P(), P()),
        check_vma=False,
    )
```

```python
import functools

import jax
import jax.numpy as jnp
import numpy as np
from jax import lax
from jax.experimental import pallas as pl
from jax.experimental.pallas import tpu as pltpu
from jax.sharding import Mesh, PartitionSpec as P

D = 384
HEADS = 12
HDIM = 32
WIN = 8
HALF = WIN // 2
ROWS = WIN**3
PIECE = HALF**3
HALF_ROWS = ROWS // 2
EPSILON = 1e-05
BF = jnp.bfloat16
F32 = jnp.float32
LANES = 128
PER = LANES // HDIM
CHUNK = 256
SCALE = HDIM ** (-0.5)
LOG2E = 1.4426950408889634
GRAD_ROWS = 12 * D


def dot(left, right):
    return jnp.dot(left, right, preferred_element_type=F32)


def dot_t(left, right):
    return lax.dot_general(left, right, (((1,), (1,)), ((), ())), preferred_element_type=F32)


def window_kernel(
    own, behind, side_3, side_2, side_1, w_qkv, w_proj, gain, grads, mixed_t, d_qkv, unit,
    cot, qkv, d_mixed, keys_t, values_t, d_queries_t, normed,
):
    step = 2 * PIECE
    gain_row = gain[...]

    def arrived(group, array):
        if group == 0:
            return own[0, array], behind[0, array]
        side = (side_1, side_2, side_3)[group - 1]
        return side[0, array], side[1, array]

    for group in range(4):
        part = pl.ds(group * step, step)
        cot[part, :] = jnp.concatenate(arrived(group, 1), axis=0)
        rows = jnp.concatenate(arrived(group, 0), axis=0).astype(F32)
        centred = rows - jnp.mean(rows, axis=-1, keepdims=True)
        inverse = lax.rsqrt(jnp.mean(centred * centred, axis=-1, keepdims=True) + EPSILON)
        unit_rows = centred * inverse
        unit[part, :D] = unit_rows
        unit[part, D:] = jnp.broadcast_to(inverse, (step, LANES))
        normed[part, :] = (unit_rows * gain_row).astype(BF)
    qkv[...] = dot(normed[...], w_qkv[...]).astype(BF)
    d_mixed[...] = dot_t(cot[...], w_proj[...]).astype(BF)
    keys_t[...] = qkv[:, D : 2 * D].T
    values_t[...] = qkv[:, 2 * D :].T
    lane = lax.broadcasted_iota(jnp.int32, (1, LANES), 1)

    def first_products(head, start):
        block = slice(head // PER * LANES, (head // PER + 1) * LANES)
        mine = (lane // HDIM) == head % PER
        queries = pl.ds(start, CHUNK)
        zeros = jnp.zeros((CHUNK, LANES), BF)
        q_part = jnp.where(mine, qkv[queries, block], zeros)
        m_part = jnp.where(mine, d_mixed[queries, block], zeros)
        scores = dot_t(qkv[:, D + block.start : D + block.stop], q_part)
        d_probs = dot_t(qkv[:, 2 * D + block.start : 2 * D + block.stop], m_part)
        return q_part, m_part, scores, d_probs

    steps = [(head, start) for head in range(HEADS) for start in range(0, ROWS, CHUNK)]
    ready = first_products(*steps[0])
    for index, (head, start) in enumerate(steps):
        q_part, m_part, scores, d_probs = ready
        if index + 1 < len(steps):
            ready = first_products(*steps[index + 1])
        if head % PER == 0 and start == 0:
            d_keys = jnp.zeros((ROWS, LANES), F32)
            d_values = jnp.zeros((ROWS, LANES), F32)
        rows = pl.ds(head * HDIM, HDIM)
        top = jnp.max(scores, axis=0, keepdims=True)
        terms = jnp.exp2(scores * (SCALE * LOG2E) - top * (SCALE * LOG2E))
        inverse = 1.0 / jnp.sum(terms, axis=0, keepdims=True)
        probs_low = (terms * inverse).astype(BF)
        mixed_t[rows, pl.ds(start, CHUNK)] = dot(values_t[rows, :], probs_low).astype(BF)
        d_values = d_values + dot(probs_low, m_part)
        scaled = inverse * SCALE
        shift = jnp.sum(terms * d_probs, axis=0, keepdims=True) * (inverse * scaled)
        d_scores = (terms * (d_probs * scaled - shift)).astype(BF)
        d_queries_t[rows, pl.ds(start, CHUNK)] = dot(keys_t[rows, :], d_scores).astype(BF)
        d_keys = d_keys + dot(d_scores, q_part)
        if head % PER == PER - 1 and start + CHUNK == ROWS:
            block = head // PER * LANES
            d_qkv[:, D + block : D + block + LANES] = d_keys.astype(BF)
            d_qkv[:, 2 * D + block : 2 * D + block + LANES] = d_values.astype(BF)

    d_qkv[:, pl.ds(0, D)] = d_queries_t[...].T
    normed_t = normed[...].T
    for block in range(9):
        term = dot(normed_t, d_qkv[:, block * LANES : (block + 1) * LANES])
        grads[pl.ds(block * D, D), :] = term.astype(BF)
    for block in range(3):
        term = dot(mixed_t[...], cot[:, block * LANES : (block + 1) * LANES])
        grads[pl.ds((9 + block) * D, D), :] = term.astype(BF)


def rows_kernel(mixed_t, d_qkv, unit, w_qkv, w_proj, gain, back_0, back_1, back_y):
    step = 2 * PIECE
    backs = (back_0, back_1, back_y.at[0], back_y.at[1])
    branch = dot(mixed_t[...].T, w_proj[...]).astype(BF)
    for group in range(4):
        part = pl.ds(group * step, step)
        d_normed = dot_t(d_qkv[part, :], w_qkv[...])
        unit_rows = unit[part, :D]
        scaled = d_normed * gain[...]
        mean_1 = jnp.mean(scaled, axis=-1, keepdims=True)
        mean_2 = jnp.mean(scaled * unit_rows, axis=-1, keepdims=True)
        d_rows = (unit[part, D : D + 1] * (scaled - mean_1 - unit_rows * mean_2)).astype(BF)
        for place in range(2):
            start = (2 * group + place) * PIECE
            backs[group][place, 0] = branch[start : start + PIECE]
            backs[group][place, 1] = d_rows[place * PIECE : (place + 1) * PIECE]


def order(odd, upper, inverse):
    flip = odd if upper == 0 else 1 - odd
    shape = (WIN * WIN, WIN * WIN)
    row = lax.broadcasted_iota(jnp.int32, shape, 1 if inverse else 0)
    token = lax.broadcasted_iota(jnp.int32, shape, 0 if inverse else 1)
    along_y = ((row >> 5) ^ flip) * HALF + ((row >> 2) & 3)
    along_z = (((row >> 4) & 1) ^ flip) * HALF + (row & 3)
    return token == along_y * WIN + along_z


def ones_where(chosen):
    return jnp.where(chosen, 1.0, 0.0)


def keep_rows(frozen):
    planes = frozen.shape[0]
    table = ones_where(frozen[...].reshape(planes * WIN, WIN) == 1).astype(BF)
    column = lax.broadcasted_iota(jnp.int32, (WIN, WIN * WIN), 1)
    row = lax.broadcasted_iota(jnp.int32, (WIN, WIN * WIN), 0)
    spread = dot(table, ones_where((column & 7) == row).astype(BF))
    chosen = ones_where((column >> 3) == row)
    return [
        jnp.sum(spread[plane * WIN : (plane + 1) * WIN] * chosen, axis=0, keepdims=True)
        for plane in range(planes)
    ]


def cut_kernel(odd, tokens_in, frozen_in, cotangent_in, target, tokens, frozen, cotangent, arrivals, *, upper):
    rows = pl.ds(upper * HALF_ROWS, HALF_ROWS)
    moves = [
        pltpu.make_async_copy(source, target, arrivals.at[index])
        for index, (source, target) in enumerate(
            (
                (frozen_in.at[pl.ds(upper * HALF, HALF)], frozen),
                (tokens_in.at[rows], tokens),
                (cotangent_in.at[rows], cotangent),
            )
        )
    ]
    for move in moves:
        move.start()
    for move in moves:
        move.wait()
    keeps = keep_rows(frozen)
    matrix = ones_where(order(odd[0], upper, False))
    for plane in range(HALF):
        part = pl.ds(plane * WIN * WIN, WIN * WIN)
        kept = dot((matrix * keeps[plane]).astype(BF), tokens[part, :]).astype(BF)
        cot = dot(matrix.astype(BF), cotangent[part, :]).astype(BF)
        for group in range(4):
            rows = slice(group * 16, group * 16 + 16)
            target[group, 0, pl.ds(plane * 16, 16), :] = kept[rows]
            target[group, 1, pl.ds(plane * 16, 16), :] = cot[rows]


def cut(core, tokens, frozen, cotangent, upper):
    return pl.pallas_call(
        functools.partial(cut_kernel, upper=upper),
        out_shape=jax.ShapeDtypeStruct((4, 2, PIECE, D), BF),
        in_specs=[SCALAR] + [pl.BlockSpec(memory_space=pltpu.HBM)] * 3,
        scratch_shapes=[
            pltpu.VMEM((HALF_ROWS, D), BF),
            pltpu.VMEM((HALF, WIN, WIN), jnp.int32),
            pltpu.VMEM((HALF_ROWS, D), BF),
            pltpu.SemaphoreType.DMA((3,)),
        ],
        compiler_params=pltpu.CompilerParams(vmem_limit_bytes=56 * 1024 * 1024),
    )(core, tokens, frozen, cotangent)


def join_kernel(odd, tokens, frozen, cotangent, *rest, upper):
    if upper:
        pieces, (block_out, tokens_grad, token) = rest[:3], rest[-3:]
        token[...] = jnp.zeros_like(token)
    else:
        pieces, (block_out, tokens_grad) = rest[:1], rest[-2:]
    keeps = keep_rows(frozen)
    shape = (WIN * WIN, WIN * WIN)
    diagonal = ones_where(lax.broadcasted_iota(jnp.int32, shape, 0) == lax.broadcasted_iota(jnp.int32, shape, 1))
    matrix = ones_where(order(odd[0], upper, True)).astype(BF)
    for plane in range(HALF):
        part = pl.ds(plane * WIN * WIN, WIN * WIN)
        keep = (diagonal * keeps[plane]).astype(BF)
        rows = pl.ds(plane * 16, 16)

        def piece(group, array):
            if not upper:
                return pieces[0][group, array, rows, :]
            home_0, home_x, home_y = pieces
            home = (home_0, home_x.at[0], home_y.at[0], home_x.at[1])[group]
            return home[0, array, rows, :]

        def ordered(array):
            return dot(matrix, jnp.concatenate([piece(group, array) for group in range(4)], axis=0))

        block_out[part, :] = (dot(keep, tokens[part, :]) + ordered(0)).astype(BF)
        grown = (cotangent[part, :].astype(F32) + ordered(1)).astype(BF)
        tokens_grad[part, :] = dot(keep, grown).astype(BF)


def join(core, tokens, frozen, cotangent, pieces, upper, begun=()):
    half = pl.BlockSpec((HALF_ROWS, D), lambda step: (upper, 0))
    return pl.pallas_call(
        functools.partial(join_kernel, upper=upper),
        grid=(1,),
        out_shape=(jax.ShapeDtypeStruct((ROWS, D), BF),) * 2
        + (jax.ShapeDtypeStruct((8, LANES), F32),) * upper,
        in_specs=[SCALAR, half, pl.BlockSpec((HALF, WIN, WIN), lambda step: (upper, 0, 0)), half]
        + [WHOLE] * len(pieces)
        + [pl.BlockSpec(memory_space=pl.ANY)] * len(begun),
        out_specs=(half, half) + (WHOLE,) * upper,
        input_output_aliases={4 + len(pieces) + at: at for at in range(len(begun))},
        compiler_params=SMALL,
        cost_estimate=pl.CostEstimate(flops=150_000_000, bytes_accessed=2_000_000, transcendentals=0),
    )(core, tokens, frozen, cotangent, *pieces, *begun)


SCALAR = pl.BlockSpec(memory_space=pltpu.SMEM)
WHOLE = pl.BlockSpec(memory_space=pltpu.VMEM)
SMALL = pltpu.CompilerParams(vmem_limit_bytes=12 * 1024 * 1024)


def total_kernel(parts, *rest, copies, out_at):
    out = rest[out_at]
    total = parts[0].astype(F32)
    for index in range(1, parts.shape[0]):
        total = total + parts[index].astype(F32)
    total = total.astype(BF)
    for index in range(copies):
        out[index] = total


def total_of(parts, copies, after=(), through=()):
    anywhere = pl.BlockSpec(memory_space=pl.ANY)
    total, *passed = pl.pallas_call(
        functools.partial(total_kernel, copies=copies, out_at=len(after) + len(through)),
        out_shape=[jax.ShapeDtypeStruct((copies,) + parts.shape[1:], BF)]
        + [jax.ShapeDtypeStruct(array.shape, array.dtype) for array in through],
        in_specs=[WHOLE] + [anywhere] * (len(after) + len(through)),
        out_specs=[WHOLE] + [anywhere] * len(through),
        input_output_aliases={1 + len(after) + at: 1 + at for at in range(len(through))},
        compiler_params=SMALL,
    )(parts, *after, *through)
    return (total, *passed) if through else total


def hold(array, *until):
    anywhere = pl.BlockSpec(memory_space=pl.ANY)
    return pl.pallas_call(
        lambda *refs: None,
        out_shape=jax.ShapeDtypeStruct(array.shape, array.dtype),
        in_specs=[anywhere] * (1 + len(until)),
        out_specs=anywhere,
        input_output_aliases={0: 0},
        compiler_params=SMALL,
    )(array, *until)


def grads_kernel(core, mine, other, w_qkv, gain, qkv_grad, proj_grad, gain_grad):
    grad_scale = (ROWS * 512) ** (-0.5)
    half = GRAD_ROWS // 2
    first = core[0] == 0
    weighted = jnp.zeros((D, LANES), F32)
    for block in range(12):
        start = block * D
        if start < half:
            part = pl.ds(start, D)
            found = jnp.where(first, mine[part, :].astype(F32), other[part, :].astype(F32))
        else:
            part = pl.ds(start - half, D)
            found = jnp.where(first, other[part, :].astype(F32), mine[part, :].astype(F32))
        found = found * grad_scale
        target, column = (qkv_grad, block) if block < 9 else (proj_grad, block - 9)
        columns = slice(column * LANES, (column + 1) * LANES)
        target[:, columns] = found
        if block < 9:
            weighted = weighted + found * w_qkv[:, columns].astype(F32)
    gain_grad[...] = (jnp.sum(weighted.T, axis=0, keepdims=True) / gain[...]).reshape(D)


def window_pass(own, behind, sides, w_qkv, w_proj, norm_gain):
    def buffer(shape, kind):
        return pltpu.VMEM(shape, kind)

    gain = norm_gain.reshape(1, D)
    grads, *kept = pl.pallas_call(
        window_kernel,
        out_shape=(
            jax.ShapeDtypeStruct((GRAD_ROWS, LANES), BF),
            jax.ShapeDtypeStruct((D, ROWS), BF),
            jax.ShapeDtypeStruct((ROWS, 3 * D), BF),
            jax.ShapeDtypeStruct((ROWS, D + LANES), F32),
        ),
        scratch_shapes=[
            buffer((ROWS, D), BF),
            buffer((ROWS, 3 * D), BF),
            buffer((ROWS, D), BF),
            buffer((D, ROWS), BF),
            buffer((D, ROWS), BF),
            buffer((D, ROWS), BF),
            buffer((ROWS, D), BF),
        ],
        compiler_params=pltpu.CompilerParams(vmem_limit_bytes=32 * 1024 * 1024),
        cost_estimate=pl.CostEstimate(
            flops=12_000_000_000, bytes_accessed=5_000_000, transcendentals=3_200_000
        ),
    )(own, behind, *sides, w_qkv, w_proj, gain)
    backs = pl.pallas_call(
        rows_kernel,
        out_shape=(jax.ShapeDtypeStruct((2, 2, PIECE, D), BF),) * 2
        + (jax.ShapeDtypeStruct((2, 2, 2, PIECE, D), BF),),
        compiler_params=pltpu.CompilerParams(vmem_limit_bytes=24 * 1024 * 1024),
        cost_estimate=pl.CostEstimate(flops=2_000_000_000, bytes_accessed=4_000_000, transcendentals=0),
    )(*kept, w_qkv, w_proj, gain)
    return *backs, grads


LATTICE = ("z_hi", "z_lo", "core", "y_hi", "y_lo", "x")
FIRST = ("z_hi", "z_lo", "core")
SECOND = ("y_hi",)
THIRD = ("y_lo", "x")
SIZES = {"z_hi": 4, "z_lo": 2, "core": 2, "y_hi": 4, "y_lo": 2, "x": 4}
NEAR = ("x", "y_lo", "z_lo")
GROUP = 16
FAR = 4


def near_sum(rows):
    halves = lax.all_to_all(rows.reshape(2, GRAD_ROWS // 2, LANES), "core", 0, 0)
    parts = total_of(halves, 1).reshape(GROUP, GRAD_ROWS // 2 // GROUP, LANES)
    parts = lax.all_to_all(parts, NEAR, 0, 0)
    return parts


def device_at(first, second, third):
    return ((first % 16) * 4 + second % 4) * 8 + third % 8


def route(kind, back):
    pairs = []
    for first in range(16):
        for second in range(4):
            for third in range(8):
                sign = 1 if first % 2 else -1
                if kind == 0:
                    move = (first - 1, second, third)
                else:
                    move = (first, second + sign * (kind >> 1), third + sign * (kind & 1))
                pair = (device_at(first, second, third), device_at(*move))
                pairs.append(pair[::-1] if back else pair)
    return pairs


def send(block, kind, back=False):
    return lax.ppermute(block, LATTICE, route(kind, back))


def local(tokens, frozen, cotangent, w_qkv, w_proj, norm_gain):
    core = lax.axis_index("core").reshape(1)
    token_rows, cot_rows = tokens.reshape(ROWS, D), cotangent.reshape(ROWS, D)
    behind = send(cut(core, token_rows, frozen, cot_rows, 0), 0)
    own = cut(core, token_rows, frozen, cot_rows, 1)
    sides = [send(jnp.stack([own[kind], behind[kind]]), kind) for kind in (3, 2, 1)]
    back_0, back_1, back_y, grads = window_pass(own, behind, sides, w_qkv, w_proj, norm_gain)
    parts = near_sum(grads)
    parts = total_of(parts, FAR)
    home_y = send(back_y, 2, True)
    parts, home_y = total_of(lax.all_to_all(parts, "z_hi", 0, 0), FAR, through=(home_y,))
    home_x = send(jnp.stack([back_1, home_y[1]]), 1, True)
    parts = total_of(lax.all_to_all(parts, "y_hi", 0, 0), GROUP)
    mine = lax.all_to_all(parts, NEAR, 0, 0).reshape(GRAD_ROWS // 2, LANES)
    ahead = send(jnp.stack([back_0[1], home_x[0, 1], home_y[0, 1], home_x[1, 1]]), 0, True)
    *begun, token = join(core, token_rows, frozen, cot_rows, (back_0, home_x, home_y), 1)
    mine = hold(mine, ahead, token)
    block_out, tokens_grad = join(core, token_rows, frozen, cot_rows, (ahead,), 0, begun)
    other = lax.ppermute(mine, "core", [(0, 1), (1, 0)])
    qkv_grad, proj_grad, gain_grad = pl.pallas_call(
        grads_kernel,
        out_shape=(
            jax.ShapeDtypeStruct((D, 3 * D), F32),
            jax.ShapeDtypeStruct((D, D), F32),
            jax.ShapeDtypeStruct((D,), F32),
        ),
        in_specs=[SCALAR] + [WHOLE] * 4,
        compiler_params=SMALL,
    )(core, mine, other, w_qkv, norm_gain.reshape(1, D))
    shape = (WIN, WIN, WIN, D)
    return block_out.reshape(shape), tokens_grad.reshape(shape), qkv_grad, proj_grad, gain_grad


def solution(mesh):
    inner = Mesh(mesh.devices.reshape([SIZES[axis] for axis in LATTICE]), LATTICE)
    lattice = P(FIRST, SECOND, THIRD)
    wide = P(FIRST, SECOND, THIRD, None)
    return jax.shard_map(
        local,
        mesh=inner,
        in_specs=(wide, lattice, wide, P(), P(), P()),
        out_specs=(wide, wide, P(), P(), P()),
        check_vma=False,
    )
```
